256 devices in a mesh: grp: 2 (over x_lo), gx: 16 (over z, x_hi), gy: 8 (over y, core).
Axes of the slice: x: 4 (x_hi: 2, x_lo: 2; x = x_hi * 2 + x_lo), y: 4, z: 8, core: 2. Of those that a mesh axis runs over, the one named last changes fastest.
Arguments:
- theta_anomaly: float32 [768, 128, 128], P(('grp', 'gx'), 'gy'), may hold values from -4 to 4
- humidity_ratio: float32 [768, 128, 128], P(('grp', 'gx'), 'gy'), may hold values from 0.6 to 1.4
- zonal_velocity: float32 [768, 128, 128], P(('grp', 'gx'), 'gy'), may hold values from -1.8 to 1.8
- meridional_velocity: float32 [768, 128, 128], P(('grp', 'gx'), 'gy'), may hold values from -1.8 to 1.8
- vertical_velocity: float32 [768, 128, 128], P(('grp', 'gx'), 'gy'), may hold values from -1.8 to 1.8
- patch_processor_map: int32 [32, 8, 8], P(('grp', 'gx'), 'gy'), may hold values from 0 to 15, as said below
- particle_bucket_population: int32 [32, 8, 16], P(('grp', 'gx'), 'gy'), may hold values from 0 to 1024, as said below
- particle_size_quadratic: float32 [32, 8, 16, 1024], P(('grp', 'gx'), 'gy'), may hold values from 0.25 to 4
- represented_number: float32 [32, 8, 16, 1024], P(('grp', 'gx'), 'gy'), may hold values from 0.5 to 2
- particle_location_number: int32 [32, 8, 16, 1024], P(('grp', 'gx'), 'gy'), may hold values from 48 to 6095, as said below
Outputs:
- final_temperature: float32 [768, 128, 128], P(('grp', 'gx'), 'gy')
- final_vapour: float32 [768, 128, 128], P(('grp', 'gx'), 'gy')
- final_east: float32 [768, 128, 128], P(('grp', 'gx'), 'gy')
- final_north: float32 [768, 128, 128], P(('grp', 'gx'), 'gy')
- final_vertical: float32 [768, 128, 128], P(('grp', 'gx'), 'gy')
- final_size_quadratic: float32 [32, 8, 16, 1024], P(('grp', 'gx'), 'gy')
The draws below stay inside these ranges and needn't reach their ends.
Inputs may be any that keep to these rules, and one draw needn't show every extreme that they name: `patch_processor_map`: entry [a, y, b] is the index along gx of the device in the same row (same grp half, same gy) that holds the droplets of column block b of device (a, y). Different blocks of one device go to different owners, so one device sends at most 1 block to one owner; in every row some owner holds 1 block from every device of the row. `particle_bucket_population`: entry [a, y, r] counts the live droplets of slot r = s x 1 + t of the owner (a, y); they are the first ones of the slot. A slot that receives no block has none; every slot of an owner that holds 1 block from every device is full. `particle_location_number`: the cell within the slot's block, column 128 + level, with levels from 48 to 79. Within a slot the live droplets are sorted by column, and so are the others.
All inputs are finite; a program needn't handle non-finite values.
Results may differ from the reference program's by a relative error of at most 0.0003.
Values sent between devices are 32-bit elements; how exact they have to be, the bound alone decides.
No kernel may reach another device: no remote copies, remote signals or barrier semaphores. Data moves between devices by JAX's collectives and lax.ppermute only.
A program may use at most 64 MiB of HBM per device.

```python
import math
import jax
import jax.numpy as jnp

CX = 24
VERTICAL_LAYERS = 128
NBD = 8
KLO = 48
KHI = 80
DPB = 1024
NSUB = 4
ITERS = 4
NSTEP = 1
XPEERS = 16
XTILES = 32
YTILES = 8
SPAN_COUNT_EAST = 768
SPAN_COUNT_NORTH = 128
BY = 2
BCOL = 48
SLOTS = 1
ROWSLOTS = 16


def wind_draw(key, salt):
    normals = jnp.clip(jax.random.normal(jax.random.fold_in(key, salt), (SPAN_COUNT_EAST, SPAN_COUNT_NORTH, VERTICAL_LAYERS), jnp.float32), -4.0, 4.0)
    x_place = jnp.arange(SPAN_COUNT_EAST, dtype=jnp.float32)
    y_place = jnp.arange(SPAN_COUNT_NORTH, dtype=jnp.float32)
    x_frac = x_place / max(SPAN_COUNT_EAST - 1, 1)
    y_frac = y_place / max(SPAN_COUNT_NORTH - 1, 1)
    amplitude = 0.05 * jnp.exp(jnp.log(3.0) * (x_frac[:, None] + y_frac[None, :]))
    return amplitude[..., None] * normals


def draw_zonal_velocity(key, part):
    return wind_draw(key, 21)


def draw_meridional_velocity(key, part):
    return wind_draw(key, 22)


def draw_vertical_velocity(key, part):
    return wind_draw(key, 23)


def plan_owners(key):
    groups = XTILES // XPEERS
    busiest = jax.random.randint(jax.random.fold_in(key, 11), (groups, 1, YTILES, 1), 0, XPEERS)
    spread = (NBD + SLOTS - 1) // SLOTS
    offsets = jax.random.randint(jax.random.fold_in(key, 12), (groups, XPEERS, YTILES, 1), 0, spread)
    blocks = jnp.arange(NBD, dtype=jnp.int32)
    owners = (busiest - offsets + blocks // SLOTS) % XPEERS
    return (owners, busiest)


def plan_counts(key):
    owners, busiest = plan_owners(key)
    target = jnp.arange(XPEERS, dtype=jnp.int32)
    slot_index = jnp.arange(SLOTS, dtype=jnp.int32)
    blocks = jnp.arange(NBD, dtype=jnp.int32)
    owner_rows = owners.transpose(0, 2, 1, 3)
    matches = (owner_rows[:, None, :, :, :, None] == target[None, :, None, None, None, None]) & ((blocks % SLOTS)[None, None, None, None, :, None] == slot_index[None, None, None, None, None, :])
    assigned = jnp.any(matches, axis=4)
    drawn_count = jax.random.randint(jax.random.fold_in(key, 13), assigned.shape, DPB // 4, DPB + 1)
    busy_owner = target[None, :, None, None, None] == busiest[..., None]
    counts = jnp.where(assigned, jnp.where(busy_owner, DPB, drawn_count), 0)
    return counts.reshape(XTILES, YTILES, ROWSLOTS)


def draw_patch_processor_map(key, part):
    owners, busiest = plan_owners(key)
    return owners.reshape(XTILES, YTILES, NBD).astype(jnp.int32)


def draw_particle_bucket_population(key, part):
    return plan_counts(key).astype(jnp.int32)


def draw_particle_location_number(key, part):
    counts = plan_counts(key)
    extent = (XTILES, YTILES, ROWSLOTS, DPB)
    column = jax.random.randint(jax.random.fold_in(key, 14), extent, 0, BCOL)
    alive_mask = jnp.arange(DPB, dtype=jnp.int32) < counts[..., None]
    ordered = jnp.sort(jnp.where(alive_mask, column, column + BCOL), axis=-1)
    column = jnp.where(ordered >= BCOL, ordered - BCOL, ordered)
    height = jax.random.randint(jax.random.fold_in(key, 15), extent, KLO, KHI)
    return (column * VERTICAL_LAYERS + height).astype(jnp.int32)


def level_of(key, shape, cuts, smallest, top_value):
    loudness = 1.0
    for dim, parts in cuts:
        draws = jax.random.uniform(jax.random.fold_in(jax.random.fold_in(key, 6), dim), (parts,), jnp.float32, smallest / len(cuts), top_value / len(cuts))
        loudness = loudness * jnp.repeat(jnp.exp(draws), shape[dim] // parts).reshape((-1,) + (1,) * (len(shape) - 1 - dim))
    return loudness


def gaussian(own_key, shape, scale, bound, split=(), kind=jnp.bfloat16):
    values = scale * jax.random.normal(own_key, shape, jnp.float32)
    if split:
        values = values * level_of(own_key, shape, split, -0.22, 0.18)
    return jnp.clip(values, -bound, bound).astype(kind)


def setup_inputs(seed: int = 0) -> dict:
    key_list = jax.random.split(jax.random.key(seed), 11)
    return {
        "theta_anomaly": gaussian(key_list[0], (SPAN_COUNT_EAST, SPAN_COUNT_NORTH, VERTICAL_LAYERS), 1.0, 4.0, ((0, 32), (1, 8)), jnp.float32),
        "humidity_ratio": jnp.clip(0.6 + 0.79999995 * jax.random.uniform(key_list[1], (SPAN_COUNT_EAST, SPAN_COUNT_NORTH, VERTICAL_LAYERS), jnp.float32) ** level_of(key_list[1], (SPAN_COUNT_EAST, SPAN_COUNT_NORTH, VERTICAL_LAYERS), ((0, 32), (1, 8)), -0.2, 0.2), 0.6, 1.4),
        "zonal_velocity": draw_zonal_velocity(jax.random.fold_in(key_list[10], 71), 0),
        "meridional_velocity": draw_meridional_velocity(jax.random.fold_in(key_list[10], 71), 0),
        "vertical_velocity": draw_vertical_velocity(jax.random.fold_in(key_list[10], 71), 0),
        "patch_processor_map": draw_patch_processor_map(jax.random.fold_in(key_list[10], 71), 0),
        "particle_bucket_population": draw_particle_bucket_population(jax.random.fold_in(key_list[10], 71), 0),
        "particle_size_quadratic": jnp.clip(jnp.exp(math.log(4.0) - 2.7725887 * jax.random.uniform(key_list[7], (XTILES, YTILES, ROWSLOTS, DPB), jnp.float32) ** level_of(key_list[7], (XTILES, YTILES, ROWSLOTS, DPB), ((0, 32), (1, 8)), -0.2, 0.2)), 0.25, 4.0),
        "represented_number": jnp.clip(jnp.exp(math.log(2.0) - 1.3862944 * jax.random.uniform(key_list[8], (XTILES, YTILES, ROWSLOTS, DPB), jnp.float32) ** level_of(key_list[8], (XTILES, YTILES, ROWSLOTS, DPB), ((0, 32), (1, 8)), -0.2, 0.2)), 0.5, 2.0),
        "particle_location_number": draw_particle_location_number(jax.random.fold_in(key_list[10], 71), 0),
    }


TIME_INCREMENT = 0.15
THERMAL_LIFT = 0.5
HUMID_LIFT = 0.3
HELMHOLTZ = 0.001
CLAUSIUS_FACTOR = 0.2
GROWTH = 0.5
GROWTH_SLOPE = 0.1
SUB_STEP = 0.25
CURVATURE = 0.05
FLOOR_SQUARE = 0.04
CONDENSE = 0.2
PHASE_WARMING = 2.5

def profiles():
    heights = jnp.arange(VERTICAL_LAYERS, dtype=jnp.float32)
    midpoint_mass_per_volume = jnp.exp(-(heights + 0.5) / VERTICAL_LAYERS)
    interface_mass_per_volume = jnp.where(heights < VERTICAL_LAYERS - 1, jnp.exp(-(heights + 1.0) / VERTICAL_LAYERS), 0.0)
    return (midpoint_mass_per_volume, interface_mass_per_volume)

def level_above(values):
    return jnp.concatenate([values[..., 1:], jnp.zeros_like(values[..., :1])], axis=-1)

def level_below(values):
    return jnp.concatenate([jnp.zeros_like(values[..., :1]), values[..., :-1]], axis=-1)

def beside_all(values):
    return (jnp.roll(values, -1, 0), jnp.roll(values, 1, 0), jnp.roll(values, -1, 1), jnp.roll(values, 1, 1))

def operate(values, midpoint_mass_per_volume, interface_mass_per_volume):
    east_side, west_side, north_side, south_side = beside_all(values)
    return midpoint_mass_per_volume * ((4.0 + HELMHOLTZ) * values - east_side - west_side - north_side - south_side) + interface_mass_per_volume * (values - level_above(values)) + level_below(interface_mass_per_volume) * (values - level_below(values))

def solve_pressure(right_side, midpoint_mass_per_volume, interface_mass_per_volume):
    potential = jnp.zeros_like(right_side)
    residual = right_side
    direction = right_side
    norm_now = jnp.sum(residual * residual)
    for iteration in range(ITERS):
        applied = operate(direction, midpoint_mass_per_volume, interface_mass_per_volume)
        step_length = norm_now / jnp.sum(direction * applied)
        potential = potential + step_length * direction
        residual = residual - step_length * applied
        norm_next = jnp.sum(residual * residual)
        direction = residual + norm_next / norm_now * direction
        norm_now = norm_next
    return potential

def advect_scalars(values, zonal_velocity, meridional_velocity, vertical_velocity):
    east_side, west_side, north_side, south_side = beside_all(values)
    lower_level = jnp.concatenate([values[..., :1], values[..., :-1]], axis=-1)
    upper_level = jnp.concatenate([values[..., 1:], values[..., -1:]], axis=-1)
    tendency = jnp.maximum(zonal_velocity, 0.0) * (values - west_side) + jnp.minimum(zonal_velocity, 0.0) * (east_side - values) + jnp.maximum(meridional_velocity, 0.0) * (values - south_side) + jnp.minimum(meridional_velocity, 0.0) * (north_side - values) + jnp.maximum(vertical_velocity, 0.0) * (values - lower_level) + jnp.minimum(vertical_velocity, 0.0) * (upper_level - values)
    return values - TIME_INCREMENT * tendency

def grow_droplets(supersat_ratio, warmth, particle_size_quadratic, represented_number, alive_mask):
    growth_rate = GROWTH * jnp.exp(GROWTH_SLOPE * warmth)
    square_now = particle_size_quadratic
    for substep in range(NSUB):
        square_now = jnp.maximum(square_now + 2.0 * SUB_STEP * growth_rate * (supersat_ratio - CURVATURE / jnp.sqrt(square_now)), FLOOR_SQUARE)
    grown_square = jnp.where(alive_mask, square_now, particle_size_quadratic)
    mass_change = jnp.where(alive_mask, represented_number * (grown_square * jnp.sqrt(grown_square) - particle_size_quadratic * jnp.sqrt(particle_size_quadratic)), 0.0)
    return (grown_square, mass_change)

def into_patches(values):
    shaped = values.reshape(XTILES, CX, YTILES, NBD, BY, VERTICAL_LAYERS)
    return shaped.transpose(0, 2, 3, 1, 4, 5).reshape(XTILES, YTILES, NBD, BCOL * VERTICAL_LAYERS)

def from_blocks(blocks):
    shaped = blocks.reshape(XTILES, YTILES, NBD, CX, BY, VERTICAL_LAYERS)
    return shaped.transpose(0, 3, 1, 2, 4, 5).reshape(SPAN_COUNT_EAST, SPAN_COUNT_NORTH, VERTICAL_LAYERS)

def reference(theta_anomaly, humidity_ratio, zonal_velocity, meridional_velocity, vertical_velocity, patch_processor_map, particle_bucket_population, particle_size_quadratic, represented_number, particle_location_number):
    midpoint_mass_per_volume, interface_mass_per_volume = profiles()
    tile_x = jnp.arange(XTILES, dtype=jnp.int32)[:, None, None]
    tile_y = jnp.arange(YTILES, dtype=jnp.int32)[None, :, None]
    block_index = jnp.arange(NBD, dtype=jnp.int32)[None, None, :]
    owner_row = (tile_x // XPEERS * XPEERS + patch_processor_map).astype(jnp.int32)
    slot_index = (tile_x % XPEERS * SLOTS + block_index % SLOTS).astype(jnp.int32)
    row_y = jnp.broadcast_to(tile_y, patch_processor_map.shape).astype(jnp.int32)
    block_count = particle_bucket_population[owner_row, row_y, slot_index]
    patch_location = particle_location_number[owner_row, row_y, slot_index]
    block_mult = represented_number[owner_row, row_y, slot_index]
    block_radius = particle_size_quadratic[owner_row, row_y, slot_index]
    alive_mask = jnp.arange(DPB, dtype=jnp.int32) < block_count[..., None]
    offsets = (jnp.arange(XTILES * YTILES * NBD, dtype=jnp.int32) * (BCOL * VERTICAL_LAYERS)).reshape(XTILES, YTILES, NBD, 1)
    flat_cell = (patch_location + offsets).reshape(-1)
    for stepping in range(NSTEP):
        raised_airmass = vertical_velocity + TIME_INCREMENT * (THERMAL_LIFT * theta_anomaly + HUMID_LIFT * humidity_ratio)
        divergence = midpoint_mass_per_volume * ((jnp.roll(zonal_velocity, -1, 0) - jnp.roll(zonal_velocity, 1, 0)) * 0.5 + (jnp.roll(meridional_velocity, -1, 1) - jnp.roll(meridional_velocity, 1, 1)) * 0.5) + 0.5 * (level_above(midpoint_mass_per_volume * raised_airmass) - level_below(midpoint_mass_per_volume * raised_airmass))
        potential = solve_pressure(-divergence / TIME_INCREMENT, midpoint_mass_per_volume, interface_mass_per_volume)
        zonal_velocity = zonal_velocity - TIME_INCREMENT * 0.5 * (jnp.roll(potential, -1, 0) - jnp.roll(potential, 1, 0))
        meridional_velocity = meridional_velocity - TIME_INCREMENT * 0.5 * (jnp.roll(potential, -1, 1) - jnp.roll(potential, 1, 1))
        vertical_velocity = raised_airmass - TIME_INCREMENT * 0.5 * (level_above(potential) - level_below(potential))
        advected_theta = advect_scalars(theta_anomaly, zonal_velocity, meridional_velocity, vertical_velocity)
        advected_humidity = advect_scalars(humidity_ratio, zonal_velocity, meridional_velocity, vertical_velocity)
        supersat_ratio = advected_humidity * jnp.exp(-CLAUSIUS_FACTOR * advected_theta) - 1.0
        sat_drops = jnp.take_along_axis(into_patches(supersat_ratio), patch_location, axis=3)
        grow_particles = jnp.take_along_axis(into_patches(advected_theta), patch_location, axis=3)
        block_radius, mass_change = grow_droplets(sat_drops, grow_particles, block_radius, block_mult, alive_mask)
        liquid_content = CONDENSE * jax.ops.segment_sum(mass_change.reshape(-1), flat_cell, num_segments=XTILES * YTILES * NBD * BCOL * VERTICAL_LAYERS)
        liquid_content = from_blocks(liquid_content.reshape(XTILES, YTILES, NBD, BCOL * VERTICAL_LAYERS))
        theta_anomaly = advected_theta + PHASE_WARMING * liquid_content
        humidity_ratio = advected_humidity - liquid_content
    final_size_quadratic = particle_size_quadratic.at[owner_row, row_y, slot_index].set(block_radius)
    return (theta_anomaly, humidity_ratio, zonal_velocity, meridional_velocity, vertical_velocity, final_size_quadratic)
```

```python
import functools

import jax
import jax.numpy as jnp
from jax import lax
from jax.experimental import pallas as pl
from jax.experimental.pallas import tpu as pltpu
from jax.sharding import PartitionSpec as P

TIME_INCREMENT = 0.15
THERMAL_LIFT = 0.5
HUMID_LIFT = 0.3
HELMHOLTZ = 0.001
CLAUSIUS_FACTOR = 0.2
GROWTH = 0.5
GROWTH_SLOPE = 0.1
SUB_STEP = 0.25
CURVATURE = 0.05
FLOOR_SQUARE = 0.04
CONDENSE = 0.2
PHASE_WARMING = 2.5

NSUB = 4
ITERS = 4
NBD = 8
CX = 24
CY = 16
LEVELS = 128
KLO = 48
BAND = 32
EX = 32
EY = 24
SLOT_ROWS = 16
DPB = 1024
CHUNKS = DPB // LEVELS
PARCEL = 32
SCALE = 1.0 / 6.0
VMEM_LIMIT = 24 * 1024 * 1024

f32 = jnp.float32
bf16 = jnp.bfloat16


def iota(shape, axis):
    return lax.broadcasted_iota(jnp.int32, shape, axis)


def vertical_profiles():
    level = iota((1, LEVELS), 1)
    height = level.astype(f32)
    centre = jnp.exp(-(height + 0.5) / LEVELS)
    face = jnp.where(level < LEVELS - 1, jnp.exp(-(height + 1.0) / LEVELS), 0.0)
    face_below = jnp.where(level > 0, jnp.exp(-height / LEVELS), 0.0)
    return level, centre, face, face_below


def turn(values, by, axis):
    return pltpu.roll(values, by % values.shape[axis], axis)


def lifted_row(i, theta, humidity, vertical):
    return vertical[i] + TIME_INCREMENT * (THERMAL_LIFT * theta[i] + HUMID_LIFT * humidity[i])


def right_side_kernel(theta, humidity, zonal, meridional, vertical, partial, to_south, to_north):
    level, centre, _, _ = vertical_profiles()
    sub = iota((CY, LEVELS), 0)
    sub8 = iota((8, LEVELS), 0)
    for i in range(CX):
        weighted = centre * lifted_row(i, theta, humidity, vertical)
        rise = jnp.where(level < LEVELS - 1, turn(weighted, -1, 1), 0.0) - jnp.where(
            level > 0, turn(weighted, 1, 1), 0.0
        )
        if i == 0:
            across = zonal[1]
        elif i == CX - 1:
            across = -zonal[CX - 2]
        else:
            across = zonal[i + 1] - zonal[i - 1]
        wind = meridional[i]
        along = jnp.where(sub < CY - 1, turn(wind, -1, 0), 0.0) - jnp.where(
            sub > 0, turn(wind, 1, 0), 0.0
        )
        right = (centre * (across * 0.5 + along * 0.5) + 0.5 * rise) * (-1.0 / TIME_INCREMENT)
        partial[i] = right
        warm = theta[i]
        damp = humidity[i]
        to_south[i] = jnp.where(
            sub8 < 4,
            right[0:8],
            jnp.where(sub8 == 4, wind[0:1], jnp.where(sub8 == 5, warm[0:1], damp[0:1])),
        )
        to_north[i] = jnp.where(
            sub8 >= 4,
            right[8:16],
            jnp.where(sub8 == 0, wind[15:16], jnp.where(sub8 == 1, warm[15:16], damp[15:16])),
        )
    for place, i in ((CX, 0), (CX + 1, CX - 1)):
        to_south[place] = zonal[i, 0:8]
        to_north[place] = zonal[i, 8:16]


def joined(north, south):
    return jnp.where(iota((8, LEVELS), 0) < 4, north, south)


def completed_row(i, partial, meridional, from_north, from_south, third):
    sub8 = iota((8, LEVELS), 0)
    north = from_north[i]
    south = from_south[i]
    wind = meridional[i]
    low = partial[i, 0:8] + jnp.where(sub8 == 0, third * south[0:1], 0.0)
    high = partial[i, 8:16] - jnp.where(sub8 == 7, third * north[4:5], 0.0)
    halo = (
        joined(north, south)
        + jnp.where(sub8 == 0, third * wind[15:16], 0.0)
        - jnp.where(sub8 == 7, third * wind[0:1], 0.0)
    )
    return low, high, halo


def side_kernel(
    partial, from_north, from_south, theta, humidity, zonal, meridional, to_west, to_east
):
    _, centre, _, _ = vertical_profiles()
    third = centre * (0.5 / TIME_INCREMENT)
    for target, first, edge, place in ((to_west, 0, 0, CX), (to_east, CX - 4, CX - 1, CX + 1)):
        for t in range(4):
            low, high, halo = completed_row(
                first + t, partial, meridional, from_north, from_south, third
            )
            target[t, 0:8] = low
            target[t, 8:16] = high
            target[t, 16:24] = halo
        target[4, 0:16] = zonal[edge]
        target[4, 16:24] = joined(from_north[place], from_south[place])
        target[5, 0:16] = theta[edge]
        target[5, 16:24] = jnp.zeros((8, LEVELS), f32)
        target[6, 0:16] = humidity[edge]
        target[6, 16:24] = jnp.zeros((8, LEVELS), f32)


def power_kernel(
    counts,
    partial,
    from_north,
    from_south,
    meridional,
    to_west,
    to_east,
    from_east,
    from_west,
    squares,
    numbers,
    cells,
    powers,
    parcels,
):
    _, centre, face, face_below = vertical_profiles()
    third = centre * (0.5 / TIME_INCREMENT)
    for i in range(4, CX - 4):
        low, high, halo = completed_row(i, partial, meridional, from_north, from_south, third)
        powers[0, i, 0:8] = low
        powers[0, i, 8:16] = high
        powers[0, i, 16:24] = halo
    for t in range(4):
        west = to_west[t]
        east = to_east[t]
        far_east = from_east[t]
        far_west = from_west[t]
        if t == 0:
            west = west + third * from_west[4]
            far_east = far_east + third * to_east[4]
        if t == 3:
            east = east - third * from_east[4]
            far_west = far_west - third * to_west[4]
        powers[0, t] = west
        powers[0, CX - 4 + t] = east
        powers[0, CX + t] = far_east
        powers[0, CX + 4 + t] = far_west
    here = ((4.0 + HELMHOLTZ) * centre + face + face_below) * SCALE
    beside = centre * SCALE
    above = face * SCALE
    below = face_below * SCALE

    def applied(j, i):
        values = powers[j, i]
        lateral = (
            powers[j, (i + 1) % EX]
            + powers[j, (i - 1) % EX]
            + turn(values, -1, 0)
            + turn(values, 1, 0)
        )
        return (
            here * values
            - beside * lateral
            - above * turn(values, -1, 1)
            - below * turn(values, 1, 1)
        )

    for j in range(ITERS - 1):
        reach = ITERS - 1 - j
        for i in range(-reach, CX + reach):
            powers[j + 1, i % EX] = applied(j, i % EX)
    sums = [jnp.zeros((8, LEVELS), f32) for _ in range(2 * ITERS)]
    for i in range(CX):
        rows = [powers[j, i, 0:16] for j in range(ITERS)]
        rows.append(applied(ITERS - 1, i)[0:16])
        for k in range(2 * ITERS):
            product = rows[k // 2] * rows[(k + 1) // 2]
            sums[k] = sums[k] + (product[0:8] + product[8:16])
    sub8 = iota((8, LEVELS), 0)
    packed = jnp.zeros((8, LEVELS), f32)
    for k in range(2 * ITERS):
        packed = jnp.where(sub8 == k, jnp.sum(sums[k], axis=0, keepdims=True), packed)
    for r in range(SLOT_ROWS):
        parcels[PARCEL * r + 24 : PARCEL * r + 32] = packed
    row = iota((SLOT_ROWS, LEVELS), 0)
    lane = iota((SLOT_ROWS, LEVELS), 1)
    live = jnp.zeros((SLOT_ROWS, LEVELS), jnp.int32)
    for r in range(SLOT_ROWS):
        live = jnp.where(row == r, counts[r], live)
    for s in range(CHUNKS):
        part = slice(LEVELS * s, LEVELS * (s + 1))
        parcels[pl.ds(s, SLOT_ROWS, stride=PARCEL), :] = squares[:, part]
        parcels[pl.ds(8 + s, SLOT_ROWS, stride=PARCEL), :] = jnp.where(
            lane + LEVELS * s < live, numbers[:, part], 0.0
        )
        parcels[pl.ds(16 + s, SLOT_ROWS, stride=PARCEL), :] = cells[:, part].astype(f32)


def two_sum(a, b):
    s = a + b
    t = s - a
    return s, (a - (s - t)) + (b - t)


def quick_sum(a, b):
    s = a + b
    return s, b - (s - a)


def split(a):
    t = a * 4097.0
    high = t - (t - a)
    return high, a - high


def two_product(a, b):
    p = a * b
    ah, al = split(a)
    bh, bl = split(b)
    return p, ((ah * bh - p) + ah * bl + al * bh) + al * bl


def pair_add(a, b):
    s, e = two_sum(a[0], b[0])
    return quick_sum(s, e + (a[1] + b[1]))


def pair_mul(a, b):
    p, e = two_product(a[0], b[0])
    return quick_sum(p, e + (a[0] * b[1] + a[1] * b[0]))


def pair_sub_mul(a, b, c):
    p = pair_mul(b, c)
    return pair_add(a, (-p[0], -p[1]))


def pair_inverse(a):
    guess = 1.0 / a[0]
    p = pair_mul(a, (guess, jnp.zeros_like(guess)))
    rest = (1.0 - p[0]) - p[1]
    return quick_sum(guess, guess * rest)


def coefficients(totals):
    high = totals[0]
    low = jnp.zeros_like(high)
    for t in range(1, totals.shape[0]):
        high, e = two_sum(high, totals[t])
        low = low + e
    by = LEVELS // 2
    high, low = quick_sum(high, low)
    while by:
        high, low = pair_add((high, low), (turn(high, by, 1), turn(low, by, 1)))
        by //= 2
    moment = []
    for k in range(2 * ITERS):
        moment.append(
            (
                jnp.broadcast_to(high[k : k + 1], (8, LEVELS)),
                jnp.broadcast_to(low[k : k + 1], (8, LEVELS)),
            )
        )
    matrix = [[moment[i + j + 1] for j in range(ITERS)] for i in range(ITERS)]
    side = [moment[i] for i in range(ITERS)]
    inverse = []
    for k in range(ITERS):
        inverse.append(pair_inverse(matrix[k][k]))
        for i in range(k + 1, ITERS):
            factor = pair_mul(matrix[k][i], inverse[k])
            for j in range(i, ITERS):
                matrix[i][j] = pair_sub_mul(matrix[i][j], factor, matrix[k][j])
            side[i] = pair_sub_mul(side[i], factor, side[k])
    result = [None] * ITERS
    for k in reversed(range(ITERS)):
        rest = side[k]
        for j in range(k + 1, ITERS):
            rest = pair_sub_mul(rest, matrix[k][j], result[j])
        result[k] = pair_mul(rest, inverse[k])
    return [(r[0] + r[1])[0:1] * SCALE for r in result]


def halves(values):
    high = values.astype(bf16).astype(f32)
    return high, values - high


def step_kernel(
    owners,
    totals,
    powers,
    arrived,
    theta,
    humidity,
    zonal,
    meridional,
    vertical,
    from_north,
    from_south,
    from_east,
    from_west,
    new_theta,
    new_humidity,
    new_zonal,
    new_meridional,
    new_vertical,
    returned,
    potential,
    excess,
    warmth,
    vapour,
    picked_excess,
    picked_warmth,
    mass,
    condensed,
):
    level, _, _, _ = vertical_profiles()
    sub = iota((CY, LEVELS), 0)
    weights = coefficients(totals)
    for t in range(CX + 2):
        i = (t - 1) % EX
        total = weights[0] * powers[0, i]
        for j in range(1, ITERS):
            total = total + weights[j] * powers[j, i]
        potential[t] = total
    half = TIME_INCREMENT * 0.5
    for i in range(CX):
        here = potential[i + 1]
        east = zonal[i] - half * (potential[i + 2, 0:16] - potential[i, 0:16])
        north = meridional[i] - half * (turn(here, -1, 0)[0:16] - turn(here, 1, 0)[0:16])
        mid = here[0:16]
        up = lifted_row(i, theta, humidity, vertical) - half * (
            jnp.where(level < LEVELS - 1, turn(mid, -1, 1), 0.0)
            - jnp.where(level > 0, turn(mid, 1, 1), 0.0)
        )
        new_zonal[i] = east
        new_meridional[i] = north
        new_vertical[i] = up
        moved = []
        for f, (field, side, in_north, in_south) in enumerate(
            ((theta, 5, 5, 1), (humidity, 6, 6, 2))
        ):
            values = field[i]
            f_e = field[i + 1] if i < CX - 1 else from_east[side, 0:16]
            f_w = field[i - 1] if i > 0 else from_west[side, 0:16]
            f_n = jnp.where(
                sub < CY - 1, turn(values, -1, 0), from_north[i, in_north : in_north + 1]
            )
            f_s = jnp.where(sub > 0, turn(values, 1, 0), from_south[i, in_south : in_south + 1])
            f_t = jnp.where(level < LEVELS - 1, turn(values, -1, 1), values)
            f_b = jnp.where(level > 0, turn(values, 1, 1), values)
            tendency = (
                jnp.maximum(east, 0.0) * (values - f_w)
                + jnp.minimum(east, 0.0) * (f_e - values)
                + jnp.maximum(north, 0.0) * (values - f_s)
                + jnp.minimum(north, 0.0) * (f_n - values)
                + jnp.maximum(up, 0.0) * (values - f_b)
                + jnp.minimum(up, 0.0) * (f_t - values)
            )
            moved.append(values - TIME_INCREMENT * tendency)
        rows = slice(CY * i, CY * (i + 1))
        warmth[rows] = moved[0]
        vapour[rows] = moved[1]
        excess[rows] = moved[1] * jnp.exp(-CLAUSIUS_FACTOR * moved[0]) - 1.0

    lane = iota((2 * CX, LEVELS), 1)
    height = iota((BAND, 2 * LEVELS), 0)
    place = iota((2 * CX, 2 * LEVELS), 0)

    def band(field, b):
        values = jnp.concatenate(
            [
                field[pl.ds(2 * b, CX, stride=CY), :],
                field[pl.ds(2 * b + 1, CX, stride=CY), :],
            ],
            axis=0,
        )
        high, low = halves(values)
        both = jnp.where(lane < BAND, turn(high, -KLO, 1), turn(low, BAND - KLO, 1))
        return both[:, : 2 * BAND].astype(bf16)

    def chunk(values, t):
        return jnp.concatenate([values[2 * t : 2 * t + 1], values[2 * t + 1 : 2 * t + 2]], axis=1)

    def where_at(b):
        cell = arrived[owners[b], 16:24].astype(jnp.int32)
        column = lax.shift_right_logical(cell, 7)
        return (
            jnp.bitwise_and(cell, LEVELS - 1) - KLO,
            jnp.bitwise_and(column, 1) * CX + lax.shift_right_logical(column, 1),
        )

    for b in range(NBD):
        table = jnp.concatenate([band(excess, b), band(warmth, b)], axis=0)
        heights, places = where_at(b)
        for t in range(CHUNKS // 2):
            hot = jnp.where(height == chunk(heights, t), 1.0, 0.0).astype(bf16)
            found = jnp.dot(
                table, jnp.concatenate([hot, hot], axis=0), preferred_element_type=f32
            )
            mine = place == chunk(places, t)
            for target, part in ((picked_excess, found[: 2 * CX]), (picked_warmth, found[2 * CX :])):
                value = jnp.sum(jnp.where(mine, part, 0.0), axis=0, keepdims=True)
                row = CHUNKS * b + 2 * t
                target[row : row + 1] = value[:, :LEVELS]
                target[row + 1 : row + 2] = value[:, LEVELS:]
    returned[...] = jnp.zeros(returned.shape, f32)
    for b in range(NBD):
        rows = slice(CHUNKS * b, CHUNKS * (b + 1))
        owner = owners[b]
        old = arrived[owner, 0:8]
        number = arrived[owner, 8:16]
        oversaturation = picked_excess[rows]
        rate = GROWTH * jnp.exp(GROWTH_SLOPE * picked_warmth[rows])
        now = old
        for substep in range(NSUB):
            now = jnp.maximum(
                now + 2.0 * SUB_STEP * rate * (oversaturation - CURVATURE / jnp.sqrt(now)),
                FLOOR_SQUARE,
            )
        mass[rows] = jnp.where(
            number > 0.0, number * (now * jnp.sqrt(now) - old * jnp.sqrt(old)), 0.0
        )
        returned[owner] = now
    for b in range(NBD):
        heights, places = where_at(b)
        gained = mass[CHUNKS * b : CHUNKS * (b + 1)]
        total = jnp.zeros((4 * CX, BAND), f32)
        for t in range(CHUNKS // 2):
            hot = jnp.where(height == chunk(heights, t), 1.0, 0.0).astype(bf16)
            mine = place == chunk(places, t)
            high, low = halves(chunk(gained, t))
            spread = jnp.concatenate(
                [
                    jnp.where(mine, high, 0.0).astype(bf16),
                    jnp.where(mine, low, 0.0).astype(bf16),
                ],
                axis=0,
            )
            total = total + lax.dot_general(
                spread, hot, (((1,), (1,)), ((), ())), preferred_element_type=f32
            )
        liquid = CONDENSE * (total[: 2 * CX] + total[2 * CX :])
        liquid = jnp.concatenate([liquid, jnp.zeros((2 * CX, LEVELS - BAND), f32)], axis=1)
        liquid = turn(liquid, KLO, 1)
        condensed[pl.ds(2 * b, CX, stride=CY), :] = liquid[:CX]
        condensed[pl.ds(2 * b + 1, CX, stride=CY), :] = liquid[CX:]
    for i in range(CX):
        rows = slice(CY * i, CY * (i + 1))
        new_theta[i] = warmth[rows] + PHASE_WARMING * condensed[rows]
        new_humidity[i] = vapour[rows] - condensed[rows]


def size_kernel(counts, returned, squares, new_squares):
    row = iota((SLOT_ROWS, LEVELS), 0)
    lane = iota((SLOT_ROWS, LEVELS), 1)
    live = jnp.zeros((SLOT_ROWS, LEVELS), jnp.int32)
    for r in range(SLOT_ROWS):
        live = jnp.where(row == r, counts[r], live)
    for s in range(CHUNKS):
        part = slice(LEVELS * s, LEVELS * (s + 1))
        new_squares[:, part] = jnp.where(
            lane + LEVELS * s < live,
            returned[pl.ds(s, SLOT_ROWS, stride=CHUNKS), :],
            squares[:, part],
        )


def local(kernel, outs, scalars, operands, scratch=(), cost=(1_000_000, 1_000_000)):
    whole = pl.BlockSpec(memory_space=pltpu.VMEM)
    single = len(outs) == 1
    return pl.pallas_call(
        kernel,
        out_shape=outs[0] if single else outs,
        in_specs=[pl.BlockSpec(memory_space=pltpu.SMEM)] * len(scalars) + [whole] * len(operands),
        out_specs=whole if single else [whole] * len(outs),
        scratch_shapes=list(scratch),
        compiler_params=pltpu.CompilerParams(vmem_limit_bytes=VMEM_LIMIT),
        cost_estimate=pl.CostEstimate(flops=cost[0], bytes_accessed=cost[1], transcendentals=0),
    )(*scalars, *operands)


def shape(*dims):
    return jax.ShapeDtypeStruct(dims, f32)


def ring(axes, step):
    count = lax.axis_size(axes)
    return [(i, (i + step) % count) for i in range(count)]


def on_device(
    theta, humidity, zonal, meridional, vertical, owner_map, population, squares, numbers, cells
):
    owners = owner_map.reshape(NBD)
    counts = population.reshape(SLOT_ROWS)
    squares = squares.reshape(SLOT_ROWS, DPB)
    numbers = numbers.reshape(SLOT_ROWS, DPB)
    cells = cells.reshape(SLOT_ROWS, DPB)
    tiles = ("grp", "gx")
    tile = shape(CX, CY, LEVELS)
    partial, to_south, to_north = local(
        right_side_kernel,
        [tile, shape(CX + 2, 8, LEVELS), shape(CX + 2, 8, LEVELS)],
        [],
        [theta, humidity, zonal, meridional, vertical],
    )
    from_north = lax.ppermute(to_south, "gy", ring("gy", -1))
    from_south = lax.ppermute(to_north, "gy", ring("gy", 1))
    to_west, to_east = local(
        side_kernel,
        [shape(7, EY, LEVELS), shape(7, EY, LEVELS)],
        [],
        [partial, from_north, from_south, theta, humidity, zonal, meridional],
    )
    from_east = lax.ppermute(to_west, tiles, ring(tiles, -1))
    from_west = lax.ppermute(to_east, tiles, ring(tiles, 1))
    powers, parcels = local(
        power_kernel,
        [shape(ITERS, EX, EY, LEVELS), shape(SLOT_ROWS * PARCEL, LEVELS)],
        [counts],
        [
            partial,
            from_north,
            from_south,
            meridional,
            to_west,
            to_east,
            from_east,
            from_west,
            squares,
            numbers,
            cells,
        ],
    )
    parcels = parcels.reshape(SLOT_ROWS, PARCEL, LEVELS)
    arrived = lax.all_to_all(parcels, "gx", split_axis=0, concat_axis=0, tiled=True)
    shared = jnp.broadcast_to(jnp.sum(arrived[:, 24:], axis=0)[None], (16, 8, LEVELS))
    totals = lax.all_to_all(shared, ("grp", "gy"), split_axis=0, concat_axis=0, tiled=True)
    flat = (CX * CY, LEVELS)
    picked = (NBD * CHUNKS, LEVELS)
    new_theta, new_humidity, new_zonal, new_meridional, new_vertical, returned = local(
        step_kernel,
        [tile] * 5 + [shape(SLOT_ROWS, CHUNKS, LEVELS)],
        [owners],
        [
            totals,
            powers,
            arrived,
            theta,
            humidity,
            zonal,
            meridional,
            vertical,
            from_north,
            from_south,
            from_east,
            from_west,
        ],
        [pltpu.VMEM((CX + 2, EY, LEVELS), f32)]
        + [pltpu.VMEM(flat, f32)] * 3
        + [pltpu.VMEM(picked, f32)] * 3
        + [pltpu.VMEM(flat, f32)],
    )
    returned = lax.all_to_all(returned, "gx", split_axis=0, concat_axis=0, tiled=True)
    new_squares = local(
        size_kernel,
        [shape(SLOT_ROWS, DPB)],
        [counts],
        [returned.reshape(SLOT_ROWS * CHUNKS, LEVELS), squares],
    )
    return (
        new_theta,
        new_humidity,
        new_zonal,
        new_meridional,
        new_vertical,
        new_squares[None, None],
    )


def solution(mesh):
    field = P(("grp", "gx"), "gy", None)
    slots = P(("grp", "gx"), "gy", None, None)
    return jax.shard_map(
        on_device,
        mesh=mesh,
        in_specs=(field,) * 7 + (slots,) * 3,
        out_specs=(field,) * 5 + (slots,),
        check_vma=False,
    )
```

```python
import functools

import jax
import jax.numpy as jnp
from jax import lax
from jax.experimental import pallas as pl
from jax.experimental.pallas import tpu as pltpu
from jax.sharding import PartitionSpec as P

TIME_INCREMENT = 0.15
THERMAL_LIFT = 0.5
HUMID_LIFT = 0.3
HELMHOLTZ = 0.001
CLAUSIUS_FACTOR = 0.2
GROWTH = 0.5
GROWTH_SLOPE = 0.1
SUB_STEP = 0.25
CURVATURE = 0.05
FLOOR_SQUARE = 0.04
CONDENSE = 0.2
PHASE_WARMING = 2.5

NSUB = 4
ITERS = 4
NBD = 8
CX = 24
CY = 16
LEVELS = 128
KLO = 48
BAND = 32
EX = 32
EY = 24
SLOT_ROWS = 16
DPB = 1024
CHUNKS = DPB // LEVELS
DROPS = 24
PARCEL = 32
SCALE = 1.0 / 6.0
PACK_LIMIT = 24 * 1024 * 1024
VMEM_LIMIT = 24 * 1024 * 1024
FIRST_LIMIT = 54600 * 1024

f32 = jnp.float32
bf16 = jnp.bfloat16


def iota(shape, axis):
    return lax.broadcasted_iota(jnp.int32, shape, axis)


def vertical_profiles():
    level = iota((1, LEVELS), 1)
    height = level.astype(f32)
    centre = jnp.exp(-(height + 0.5) / LEVELS)
    face = jnp.where(level < LEVELS - 1, jnp.exp(-(height + 1.0) / LEVELS), 0.0)
    face_below = jnp.where(level > 0, jnp.exp(-height / LEVELS), 0.0)
    return level, centre, face, face_below


def turn(values, by, axis):
    return pltpu.roll(values, by % values.shape[axis], axis)


def lifted_row(i, theta, humidity, vertical):
    return vertical[i] + TIME_INCREMENT * (THERMAL_LIFT * theta[i] + HUMID_LIFT * humidity[i])


def right_side_kernel(
    theta_far,
    humidity_far,
    zonal_far,
    meridional_far,
    vertical_far,
    partial,
    to_south,
    to_north,
    edges,
    theta,
    humidity,
    zonal,
    meridional,
    vertical,
    arrivals,
):
    copies = [
        pltpu.make_async_copy(far, near, arrivals.at[n])
        for n, (far, near) in enumerate(
            (
                (theta_far, theta),
                (humidity_far, humidity),
                (zonal_far, zonal),
                (meridional_far, meridional),
                (vertical_far, vertical),
            )
        )
    ]
    for copy in copies:
        copy.start()
    for copy in copies:
        copy.wait()
    level, centre, _, _ = vertical_profiles()
    sub = iota((CY, LEVELS), 0)
    sub8 = iota((8, LEVELS), 0)
    for i in range(CX):
        weighted = centre * lifted_row(i, theta, humidity, vertical)
        rise = jnp.where(level < LEVELS - 1, turn(weighted, -1, 1), 0.0) - jnp.where(
            level > 0, turn(weighted, 1, 1), 0.0
        )
        if i == 0:
            across = zonal[1]
        elif i == CX - 1:
            across = -zonal[CX - 2]
        else:
            across = zonal[i + 1] - zonal[i - 1]
        wind = meridional[i]
        along = jnp.where(sub < CY - 1, turn(wind, -1, 0), 0.0) - jnp.where(
            sub > 0, turn(wind, 1, 0), 0.0
        )
        right = (centre * (across * 0.5 + along * 0.5) + 0.5 * rise) * (-1.0 / TIME_INCREMENT)
        partial[i] = right
        warm = theta[i]
        damp = humidity[i]
        to_south[i] = jnp.where(
            sub8 < 4,
            right[0:8],
            jnp.where(sub8 == 4, wind[0:1], jnp.where(sub8 == 5, warm[0:1], damp[0:1])),
        )
        to_north[i] = jnp.where(
            sub8 >= 4,
            right[8:16],
            jnp.where(sub8 == 0, wind[15:16], jnp.where(sub8 == 1, warm[15:16], damp[15:16])),
        )
    for n, i in enumerate((0, CX - 1)):
        to_south[CX + n] = zonal[i, 0:8]
        to_north[CX + n] = zonal[i, 8:16]
        edges[7 * n + 4] = zonal[i]
        edges[7 * n + 5] = theta[i]
        edges[7 * n + 6] = humidity[i]
    for t in range(4):
        edges[t] = meridional[t]
        edges[7 + t] = meridional[CX - 4 + t]


def joined(north, south):
    return jnp.where(iota((8, LEVELS), 0) < 4, north, south)


def completed_row(i, partial, wind, from_north, from_south, third):
    sub8 = iota((8, LEVELS), 0)
    north = from_north[i]
    south = from_south[i]
    low = partial[i, 0:8] + jnp.where(sub8 == 0, third * south[0:1], 0.0)
    high = partial[i, 8:16] - jnp.where(sub8 == 7, third * north[4:5], 0.0)
    halo = (
        joined(north, south)
        + jnp.where(sub8 == 0, third * wind[15:16], 0.0)
        - jnp.where(sub8 == 7, third * wind[0:1], 0.0)
    )
    return low, high, halo


def side_kernel(partial, from_north, from_south, edges, to_west, to_east):
    _, centre, _, _ = vertical_profiles()
    third = centre * (0.5 / TIME_INCREMENT)
    for n, (target, first) in enumerate(((to_west, 0), (to_east, CX - 4))):
        for t in range(4):
            low, high, halo = completed_row(
                first + t, partial, edges[7 * n + t], from_north, from_south, third
            )
            target[t, 0:8] = low
            target[t, 8:16] = high
            target[t, 16:24] = halo
        target[4, 0:16] = edges[7 * n + 4]
        target[4, 16:24] = joined(from_north[CX + n], from_south[CX + n])
        for t in (5, 6):
            target[t, 0:16] = edges[7 * n + t]
            target[t, 16:24] = jnp.zeros((8, LEVELS), f32)


def pack_kernel(
    counts, squares_far, numbers_far, cells_far, drops, squares, numbers, cells, arrivals
):
    copies = [
        pltpu.make_async_copy(far, near, arrivals.at[n])
        for n, (far, near) in enumerate(
            ((squares_far, squares), (numbers_far, numbers), (cells_far, cells))
        )
    ]
    for copy in copies:
        copy.start()
    for copy in copies:
        copy.wait()
    row = iota((SLOT_ROWS, LEVELS), 0)
    lane = iota((SLOT_ROWS, LEVELS), 1)
    live = jnp.zeros((SLOT_ROWS, LEVELS), jnp.int32)
    for r in range(SLOT_ROWS):
        live = jnp.where(row == r, counts[r], live)
    for s in range(CHUNKS):
        part = slice(LEVELS * s, LEVELS * (s + 1))
        drops[pl.ds(s, SLOT_ROWS, stride=DROPS), :] = squares[:, part]
        drops[pl.ds(8 + s, SLOT_ROWS, stride=DROPS), :] = jnp.where(
            lane + LEVELS * s < live, numbers[:, part], 0.0
        )
        drops[pl.ds(16 + s, SLOT_ROWS, stride=DROPS), :] = cells[:, part].astype(f32)


def power_kernel(
    partial,
    from_north,
    from_south,
    meridional,
    to_west,
    to_east,
    from_east,
    from_west,
    drops,
    powers,
    parcels,
):
    _, centre, face, face_below = vertical_profiles()
    third = centre * (0.5 / TIME_INCREMENT)
    for i in range(4, CX - 4):
        low, high, halo = completed_row(i, partial, meridional[i], from_north, from_south, third)
        powers[0, i, 0:8] = low
        powers[0, i, 8:16] = high
        powers[0, i, 16:24] = halo
    for t in range(4):
        west = to_west[t]
        east = to_east[t]
        far_east = from_east[t]
        far_west = from_west[t]
        if t == 0:
            west = west + third * from_west[4]
            far_east = far_east + third * to_east[4]
        if t == 3:
            east = east - third * from_east[4]
            far_west = far_west - third * to_west[4]
        powers[0, t] = west
        powers[0, CX - 4 + t] = east
        powers[0, CX + t] = far_east
        powers[0, CX + 4 + t] = far_west
    here = ((4.0 + HELMHOLTZ) * centre + face + face_below) * SCALE
    beside = centre * SCALE
    above = face * SCALE
    below = face_below * SCALE

    def applied(j, i):
        values = powers[j, i]
        lateral = (
            powers[j, (i + 1) % EX]
            + powers[j, (i - 1) % EX]
            + turn(values, -1, 0)
            + turn(values, 1, 0)
        )
        return (
            here * values
            - beside * lateral
            - above * turn(values, -1, 1)
            - below * turn(values, 1, 1)
        )

    for j in range(ITERS - 1):
        reach = ITERS - 1 - j
        for i in range(-reach, CX + reach):
            powers[j + 1, i % EX] = applied(j, i % EX)
    sums = [jnp.zeros((8, LEVELS), f32) for _ in range(2 * ITERS)]
    for i in range(CX):
        rows = [powers[j, i, 0:16] for j in range(ITERS)]
        rows.append(applied(ITERS - 1, i)[0:16])
        for k in range(2 * ITERS):
            product = rows[k // 2] * rows[(k + 1) // 2]
            sums[k] = sums[k] + (product[0:8] + product[8:16])
    sub8 = iota((8, LEVELS), 0)
    packed = jnp.zeros((8, LEVELS), f32)
    for k in range(2 * ITERS):
        packed = jnp.where(sub8 == k, jnp.sum(sums[k], axis=0, keepdims=True), packed)
    for r in range(SLOT_ROWS):
        parcels[r, 0:DROPS] = drops[DROPS * r : DROPS * (r + 1)]
        parcels[r, DROPS:PARCEL] = packed


def two_sum(a, b):
    s = a + b
    t = s - a
    return s, (a - (s - t)) + (b - t)


def quick_sum(a, b):
    s = a + b
    return s, b - (s - a)


def split(a):
    t = a * 4097.0
    high = t - (t - a)
    return high, a - high


def two_product(a, b):
    p = a * b
    ah, al = split(a)
    bh, bl = split(b)
    return p, ((ah * bh - p) + ah * bl + al * bh) + al * bl


def pair_add(a, b):
    s, e = two_sum(a[0], b[0])
    return quick_sum(s, e + (a[1] + b[1]))


def pair_mul(a, b):
    p, e = two_product(a[0], b[0])
    return quick_sum(p, e + (a[0] * b[1] + a[1] * b[0]))


def pair_sub_mul(a, b, c):
    p = pair_mul(b, c)
    return pair_add(a, (-p[0], -p[1]))


def pair_inverse(a):
    guess = 1.0 / a[0]
    p = pair_mul(a, (guess, jnp.zeros_like(guess)))
    rest = (1.0 - p[0]) - p[1]
    return quick_sum(guess, guess * rest)


def coefficients(totals):
    high = totals[0]
    low = jnp.zeros_like(high)
    for t in range(1, totals.shape[0]):
        high, e = two_sum(high, totals[t])
        low = low + e
    by = LEVELS // 2
    high, low = quick_sum(high, low)
    while by:
        high, low = pair_add((high, low), (turn(high, by, 1), turn(low, by, 1)))
        by //= 2
    moment = []
    for k in range(2 * ITERS):
        moment.append(
            (
                jnp.broadcast_to(high[k : k + 1], (8, LEVELS)),
                jnp.broadcast_to(low[k : k + 1], (8, LEVELS)),
            )
        )
    matrix = [[moment[i + j + 1] for j in range(ITERS)] for i in range(ITERS)]
    side = [moment[i] for i in range(ITERS)]
    inverse = []
    for k in range(ITERS):
        inverse.append(pair_inverse(matrix[k][k]))
        for i in range(k + 1, ITERS):
            factor = pair_mul(matrix[k][i], inverse[k])
            for j in range(i, ITERS):
                matrix[i][j] = pair_sub_mul(matrix[i][j], factor, matrix[k][j])
            side[i] = pair_sub_mul(side[i], factor, side[k])
    result = [None] * ITERS
    for k in reversed(range(ITERS)):
        rest = side[k]
        for j in range(k + 1, ITERS):
            rest = pair_sub_mul(rest, matrix[k][j], result[j])
        result[k] = pair_mul(rest, inverse[k])
    return [(r[0] + r[1])[0:1] * SCALE for r in result]


def halves(values):
    high = values.astype(bf16).astype(f32)
    return high, values - high


HALF = TIME_INCREMENT * 0.5


def new_winds(i, potential, theta, humidity, zonal, meridional, vertical):
    level = iota((1, LEVELS), 1)
    here = potential[i + 1]
    mid = here[0:16]
    east = zonal[i] - HALF * (potential[i + 2, 0:16] - potential[i, 0:16])
    north = meridional[i] - HALF * (turn(here, -1, 0)[0:16] - turn(here, 1, 0)[0:16])
    up = lifted_row(i, theta, humidity, vertical) - HALF * (
        jnp.where(level < LEVELS - 1, turn(mid, -1, 1), 0.0)
        - jnp.where(level > 0, turn(mid, 1, 1), 0.0)
    )
    return east, north, up


def chunk(values, t):
    return jnp.concatenate([values[2 * t : 2 * t + 1], values[2 * t + 1 : 2 * t + 2]], axis=1)


def where_at(arrived, owner):
    cell = arrived[owner, 16:24].astype(jnp.int32)
    column = lax.shift_right_logical(cell, 7)
    return (
        jnp.bitwise_and(cell, LEVELS - 1) - KLO,
        jnp.bitwise_and(column, 1) * CX + lax.shift_right_logical(column, 1),
    )


def growth_kernel(
    owners,
    totals,
    powers,
    arrived,
    theta,
    humidity,
    zonal,
    meridional,
    vertical,
    from_north,
    from_south,
    from_east,
    from_west,
    returned,
    potential,
    warmth,
    vapour,
    mass,
    excess,
    picked_excess,
    picked_warmth,
):
    level, _, _, _ = vertical_profiles()
    sub = iota((CY, LEVELS), 0)
    weights = coefficients(totals)
    for t in range(CX + 2):
        i = (t - 1) % EX
        total = weights[0] * powers[0, i]
        for j in range(1, ITERS):
            total = total + weights[j] * powers[j, i]
        potential[t] = total
    for i in range(CX):
        east, north, up = new_winds(i, potential, theta, humidity, zonal, meridional, vertical)
        moved = []
        for f, (field, side, in_north, in_south) in enumerate(
            ((theta, 5, 5, 1), (humidity, 6, 6, 2))
        ):
            values = field[i]
            f_e = field[i + 1] if i < CX - 1 else from_east[side, 0:16]
            f_w = field[i - 1] if i > 0 else from_west[side, 0:16]
            f_n = jnp.where(
                sub < CY - 1, turn(values, -1, 0), from_north[i, in_north : in_north + 1]
            )
            f_s = jnp.where(sub > 0, turn(values, 1, 0), from_south[i, in_south : in_south + 1])
            f_t = jnp.where(level < LEVELS - 1, turn(values, -1, 1), values)
            f_b = jnp.where(level > 0, turn(values, 1, 1), values)
            tendency = (
                jnp.maximum(east, 0.0) * (values - f_w)
                + jnp.minimum(east, 0.0) * (f_e - values)
                + jnp.maximum(north, 0.0) * (values - f_s)
                + jnp.minimum(north, 0.0) * (f_n - values)
                + jnp.maximum(up, 0.0) * (values - f_b)
                + jnp.minimum(up, 0.0) * (f_t - values)
            )
            moved.append(values - TIME_INCREMENT * tendency)
        rows = slice(CY * i, CY * (i + 1))
        warmth[rows] = moved[0]
        vapour[rows] = moved[1]
        excess[rows] = moved[1] * jnp.exp(-CLAUSIUS_FACTOR * moved[0]) - 1.0

    lane = iota((2 * CX, LEVELS), 1)
    height = iota((BAND, 2 * LEVELS), 0)
    place = iota((2 * CX, 2 * LEVELS), 0)

    def band(field, b):
        values = jnp.concatenate(
            [
                field[pl.ds(2 * b, CX, stride=CY), :],
                field[pl.ds(2 * b + 1, CX, stride=CY), :],
            ],
            axis=0,
        )
        high, low = halves(values)
        both = jnp.where(lane < BAND, turn(high, -KLO, 1), turn(low, BAND - KLO, 1))
        return both[:, : 2 * BAND].astype(bf16)

    for b in range(NBD):
        table = jnp.concatenate([band(excess, b), band(warmth, b)], axis=0)
        heights, places = where_at(arrived, owners[b])
        for t in range(CHUNKS // 2):
            hot = jnp.where(height == chunk(heights, t), 1.0, 0.0).astype(bf16)
            found = jnp.dot(
                table, jnp.concatenate([hot, hot], axis=0), preferred_element_type=f32
            )
            mine = place == chunk(places, t)
            for target, part in ((picked_excess, found[: 2 * CX]), (picked_warmth, found[2 * CX :])):
                value = jnp.sum(jnp.where(mine, part, 0.0), axis=0, keepdims=True)
                row = CHUNKS * b + 2 * t
                target[row : row + 1] = value[:, :LEVELS]
                target[row + 1 : row + 2] = value[:, LEVELS:]
    returned[...] = jnp.zeros(returned.shape, f32)
    for b in range(NBD):
        rows = slice(CHUNKS * b, CHUNKS * (b + 1))
        owner = owners[b]
        old = arrived[owner, 0:8]
        number = arrived[owner, 8:16]
        oversaturation = picked_excess[rows]
        rate = GROWTH * jnp.exp(GROWTH_SLOPE * picked_warmth[rows])
        now = old
        for substep in range(NSUB):
            now = jnp.maximum(
                now + 2.0 * SUB_STEP * rate * (oversaturation - CURVATURE / jnp.sqrt(now)),
                FLOOR_SQUARE,
            )
        mass[rows] = jnp.where(
            number > 0.0, number * (now * jnp.sqrt(now) - old * jnp.sqrt(old)), 0.0
        )
        returned[owner] = now


def condense_kernel(
    owners,
    potential,
    warmth,
    vapour,
    mass,
    arrived,
    theta,
    humidity,
    zonal,
    meridional,
    vertical,
    new_theta,
    new_humidity,
    new_zonal,
    new_meridional,
    new_vertical,
    condensed,
):
    for i in range(CX):
        new_zonal[i], new_meridional[i], new_vertical[i] = new_winds(
            i, potential, theta, humidity, zonal, meridional, vertical
        )
    height = iota((BAND, 2 * LEVELS), 0)
    place = iota((2 * CX, 2 * LEVELS), 0)
    for b in range(NBD):
        heights, places = where_at(arrived, owners[b])
        gained = mass[CHUNKS * b : CHUNKS * (b + 1)]
        total = jnp.zeros((4 * CX, BAND), f32)
        for t in range(CHUNKS // 2):
            hot = jnp.where(height == chunk(heights, t), 1.0, 0.0).astype(bf16)
            mine = place == chunk(places, t)
            high, low = halves(chunk(gained, t))
            spread = jnp.concatenate(
                [
                    jnp.where(mine, high, 0.0).astype(bf16),
                    jnp.where(mine, low, 0.0).astype(bf16),
                ],
                axis=0,
            )
            total = total + lax.dot_general(
                spread, hot, (((1,), (1,)), ((), ())), preferred_element_type=f32
            )
        liquid = CONDENSE * (total[: 2 * CX] + total[2 * CX :])
        liquid = jnp.concatenate([liquid, jnp.zeros((2 * CX, LEVELS - BAND), f32)], axis=1)
        liquid = turn(liquid, KLO, 1)
        condensed[pl.ds(2 * b, CX, stride=CY), :] = liquid[:CX]
        condensed[pl.ds(2 * b + 1, CX, stride=CY), :] = liquid[CX:]
    for i in range(CX):
        rows = slice(CY * i, CY * (i + 1))
        new_theta[i] = warmth[rows] + PHASE_WARMING * condensed[rows]
        new_humidity[i] = vapour[rows] - condensed[rows]


def size_kernel(counts, returned, squares, new_squares):
    row = iota((SLOT_ROWS, LEVELS), 0)
    lane = iota((SLOT_ROWS, LEVELS), 1)
    live = jnp.zeros((SLOT_ROWS, LEVELS), jnp.int32)
    for r in range(SLOT_ROWS):
        live = jnp.where(row == r, counts[r], live)
    for s in range(CHUNKS):
        part = slice(LEVELS * s, LEVELS * (s + 1))
        new_squares[:, part] = jnp.where(
            lane + LEVELS * s < live,
            returned[pl.ds(s, SLOT_ROWS, stride=CHUNKS), :],
            squares[:, part],
        )


def local(kernel, outs, scalars, operands, scratch=(), far=0, limit=VMEM_LIMIT, cost=1_000_000):
    whole = pl.BlockSpec(memory_space=pltpu.VMEM)
    single = len(outs) == 1
    return pl.pallas_call(
        kernel,
        out_shape=outs[0] if single else outs,
        in_specs=[pl.BlockSpec(memory_space=pltpu.SMEM)] * len(scalars)
        + [pl.BlockSpec(memory_space=pltpu.HBM)] * far
        + [whole] * (len(operands) - far),
        out_specs=whole if single else [whole] * len(outs),
        scratch_shapes=list(scratch),
        compiler_params=pltpu.CompilerParams(vmem_limit_bytes=limit),
        cost_estimate=pl.CostEstimate(flops=cost, bytes_accessed=cost, transcendentals=0),
    )(*scalars, *operands)


def shape(*dims):
    return jax.ShapeDtypeStruct(dims, f32)


def ring(axes, step):
    count = lax.axis_size(axes)
    return [(i, (i + step) % count) for i in range(count)]


def on_device(
    theta, humidity, zonal, meridional, vertical, owner_map, population, squares, numbers, cells
):
    owners = owner_map.reshape(NBD)
    counts = population.reshape(SLOT_ROWS)
    squares = squares.reshape(SLOT_ROWS, DPB)
    numbers = numbers.reshape(SLOT_ROWS, DPB)
    cells = cells.reshape(SLOT_ROWS, DPB)
    tiles = ("grp", "gx")
    tile = shape(CX, CY, LEVELS)
    partial, to_south, to_north, edges = local(
        right_side_kernel,
        [tile, shape(CX + 2, 8, LEVELS), shape(CX + 2, 8, LEVELS), shape(14, CY, LEVELS)],
        [],
        [theta, humidity, zonal, meridional, vertical],
        [pltpu.VMEM((CX, CY, LEVELS), f32)] * 5 + [pltpu.SemaphoreType.DMA((5,))],
        far=5,
        limit=FIRST_LIMIT,
    )
    from_north = lax.ppermute(to_south, "gy", ring("gy", -1))
    from_south = lax.ppermute(to_north, "gy", ring("gy", 1))
    to_west, to_east = local(
        side_kernel,
        [shape(7, EY, LEVELS), shape(7, EY, LEVELS)],
        [],
        [partial, from_north, from_south, edges],
    )
    from_east = lax.ppermute(to_west, tiles, ring(tiles, -1))
    from_west = lax.ppermute(to_east, tiles, ring(tiles, 1))
    drops = local(
        pack_kernel,
        [shape(SLOT_ROWS * DROPS, LEVELS)],
        [counts],
        [squares, numbers, cells],
        [pltpu.VMEM((SLOT_ROWS, DPB), f32)] * 2
        + [pltpu.VMEM((SLOT_ROWS, DPB), jnp.int32), pltpu.SemaphoreType.DMA((3,))],
        far=3,
        limit=PACK_LIMIT,
    )
    powers, parcels = local(
        power_kernel,
        [shape(ITERS, EX, EY, LEVELS), shape(SLOT_ROWS, PARCEL, LEVELS)],
        [],
        [
            partial,
            from_north,
            from_south,
            meridional,
            to_west,
            to_east,
            from_east,
            from_west,
            drops,
        ],
    )
    arrived = lax.all_to_all(parcels, "gx", split_axis=0, concat_axis=0, tiled=True)
    shared = jnp.broadcast_to(jnp.sum(arrived[:, 24:], axis=0)[None], (16, 8, LEVELS))
    totals = lax.all_to_all(shared, ("grp", "gy"), split_axis=0, concat_axis=0, tiled=True)
    flat = (CX * CY, LEVELS)
    picked = (NBD * CHUNKS, LEVELS)
    returned, potential, warmth, vapour, mass = local(
        growth_kernel,
        [
            shape(SLOT_ROWS, CHUNKS, LEVELS),
            shape(CX + 2, EY, LEVELS),
            shape(*flat),
            shape(*flat),
            shape(*picked),
        ],
        [owners],
        [
            totals,
            powers,
            arrived,
            theta,
            humidity,
            zonal,
            meridional,
            vertical,
            from_north,
            from_south,
            from_east,
            from_west,
        ],
        [pltpu.VMEM(flat, f32)] + [pltpu.VMEM(picked, f32)] * 2,
    )
    returned = lax.all_to_all(returned, "gx", split_axis=0, concat_axis=0, tiled=True)
    new_theta, new_humidity, new_zonal, new_meridional, new_vertical = local(
        condense_kernel,
        [tile] * 5,
        [owners],
        [
            potential,
            warmth,
            vapour,
            mass,
            arrived,
            theta,
            humidity,
            zonal,
            meridional,
            vertical,
        ],
        [pltpu.VMEM(flat, f32)],
    )
    new_squares = local(
        size_kernel,
        [shape(SLOT_ROWS, DPB)],
        [counts],
        [returned.reshape(SLOT_ROWS * CHUNKS, LEVELS), squares],
    )
    return (
        new_theta,
        new_humidity,
        new_zonal,
        new_meridional,
        new_vertical,
        new_squares[None, None],
    )


def solution(mesh):
    field = P(("grp", "gx"), "gy", None)
    slots = P(("grp", "gx"), "gy", None, None)
    return jax.shard_map(
        on_device,
        mesh=mesh,
        in_specs=(field,) * 7 + (slots,) * 3,
        out_specs=(field,) * 5 + (slots,),
        check_vma=False,
    )
```

```python
import functools

import jax
import jax.numpy as jnp
from jax import lax
from jax.experimental import pallas as pl
from jax.experimental.pallas import tpu as pltpu
from jax.sharding import PartitionSpec as P

TIME_INCREMENT = 0.15
THERMAL_LIFT = 0.5
HUMID_LIFT = 0.3
HELMHOLTZ = 0.001
CLAUSIUS_FACTOR = 0.2
GROWTH = 0.5
GROWTH_SLOPE = 0.1
SUB_STEP = 0.25
CURVATURE = 0.05
FLOOR_SQUARE = 0.04
CONDENSE = 0.2
PHASE_WARMING = 2.5

NSUB = 4
ITERS = 4
NBD = 8
CX = 24
CY = 16
LEVELS = 128
KLO = 48
BAND = 32
EX = 32
EY = 24
SLOT_ROWS = 16
DPB = 1024
CHUNKS = DPB // LEVELS
PARCEL = 32
SCALE = 1.0 / 6.0
VMEM_LIMIT = 24 * 1024 * 1024
COSTP = 1_000_000
FIRST_LIMIT = 54600 * 1024

f32 = jnp.float32
bf16 = jnp.bfloat16


def iota(shape, axis):
    return lax.broadcasted_iota(jnp.int32, shape, axis)


def vertical_profiles():
    level = iota((1, LEVELS), 1)
    height = level.astype(f32)
    centre = jnp.exp(-(height + 0.5) / LEVELS)
    face = jnp.where(level < LEVELS - 1, jnp.exp(-(height + 1.0) / LEVELS), 0.0)
    face_below = jnp.where(level > 0, jnp.exp(-height / LEVELS), 0.0)
    return level, centre, face, face_below


def turn(values, by, axis):
    return pltpu.roll(values, by % values.shape[axis], axis)


def lifted_row(i, theta, humidity, vertical):
    return vertical[i] + TIME_INCREMENT * (THERMAL_LIFT * theta[i] + HUMID_LIFT * humidity[i])


def right_side_kernel(
    theta_far,
    humidity_far,
    zonal_far,
    meridional_far,
    vertical_far,
    partial,
    to_south,
    to_north,
    edges,
    theta,
    humidity,
    zonal,
    meridional,
    vertical,
    arrivals,
):
    copies = [
        pltpu.make_async_copy(far, near, arrivals.at[n])
        for n, (far, near) in enumerate(
            (
                (theta_far, theta),
                (humidity_far, humidity),
                (zonal_far, zonal),
                (meridional_far, meridional),
                (vertical_far, vertical),
            )
        )
    ]
    for copy in copies:
        copy.start()
    for copy in copies:
        copy.wait()
    level, centre, _, _ = vertical_profiles()
    sub = iota((CY, LEVELS), 0)
    sub8 = iota((8, LEVELS), 0)
    for i in range(CX):
        weighted = centre * lifted_row(i, theta, humidity, vertical)
        rise = jnp.where(level < LEVELS - 1, turn(weighted, -1, 1), 0.0) - jnp.where(
            level > 0, turn(weighted, 1, 1), 0.0
        )
        if i == 0:
            across = zonal[1]
        elif i == CX - 1:
            across = -zonal[CX - 2]
        else:
            across = zonal[i + 1] - zonal[i - 1]
        wind = meridional[i]
        along = jnp.where(sub < CY - 1, turn(wind, -1, 0), 0.0) - jnp.where(
            sub > 0, turn(wind, 1, 0), 0.0
        )
        right = (centre * (across * 0.5 + along * 0.5) + 0.5 * rise) * (-1.0 / TIME_INCREMENT)
        partial[i] = right
        warm = theta[i]
        damp = humidity[i]
        to_south[i] = jnp.where(
            sub8 < 4,
            right[0:8],
            jnp.where(sub8 == 4, wind[0:1], jnp.where(sub8 == 5, warm[0:1], damp[0:1])),
        )
        to_north[i] = jnp.where(
            sub8 >= 4,
            right[8:16],
            jnp.where(sub8 == 0, wind[15:16], jnp.where(sub8 == 1, warm[15:16], damp[15:16])),
        )
    for n, i in enumerate((0, CX - 1)):
        to_south[CX + n] = zonal[i, 0:8]
        to_north[CX + n] = zonal[i, 8:16]
        edges[7 * n + 4] = zonal[i]
        edges[7 * n + 5] = theta[i]
        edges[7 * n + 6] = humidity[i]
    for t in range(4):
        edges[t] = meridional[t]
        edges[7 + t] = meridional[CX - 4 + t]


def joined(north, south):
    return jnp.where(iota((8, LEVELS), 0) < 4, north, south)


def completed_row(i, partial, wind, from_north, from_south, third):
    sub8 = iota((8, LEVELS), 0)
    north = from_north[i]
    south = from_south[i]
    low = partial[i, 0:8] + jnp.where(sub8 == 0, third * south[0:1], 0.0)
    high = partial[i, 8:16] - jnp.where(sub8 == 7, third * north[4:5], 0.0)
    halo = (
        joined(north, south)
        + jnp.where(sub8 == 0, third * wind[15:16], 0.0)
        - jnp.where(sub8 == 7, third * wind[0:1], 0.0)
    )
    return low, high, halo


def side_kernel(partial, from_north, from_south, edges, to_west, to_east):
    _, centre, _, _ = vertical_profiles()
    third = centre * (0.5 / TIME_INCREMENT)
    for n, (target, first) in enumerate(((to_west, 0), (to_east, CX - 4))):
        for t in range(4):
            low, high, halo = completed_row(
                first + t, partial, edges[7 * n + t], from_north, from_south, third
            )
            target[t, 0:8] = low
            target[t, 8:16] = high
            target[t, 16:24] = halo
        target[4, 0:16] = edges[7 * n + 4]
        target[4, 16:24] = joined(from_north[CX + n], from_south[CX + n])
        for t in (5, 6):
            target[t, 0:16] = edges[7 * n + t]
            target[t, 16:24] = jnp.zeros((8, LEVELS), f32)


def pack_kernel(squares, cells, packed):
    for s in range(CHUNKS):
        part = slice(LEVELS * s, LEVELS * (s + 1))
        packed[pl.ds(s, SLOT_ROWS, stride=16), :] = squares[:, part]
        packed[pl.ds(8 + s, SLOT_ROWS, stride=16), :] = cells[:, part].astype(f32)


def pack_live_kernel(counts, numbers, packed):
    row = iota((SLOT_ROWS, LEVELS), 0)
    lane = iota((SLOT_ROWS, LEVELS), 1)
    live = jnp.zeros((SLOT_ROWS, LEVELS), jnp.int32)
    for r in range(SLOT_ROWS):
        live = jnp.where(row == r, counts[r], live)
    for s in range(CHUNKS):
        part = slice(LEVELS * s, LEVELS * (s + 1))
        packed[pl.ds(s, SLOT_ROWS, stride=8), :] = jnp.where(
            lane + LEVELS * s < live, numbers[:, part], 0.0
        )


def power_kernel(
    partial,
    from_north,
    from_south,
    meridional,
    to_west,
    to_east,
    from_east,
    from_west,
    drops,
    live,
    powers,
    parcels,
):
    _, centre, face, face_below = vertical_profiles()
    third = centre * (0.5 / TIME_INCREMENT)
    for i in range(4, CX - 4):
        low, high, halo = completed_row(i, partial, meridional[i], from_north, from_south, third)
        powers[0, i, 0:8] = low
        powers[0, i, 8:16] = high
        powers[0, i, 16:24] = halo
    for t in range(4):
        west = to_west[t]
        east = to_east[t]
        far_east = from_east[t]
        far_west = from_west[t]
        if t == 0:
            west = west + third * from_west[4]
            far_east = far_east + third * to_east[4]
        if t == 3:
            east = east - third * from_east[4]
            far_west = far_west - third * to_west[4]
        powers[0, t] = west
        powers[0, CX - 4 + t] = east
        powers[0, CX + t] = far_east
        powers[0, CX + 4 + t] = far_west
    here = ((4.0 + HELMHOLTZ) * centre + face + face_below) * SCALE
    beside = centre * SCALE
    above = face * SCALE
    below = face_below * SCALE

    def applied(j, i):
        values = powers[j, i]
        lateral = (
            powers[j, (i + 1) % EX]
            + powers[j, (i - 1) % EX]
            + turn(values, -1, 0)
            + turn(values, 1, 0)
        )
        return (
            here * values
            - beside * lateral
            - above * turn(values, -1, 1)
            - below * turn(values, 1, 1)
        )

    for j in range(ITERS - 1):
        reach = ITERS - 1 - j
        for i in range(-reach, CX + reach):
            powers[j + 1, i % EX] = applied(j, i % EX)
    sums = [jnp.zeros((8, LEVELS), f32) for _ in range(2 * ITERS)]
    for i in range(CX):
        rows = [powers[j, i, 0:16] for j in range(ITERS)]
        rows.append(applied(ITERS - 1, i)[0:16])
        for k in range(2 * ITERS):
            product = rows[k // 2] * rows[(k + 1) // 2]
            sums[k] = sums[k] + (product[0:8] + product[8:16])
    sub8 = iota((8, LEVELS), 0)
    packed = jnp.zeros((8, LEVELS), f32)
    for k in range(2 * ITERS):
        packed = jnp.where(sub8 == k, jnp.sum(sums[k], axis=0, keepdims=True), packed)
    for r in range(SLOT_ROWS):
        parcels[r, 0:8] = drops[16 * r : 16 * r + 8]
        parcels[r, 8:16] = live[8 * r : 8 * r + 8]
        parcels[r, 16:24] = drops[16 * r + 8 : 16 * r + 16]
        parcels[r, 24:PARCEL] = packed


def two_sum(a, b):
    s = a + b
    t = s - a
    return s, (a - (s - t)) + (b - t)


def quick_sum(a, b):
    s = a + b
    return s, b - (s - a)


def split(a):
    t = a * 4097.0
    high = t - (t - a)
    return high, a - high


def two_product(a, b):
    p = a * b
    ah, al = split(a)
    bh, bl = split(b)
    return p, ((ah * bh - p) + ah * bl + al * bh) + al * bl


def pair_add(a, b):
    s, e = two_sum(a[0], b[0])
    return quick_sum(s, e + (a[1] + b[1]))


def pair_mul(a, b):
    p, e = two_product(a[0], b[0])
    return quick_sum(p, e + (a[0] * b[1] + a[1] * b[0]))


def pair_sub_mul(a, b, c):
    p = pair_mul(b, c)
    return pair_add(a, (-p[0], -p[1]))


def pair_inverse(a):
    guess = 1.0 / a[0]
    p = pair_mul(a, (guess, jnp.zeros_like(guess)))
    rest = (1.0 - p[0]) - p[1]
    return quick_sum(guess, guess * rest)


def coefficients(totals):
    high = totals[0]
    low = jnp.zeros_like(high)
    for t in range(1, totals.shape[0]):
        high, e = two_sum(high, totals[t])
        low = low + e
    by = LEVELS // 2
    high, low = quick_sum(high, low)
    while by:
        high, low = pair_add((high, low), (turn(high, by, 1), turn(low, by, 1)))
        by //= 2
    moment = []
    for k in range(2 * ITERS):
        moment.append(
            (
                jnp.broadcast_to(high[k : k + 1], (8, LEVELS)),
                jnp.broadcast_to(low[k : k + 1], (8, LEVELS)),
            )
        )
    matrix = [[moment[i + j + 1] for j in range(ITERS)] for i in range(ITERS)]
    side = [moment[i] for i in range(ITERS)]
    inverse = []
    for k in range(ITERS):
        inverse.append(pair_inverse(matrix[k][k]))
        for i in range(k + 1, ITERS):
            factor = pair_mul(matrix[k][i], inverse[k])
            for j in range(i, ITERS):
                matrix[i][j] = pair_sub_mul(matrix[i][j], factor, matrix[k][j])
            side[i] = pair_sub_mul(side[i], factor, side[k])
    result = [None] * ITERS
    for k in reversed(range(ITERS)):
        rest = side[k]
        for j in range(k + 1, ITERS):
            rest = pair_sub_mul(rest, matrix[k][j], result[j])
        result[k] = pair_mul(rest, inverse[k])
    return [(r[0] + r[1])[0:1] * SCALE for r in result]


def halves(values):
    high = values.astype(bf16).astype(f32)
    return high, values - high


HALF = TIME_INCREMENT * 0.5


def new_winds(i, potential, theta, humidity, zonal, meridional, vertical):
    level = iota((1, LEVELS), 1)
    here = potential[i + 1]
    mid = here[0:16]
    east = zonal[i] - HALF * (potential[i + 2, 0:16] - potential[i, 0:16])
    north = meridional[i] - HALF * (turn(here, -1, 0)[0:16] - turn(here, 1, 0)[0:16])
    up = lifted_row(i, theta, humidity, vertical) - HALF * (
        jnp.where(level < LEVELS - 1, turn(mid, -1, 1), 0.0)
        - jnp.where(level > 0, turn(mid, 1, 1), 0.0)
    )
    return east, north, up


def chunk(values, t):
    return jnp.concatenate([values[2 * t : 2 * t + 1], values[2 * t + 1 : 2 * t + 2]], axis=1)


def where_at(arrived, owner):
    cell = arrived[owner, 16:24].astype(jnp.int32)
    column = lax.shift_right_logical(cell, 7)
    return (
        jnp.bitwise_and(cell, LEVELS - 1) - KLO,
        jnp.bitwise_and(column, 1) * CX + lax.shift_right_logical(column, 1),
    )


def growth_kernel(
    owners,
    totals,
    powers,
    arrived,
    theta,
    humidity,
    zonal,
    meridional,
    vertical,
    from_north,
    from_south,
    from_east,
    from_west,
    returned,
    potential,
    warmth,
    vapour,
    mass,
    excess,
    picked_excess,
    picked_warmth,
):
    level, _, _, _ = vertical_profiles()
    sub = iota((CY, LEVELS), 0)
    weights = coefficients(totals)
    for t in range(CX + 2):
        i = (t - 1) % EX
        total = weights[0] * powers[0, i]
        for j in range(1, ITERS):
            total = total + weights[j] * powers[j, i]
        potential[t] = total
    for i in range(CX):
        east, north, up = new_winds(i, potential, theta, humidity, zonal, meridional, vertical)
        moved = []
        for f, (field, side, in_north, in_south) in enumerate(
            ((theta, 5, 5, 1), (humidity, 6, 6, 2))
        ):
            values = field[i]
            f_e = field[i + 1] if i < CX - 1 else from_east[side, 0:16]
            f_w = field[i - 1] if i > 0 else from_west[side, 0:16]
            f_n = jnp.where(
                sub < CY - 1, turn(values, -1, 0), from_north[i, in_north : in_north + 1]
            )
            f_s = jnp.where(sub > 0, turn(values, 1, 0), from_south[i, in_south : in_south + 1])
            f_t = jnp.where(level < LEVELS - 1, turn(values, -1, 1), values)
            f_b = jnp.where(level > 0, turn(values, 1, 1), values)
            tendency = (
                jnp.maximum(east, 0.0) * (values - f_w)
                + jnp.minimum(east, 0.0) * (f_e - values)
                + jnp.maximum(north, 0.0) * (values - f_s)
                + jnp.minimum(north, 0.0) * (f_n - values)
                + jnp.maximum(up, 0.0) * (values - f_b)
                + jnp.minimum(up, 0.0) * (f_t - values)
            )
            moved.append(values - TIME_INCREMENT * tendency)
        rows = slice(CY * i, CY * (i + 1))
        warmth[rows] = moved[0]
        vapour[rows] = moved[1]
        excess[rows] = moved[1] * jnp.exp(-CLAUSIUS_FACTOR * moved[0]) - 1.0

    lane = iota((2 * CX, LEVELS), 1)
    height = iota((BAND, 2 * LEVELS), 0)
    place = iota((2 * CX, 2 * LEVELS), 0)

    def band(field, b):
        values = jnp.concatenate(
            [
                field[pl.ds(2 * b, CX, stride=CY), :],
                field[pl.ds(2 * b + 1, CX, stride=CY), :],
            ],
            axis=0,
        )
        high, low = halves(values)
        both = jnp.where(lane < BAND, turn(high, -KLO, 1), turn(low, BAND - KLO, 1))
        return both[:, : 2 * BAND].astype(bf16)

    for b in range(NBD):
        table = jnp.concatenate([band(excess, b), band(warmth, b)], axis=0)
        heights, places = where_at(arrived, owners[b])
        for t in range(CHUNKS // 2):
            hot = jnp.where(height == chunk(heights, t), 1.0, 0.0).astype(bf16)
            found = jnp.dot(
                table, jnp.concatenate([hot, hot], axis=0), preferred_element_type=f32
            )
            mine = place == chunk(places, t)
            for target, part in ((picked_excess, found[: 2 * CX]), (picked_warmth, found[2 * CX :])):
                value = jnp.sum(jnp.where(mine, part, 0.0), axis=0, keepdims=True)
                row = CHUNKS * b + 2 * t
                target[row : row + 1] = value[:, :LEVELS]
                target[row + 1 : row + 2] = value[:, LEVELS:]
    returned[...] = jnp.zeros(returned.shape, f32)
    for b in range(NBD):
        rows = slice(CHUNKS * b, CHUNKS * (b + 1))
        owner = owners[b]
        old = arrived[owner, 0:8]
        number = arrived[owner, 8:16]
        oversaturation = picked_excess[rows]
        rate = GROWTH * jnp.exp(GROWTH_SLOPE * picked_warmth[rows])
        now = old
        for substep in range(NSUB):
            now = jnp.maximum(
                now + 2.0 * SUB_STEP * rate * (oversaturation - CURVATURE / jnp.sqrt(now)),
                FLOOR_SQUARE,
            )
        mass[rows] = jnp.where(
            number > 0.0, number * (now * jnp.sqrt(now) - old * jnp.sqrt(old)), 0.0
        )
        returned[owner] = now


def condense_kernel(
    owners,
    potential,
    warmth,
    vapour,
    mass,
    arrived,
    theta,
    humidity,
    zonal,
    meridional,
    vertical,
    new_theta,
    new_humidity,
    new_zonal,
    new_meridional,
    new_vertical,
    condensed,
):
    for i in range(CX):
        new_zonal[i], new_meridional[i], new_vertical[i] = new_winds(
            i, potential, theta, humidity, zonal, meridional, vertical
        )
    height = iota((BAND, 2 * LEVELS), 0)
    place = iota((2 * CX, 2 * LEVELS), 0)
    for b in range(NBD):
        heights, places = where_at(arrived, owners[b])
        gained = mass[CHUNKS * b : CHUNKS * (b + 1)]
        total = jnp.zeros((4 * CX, BAND), f32)
        for t in range(CHUNKS // 2):
            hot = jnp.where(height == chunk(heights, t), 1.0, 0.0).astype(bf16)
            mine = place == chunk(places, t)
            high, low = halves(chunk(gained, t))
            spread = jnp.concatenate(
                [
                    jnp.where(mine, high, 0.0).astype(bf16),
                    jnp.where(mine, low, 0.0).astype(bf16),
                ],
                axis=0,
            )
            total = total + lax.dot_general(
                spread, hot, (((1,), (1,)), ((), ())), preferred_element_type=f32
            )
        liquid = CONDENSE * (total[: 2 * CX] + total[2 * CX :])
        liquid = jnp.concatenate([liquid, jnp.zeros((2 * CX, LEVELS - BAND), f32)], axis=1)
        liquid = turn(liquid, KLO, 1)
        condensed[pl.ds(2 * b, CX, stride=CY), :] = liquid[:CX]
        condensed[pl.ds(2 * b + 1, CX, stride=CY), :] = liquid[CX:]
    for i in range(CX):
        rows = slice(CY * i, CY * (i + 1))
        new_theta[i] = warmth[rows] + PHASE_WARMING * condensed[rows]
        new_humidity[i] = vapour[rows] - condensed[rows]


def size_kernel(counts, returned, squares, new_squares):
    row = iota((SLOT_ROWS, LEVELS), 0)
    lane = iota((SLOT_ROWS, LEVELS), 1)
    live = jnp.zeros((SLOT_ROWS, LEVELS), jnp.int32)
    for r in range(SLOT_ROWS):
        live = jnp.where(row == r, counts[r], live)
    for s in range(CHUNKS):
        part = slice(LEVELS * s, LEVELS * (s + 1))
        new_squares[:, part] = jnp.where(
            lane + LEVELS * s < live,
            returned[pl.ds(s, SLOT_ROWS, stride=CHUNKS), :],
            squares[:, part],
        )


def local(kernel, outs, scalars, operands, scratch=(), far=0, limit=VMEM_LIMIT, cost=1_000_000):
    whole = pl.BlockSpec(memory_space=pltpu.VMEM)
    single = len(outs) == 1
    return pl.pallas_call(
        kernel,
        out_shape=outs[0] if single else outs,
        in_specs=[pl.BlockSpec(memory_space=pltpu.SMEM)] * len(scalars)
        + [pl.BlockSpec(memory_space=pltpu.HBM)] * far
        + [whole] * (len(operands) - far),
        out_specs=whole if single else [whole] * len(outs),
        scratch_shapes=list(scratch),
        compiler_params=pltpu.CompilerParams(vmem_limit_bytes=limit),
        cost_estimate=pl.CostEstimate(flops=cost, bytes_accessed=cost, transcendentals=0),
    )(*scalars, *operands)


def shape(*dims):
    return jax.ShapeDtypeStruct(dims, f32)


def ring(axes, step):
    count = lax.axis_size(axes)
    return [(i, (i + step) % count) for i in range(count)]


def on_device(
    theta, humidity, zonal, meridional, vertical, owner_map, population, squares, numbers, cells
):
    owners = owner_map.reshape(NBD)
    counts = population.reshape(SLOT_ROWS)
    squares = squares.reshape(SLOT_ROWS, DPB)
    numbers = numbers.reshape(SLOT_ROWS, DPB)
    cells = cells.reshape(SLOT_ROWS, DPB)
    tiles = ("grp", "gx")
    tile = shape(CX, CY, LEVELS)
    partial, to_south, to_north, edges = local(
        right_side_kernel,
        [tile, shape(CX + 2, 8, LEVELS), shape(CX + 2, 8, LEVELS), shape(14, CY, LEVELS)],
        [],
        [theta, humidity, zonal, meridional, vertical],
        [pltpu.VMEM((CX, CY, LEVELS), f32)] * 5 + [pltpu.SemaphoreType.DMA((5,))],
        far=5,
        limit=FIRST_LIMIT,
    )
    from_north = lax.ppermute(to_south, "gy", ring("gy", -1))
    from_south = lax.ppermute(to_north, "gy", ring("gy", 1))
    edges, early_squares, early_cells = lax.optimization_barrier((edges, squares, cells))
    drops = local(
        pack_kernel, [shape(SLOT_ROWS * 16, LEVELS)], [], [early_squares, early_cells], cost=COSTP
    )
    edges, drops = lax.optimization_barrier((edges, drops))
    to_west, to_east = local(
        side_kernel,
        [shape(7, EY, LEVELS), shape(7, EY, LEVELS)],
        [],
        [partial, from_north, from_south, edges],
    )
    to_west, to_east, late_numbers = lax.optimization_barrier((to_west, to_east, numbers))
    live = local(pack_live_kernel, [shape(SLOT_ROWS * 8, LEVELS)], [counts], [late_numbers], cost=COSTP)
    from_east = lax.ppermute(to_west, tiles, ring(tiles, -1))
    from_west = lax.ppermute(to_east, tiles, ring(tiles, 1))
    powers, parcels = local(
        power_kernel,
        [shape(ITERS, EX, EY, LEVELS), shape(SLOT_ROWS, PARCEL, LEVELS)],
        [],
        [
            partial,
            from_north,
            from_south,
            meridional,
            to_west,
            to_east,
            from_east,
            from_west,
            drops,
            live,
        ],
    )
    arrived = lax.all_to_all(parcels, "gx", split_axis=0, concat_axis=0, tiled=True)
    shared = jnp.broadcast_to(jnp.sum(arrived[:, 24:], axis=0)[None], (16, 8, LEVELS))
    totals = lax.all_to_all(shared, ("grp", "gy"), split_axis=0, concat_axis=0, tiled=True)
    flat = (CX * CY, LEVELS)
    picked = (NBD * CHUNKS, LEVELS)
    returned, potential, warmth, vapour, mass = local(
        growth_kernel,
        [
            shape(SLOT_ROWS, CHUNKS, LEVELS),
            shape(CX + 2, EY, LEVELS),
            shape(*flat),
            shape(*flat),
            shape(*picked),
        ],
        [owners],
        [
            totals,
            powers,
            arrived,
            theta,
            humidity,
            zonal,
            meridional,
            vertical,
            from_north,
            from_south,
            from_east,
            from_west,
        ],
        [pltpu.VMEM(flat, f32)] + [pltpu.VMEM(picked, f32)] * 2,
    )
    returned = lax.all_to_all(returned, "gx", split_axis=0, concat_axis=0, tiled=True)
    new_theta, new_humidity, new_zonal, new_meridional, new_vertical = local(
        condense_kernel,
        [tile] * 5,
        [owners],
        [
            potential,
            warmth,
            vapour,
            mass,
            arrived,
            theta,
            humidity,
            zonal,
            meridional,
            vertical,
        ],
        [pltpu.VMEM(flat, f32)],
    )
    new_squares = local(
        size_kernel,
        [shape(SLOT_ROWS, DPB)],
        [counts],
        [returned.reshape(SLOT_ROWS * CHUNKS, LEVELS), squares],
    )
    return (
        new_theta,
        new_humidity,
        new_zonal,
        new_meridional,
        new_vertical,
        new_squares[None, None],
    )


def solution(mesh):
    field = P(("grp", "gx"), "gy", None)
    slots = P(("grp", "gx"), "gy", None, None)
    return jax.shard_map(
        on_device,
        mesh=mesh,
        in_specs=(field,) * 7 + (slots,) * 3,
        out_specs=(field,) * 5 + (slots,),
        check_vma=False,
    )
```

```python
import functools

import jax
import jax.numpy as jnp
from jax import lax
from jax.experimental import pallas as pl
from jax.experimental.pallas import tpu as pltpu
from jax.sharding import PartitionSpec as P

TIME_INCREMENT = 0.15
THERMAL_LIFT = 0.5
HUMID_LIFT = 0.3
HELMHOLTZ = 0.001
CLAUSIUS_FACTOR = 0.2
GROWTH = 0.5
GROWTH_SLOPE = 0.1
SUB_STEP = 0.25
CURVATURE = 0.05
FLOOR_SQUARE = 0.04
CONDENSE = 0.2
PHASE_WARMING = 2.5

NSUB = 4
ITERS = 4
NBD = 8
CX = 24
CY = 16
LEVELS = 128
KLO = 48
BAND = 32
EX = 32
EY = 24
SLOT_ROWS = 16
DPB = 1024
CHUNKS = DPB // LEVELS
PARCEL = 32
SCALE = 1.0 / 6.0
VMEM_LIMIT = 24 * 1024 * 1024
COSTP = 1_000_000
FIRST_LIMIT = 54600 * 1024

f32 = jnp.float32
bf16 = jnp.bfloat16


def iota(shape, axis):
    return lax.broadcasted_iota(jnp.int32, shape, axis)


def vertical_profiles():
    level = iota((1, LEVELS), 1)
    height = level.astype(f32)
    centre = jnp.exp(-(height + 0.5) / LEVELS)
    face = jnp.where(level < LEVELS - 1, jnp.exp(-(height + 1.0) / LEVELS), 0.0)
    face_below = jnp.where(level > 0, jnp.exp(-height / LEVELS), 0.0)
    return level, centre, face, face_below


def turn(values, by, axis):
    return pltpu.roll(values, by % values.shape[axis], axis)


def lifted_row(i, theta, humidity, vertical):
    return vertical[i] + TIME_INCREMENT * (THERMAL_LIFT * theta[i] + HUMID_LIFT * humidity[i])


def right_side_kernel(
    theta_far,
    humidity_far,
    zonal_far,
    meridional_far,
    vertical_far,
    partial,
    to_south,
    to_north,
    edges,
    theta,
    humidity,
    zonal,
    meridional,
    vertical,
    arrivals,
):
    copies = [
        pltpu.make_async_copy(far, near, arrivals.at[n])
        for n, (far, near) in enumerate(
            (
                (theta_far, theta),
                (humidity_far, humidity),
                (zonal_far, zonal),
                (meridional_far, meridional),
                (vertical_far, vertical),
            )
        )
    ]
    for copy in copies:
        copy.start()
    for copy in copies:
        copy.wait()
    level, centre, _, _ = vertical_profiles()
    sub = iota((CY, LEVELS), 0)
    sub8 = iota((8, LEVELS), 0)
    for i in range(CX):
        weighted = centre * lifted_row(i, theta, humidity, vertical)
        rise = jnp.where(level < LEVELS - 1, turn(weighted, -1, 1), 0.0) - jnp.where(
            level > 0, turn(weighted, 1, 1), 0.0
        )
        if i == 0:
            across = zonal[1]
        elif i == CX - 1:
            across = -zonal[CX - 2]
        else:
            across = zonal[i + 1] - zonal[i - 1]
        wind = meridional[i]
        along = jnp.where(sub < CY - 1, turn(wind, -1, 0), 0.0) - jnp.where(
            sub > 0, turn(wind, 1, 0), 0.0
        )
        right = (centre * (across * 0.5 + along * 0.5) + 0.5 * rise) * (-1.0 / TIME_INCREMENT)
        partial[i] = right
        warm = theta[i]
        damp = humidity[i]
        to_south[i] = jnp.where(
            sub8 < 4,
            right[0:8],
            jnp.where(sub8 == 4, wind[0:1], jnp.where(sub8 == 5, warm[0:1], damp[0:1])),
        )
        to_north[i] = jnp.where(
            sub8 >= 4,
            right[8:16],
            jnp.where(sub8 == 0, wind[15:16], jnp.where(sub8 == 1, warm[15:16], damp[15:16])),
        )
    for n, i in enumerate((0, CX - 1)):
        to_south[CX + n] = zonal[i, 0:8]
        to_north[CX + n] = zonal[i, 8:16]
        edges[7 * n + 4] = zonal[i]
        edges[7 * n + 5] = theta[i]
        edges[7 * n + 6] = humidity[i]
    for t in range(4):
        edges[t] = meridional[t]
        edges[7 + t] = meridional[CX - 4 + t]


def joined(north, south):
    return jnp.where(iota((8, LEVELS), 0) < 4, north, south)


def completed_row(i, partial, wind, from_north, from_south, third):
    sub8 = iota((8, LEVELS), 0)
    north = from_north[i]
    south = from_south[i]
    low = partial[i, 0:8] + jnp.where(sub8 == 0, third * south[0:1], 0.0)
    high = partial[i, 8:16] - jnp.where(sub8 == 7, third * north[4:5], 0.0)
    halo = (
        joined(north, south)
        + jnp.where(sub8 == 0, third * wind[15:16], 0.0)
        - jnp.where(sub8 == 7, third * wind[0:1], 0.0)
    )
    return low, high, halo


def side_kernel(partial, from_north, from_south, edges, to_west, to_east):
    _, centre, _, _ = vertical_profiles()
    third = centre * (0.5 / TIME_INCREMENT)
    for n, (target, first) in enumerate(((to_west, 0), (to_east, CX - 4))):
        for t in range(4):
            low, high, halo = completed_row(
                first + t, partial, edges[7 * n + t], from_north, from_south, third
            )
            target[t, 0:8] = low
            target[t, 8:16] = high
            target[t, 16:24] = halo
        target[4, 0:16] = edges[7 * n + 4]
        target[4, 16:24] = joined(from_north[CX + n], from_south[CX + n])
        for t in (5, 6):
            target[t, 0:16] = edges[7 * n + t]
            target[t, 16:24] = jnp.zeros((8, LEVELS), f32)


def pack_kernel(squares, cells, packed):
    for s in range(CHUNKS):
        part = slice(LEVELS * s, LEVELS * (s + 1))
        packed[pl.ds(s, SLOT_ROWS, stride=16), :] = squares[:, part]
        packed[pl.ds(8 + s, SLOT_ROWS, stride=16), :] = cells[:, part].astype(f32)


def pack_live_kernel(counts, numbers, packed):
    row = iota((SLOT_ROWS, LEVELS), 0)
    lane = iota((SLOT_ROWS, LEVELS), 1)
    live = jnp.zeros((SLOT_ROWS, LEVELS), jnp.int32)
    for r in range(SLOT_ROWS):
        live = jnp.where(row == r, counts[r], live)
    for s in range(CHUNKS):
        part = slice(LEVELS * s, LEVELS * (s + 1))
        packed[pl.ds(s, SLOT_ROWS, stride=8), :] = jnp.where(
            lane + LEVELS * s < live, numbers[:, part], 0.0
        )


def power_kernel(
    partial,
    from_north,
    from_south,
    meridional,
    to_west,
    to_east,
    from_east,
    from_west,
    drops,
    live,
    powers,
    parcels,
):
    _, centre, face, face_below = vertical_profiles()
    third = centre * (0.5 / TIME_INCREMENT)
    for i in range(4, CX - 4):
        low, high, halo = completed_row(i, partial, meridional[i], from_north, from_south, third)
        powers[0, i, 0:8] = low
        powers[0, i, 8:16] = high
        powers[0, i, 16:24] = halo
    for t in range(4):
        west = to_west[t]
        east = to_east[t]
        far_east = from_east[t]
        far_west = from_west[t]
        if t == 0:
            west = west + third * from_west[4]
            far_east = far_east + third * to_east[4]
        if t == 3:
            east = east - third * from_east[4]
            far_west = far_west - third * to_west[4]
        powers[0, t] = west
        powers[0, CX - 4 + t] = east
        powers[0, CX + t] = far_east
        powers[0, CX + 4 + t] = far_west
    here = ((4.0 + HELMHOLTZ) * centre + face + face_below) * SCALE
    beside = centre * SCALE
    above = face * SCALE
    below = face_below * SCALE

    def applied(j, i):
        values = powers[j, i]
        lateral = (
            powers[j, (i + 1) % EX]
            + powers[j, (i - 1) % EX]
            + turn(values, -1, 0)
            + turn(values, 1, 0)
        )
        return (
            here * values
            - beside * lateral
            - above * turn(values, -1, 1)
            - below * turn(values, 1, 1)
        )

    for j in range(ITERS - 1):
        reach = ITERS - 1 - j
        for i in range(-reach, CX + reach):
            powers[j + 1, i % EX] = applied(j, i % EX)
    sums = [jnp.zeros((8, LEVELS), f32) for _ in range(2 * ITERS)]
    for i in range(CX):
        rows = [powers[j, i, 0:16] for j in range(ITERS)]
        rows.append(applied(ITERS - 1, i)[0:16])
        for k in range(2 * ITERS):
            product = rows[k // 2] * rows[(k + 1) // 2]
            sums[k] = sums[k] + (product[0:8] + product[8:16])
    sub8 = iota((8, LEVELS), 0)
    packed = jnp.zeros((8, LEVELS), f32)
    for k in range(2 * ITERS):
        packed = jnp.where(sub8 == k, jnp.sum(sums[k], axis=0, keepdims=True), packed)
    for r in range(SLOT_ROWS):
        parcels[r, 0:8] = drops[16 * r : 16 * r + 8]
        parcels[r, 8:16] = live[8 * r : 8 * r + 8]
        parcels[r, 16:24] = drops[16 * r + 8 : 16 * r + 16]
        parcels[r, 24:PARCEL] = packed


def two_sum(a, b):
    s = a + b
    t = s - a
    return s, (a - (s - t)) + (b - t)


def quick_sum(a, b):
    s = a + b
    return s, b - (s - a)


def split(a):
    t = a * 4097.0
    high = t - (t - a)
    return high, a - high


def two_product(a, b):
    p = a * b
    ah, al = split(a)
    bh, bl = split(b)
    return p, ((ah * bh - p) + ah * bl + al * bh) + al * bl


def pair_add(a, b):
    s, e = two_sum(a[0], b[0])
    return quick_sum(s, e + (a[1] + b[1]))


def pair_mul(a, b):
    p, e = two_product(a[0], b[0])
    return quick_sum(p, e + (a[0] * b[1] + a[1] * b[0]))


def pair_sub_mul(a, b, c):
    p = pair_mul(b, c)
    return pair_add(a, (-p[0], -p[1]))


def pair_inverse(a):
    guess = 1.0 / a[0]
    p = pair_mul(a, (guess, jnp.zeros_like(guess)))
    rest = (1.0 - p[0]) - p[1]
    return quick_sum(guess, guess * rest)


def coefficients(totals):
    high = totals[0]
    low = jnp.zeros_like(high)
    for t in range(1, totals.shape[0]):
        high, e = two_sum(high, totals[t])
        low = low + e
    bound = 256.0 * jnp.max(jnp.abs(high), axis=1, keepdims=True)
    coarse = (bound + high) - bound
    fine = (high - coarse) + low
    high, low = quick_sum(
        jnp.sum(coarse, axis=1, keepdims=True), jnp.sum(fine, axis=1, keepdims=True)
    )
    moment = []
    for k in range(2 * ITERS):
        moment.append(
            (
                jnp.broadcast_to(high[k : k + 1], (8, LEVELS)),
                jnp.broadcast_to(low[k : k + 1], (8, LEVELS)),
            )
        )
    matrix = [[moment[i + j + 1] for j in range(ITERS)] for i in range(ITERS)]
    side = [moment[i] for i in range(ITERS)]
    inverse = []
    for k in range(ITERS):
        inverse.append(pair_inverse(matrix[k][k]))
        for i in range(k + 1, ITERS):
            factor = pair_mul(matrix[k][i], inverse[k])
            for j in range(i, ITERS):
                matrix[i][j] = pair_sub_mul(matrix[i][j], factor, matrix[k][j])
            side[i] = pair_sub_mul(side[i], factor, side[k])
    result = [None] * ITERS
    for k in reversed(range(ITERS)):
        rest = side[k]
        for j in range(k + 1, ITERS):
            rest = pair_sub_mul(rest, matrix[k][j], result[j])
        result[k] = pair_mul(rest, inverse[k])
    return [(r[0] + r[1])[0:1] * SCALE for r in result]


def halves(values):
    high = values.astype(bf16).astype(f32)
    return high, values - high


HALF = TIME_INCREMENT * 0.5


def new_winds(i, potential, theta, humidity, zonal, meridional, vertical):
    level = iota((1, LEVELS), 1)
    here = potential[i + 1]
    mid = here[0:16]
    east = zonal[i] - HALF * (potential[i + 2, 0:16] - potential[i, 0:16])
    north = meridional[i] - HALF * (turn(here, -1, 0)[0:16] - turn(here, 1, 0)[0:16])
    up = lifted_row(i, theta, humidity, vertical) - HALF * (
        jnp.where(level < LEVELS - 1, turn(mid, -1, 1), 0.0)
        - jnp.where(level > 0, turn(mid, 1, 1), 0.0)
    )
    return east, north, up


def chunk(values, t):
    return jnp.concatenate([values[2 * t : 2 * t + 1], values[2 * t + 1 : 2 * t + 2]], axis=1)


def where_at(arrived, owner):
    cell = arrived[owner, 16:24].astype(jnp.int32)
    column = lax.shift_right_logical(cell, 7)
    return (
        jnp.bitwise_and(cell, LEVELS - 1) - KLO,
        jnp.bitwise_and(column, 1) * CX + lax.shift_right_logical(column, 1),
    )


def step_kernel(
    owners,
    totals,
    powers,
    arrived,
    theta,
    humidity,
    zonal,
    meridional,
    vertical,
    from_north,
    from_south,
    from_east,
    from_west,
    new_theta,
    new_humidity,
    new_zonal,
    new_meridional,
    new_vertical,
    returned,
    potential,
    warmth,
    vapour,
    mass,
    excess,
    condensed,
    picked_excess,
    picked_warmth,
    spans,
):
    level, _, _, _ = vertical_profiles()
    sub = iota((CY, LEVELS), 0)
    for i in range(CX):
        for f, (field, side, in_north, in_south) in enumerate(
            ((theta, 5, 5, 1), (humidity, 6, 6, 2))
        ):
            values = field[i]
            f_e = field[i + 1] if i < CX - 1 else from_east[side, 0:16]
            f_w = field[i - 1] if i > 0 else from_west[side, 0:16]
            f_n = jnp.where(
                sub < CY - 1, turn(values, -1, 0), from_north[i, in_north : in_north + 1]
            )
            f_s = jnp.where(sub > 0, turn(values, 1, 0), from_south[i, in_south : in_south + 1])
            f_t = jnp.where(level < LEVELS - 1, turn(values, -1, 1), values)
            f_b = jnp.where(level > 0, turn(values, 1, 1), values)
            for n, span in enumerate(
                (values - f_w, f_e - values, values - f_s, f_n - values, values - f_b, f_t - values)
            ):
                spans[6 * f + n, i] = span
    weights = coefficients(totals)
    for t in range(CX + 2):
        i = (t - 1) % EX
        total = weights[0] * powers[0, i]
        for j in range(1, ITERS):
            total = total + weights[j] * powers[j, i]
        potential[t] = total
    for i in range(CX):
        east, north, up = new_winds(i, potential, theta, humidity, zonal, meridional, vertical)
        new_zonal[i] = east
        new_meridional[i] = north
        new_vertical[i] = up
        moved = []
        for f, field in enumerate((theta, humidity)):
            tendency = (
                east * jnp.where(east > 0.0, spans[6 * f, i], spans[6 * f + 1, i])
                + north * jnp.where(north > 0.0, spans[6 * f + 2, i], spans[6 * f + 3, i])
                + up * jnp.where(up > 0.0, spans[6 * f + 4, i], spans[6 * f + 5, i])
            )
            moved.append(field[i] - TIME_INCREMENT * tendency)
        rows = slice(CY * i, CY * (i + 1))
        warmth[rows] = moved[0]
        vapour[rows] = moved[1]
        excess[rows] = moved[1] * jnp.exp(-CLAUSIUS_FACTOR * moved[0]) - 1.0

    lane = iota((2 * CX, LEVELS), 1)
    height = iota((BAND, 2 * LEVELS), 0)
    place = iota((2 * CX, 2 * LEVELS), 0)

    def band(field, b):
        values = jnp.concatenate(
            [
                field[pl.ds(2 * b, CX, stride=CY), :],
                field[pl.ds(2 * b + 1, CX, stride=CY), :],
            ],
            axis=0,
        )
        high, low = halves(values)
        both = jnp.where(lane < BAND, turn(high, -KLO, 1), turn(low, BAND - KLO, 1))
        return both[:, : 2 * BAND].astype(bf16)

    for b in range(NBD):
        table = jnp.concatenate([band(excess, b), band(warmth, b)], axis=0)
        heights, places = where_at(arrived, owners[b])
        for t in range(CHUNKS // 2):
            hot = jnp.where(height == chunk(heights, t), 1.0, 0.0).astype(bf16)
            found = jnp.dot(
                table, jnp.concatenate([hot, hot], axis=0), preferred_element_type=f32
            )
            mine = place == chunk(places, t)
            for target, part in ((picked_excess, found[: 2 * CX]), (picked_warmth, found[2 * CX :])):
                value = jnp.sum(jnp.where(mine, part, 0.0), axis=0, keepdims=True)
                row = CHUNKS * b + 2 * t
                target[row : row + 1] = value[:, :LEVELS]
                target[row + 1 : row + 2] = value[:, LEVELS:]
    returned[...] = jnp.zeros(returned.shape, f32)
    for b in range(NBD):
        rows = slice(CHUNKS * b, CHUNKS * (b + 1))
        owner = owners[b]
        old = arrived[owner, 0:8]
        number = arrived[owner, 8:16]
        oversaturation = picked_excess[rows]
        rate = GROWTH * jnp.exp(GROWTH_SLOPE * picked_warmth[rows])
        now = old
        for substep in range(NSUB):
            now = jnp.maximum(
                now + 2.0 * SUB_STEP * rate * (oversaturation - CURVATURE / jnp.sqrt(now)),
                FLOOR_SQUARE,
            )
        mass[rows] = jnp.where(
            number > 0.0, number * (now * jnp.sqrt(now) - old * jnp.sqrt(old)), 0.0
        )
        returned[owner] = now
    for b in range(NBD):
        heights, places = where_at(arrived, owners[b])
        gained = mass[CHUNKS * b : CHUNKS * (b + 1)]
        total = jnp.zeros((4 * CX, BAND), f32)
        for t in range(CHUNKS // 2):
            hot = jnp.where(height == chunk(heights, t), 1.0, 0.0).astype(bf16)
            mine = place == chunk(places, t)
            high, low = halves(chunk(gained, t))
            spread = jnp.concatenate(
                [
                    jnp.where(mine, high, 0.0).astype(bf16),
                    jnp.where(mine, low, 0.0).astype(bf16),
                ],
                axis=0,
            )
            total = total + lax.dot_general(
                spread, hot, (((1,), (1,)), ((), ())), preferred_element_type=f32
            )
        liquid = CONDENSE * (total[: 2 * CX] + total[2 * CX :])
        liquid = jnp.concatenate([liquid, jnp.zeros((2 * CX, LEVELS - BAND), f32)], axis=1)
        liquid = turn(liquid, KLO, 1)
        condensed[pl.ds(2 * b, CX, stride=CY), :] = liquid[:CX]
        condensed[pl.ds(2 * b + 1, CX, stride=CY), :] = liquid[CX:]
    for i in range(CX):
        rows = slice(CY * i, CY * (i + 1))
        new_theta[i] = warmth[rows] + PHASE_WARMING * condensed[rows]
        new_humidity[i] = vapour[rows] - condensed[rows]


def size_kernel(counts, returned, squares, new_squares):
    row = iota((SLOT_ROWS, LEVELS), 0)
    lane = iota((SLOT_ROWS, LEVELS), 1)
    live = jnp.zeros((SLOT_ROWS, LEVELS), jnp.int32)
    for r in range(SLOT_ROWS):
        live = jnp.where(row == r, counts[r], live)
    for s in range(CHUNKS):
        part = slice(LEVELS * s, LEVELS * (s + 1))
        new_squares[:, part] = jnp.where(
            lane + LEVELS * s < live,
            returned[pl.ds(s, SLOT_ROWS, stride=CHUNKS), :],
            squares[:, part],
        )


def local(kernel, outs, scalars, operands, scratch=(), far=0, limit=VMEM_LIMIT, cost=1_000_000):
    whole = pl.BlockSpec(memory_space=pltpu.VMEM)
    single = len(outs) == 1
    return pl.pallas_call(
        kernel,
        out_shape=outs[0] if single else outs,
        in_specs=[pl.BlockSpec(memory_space=pltpu.SMEM)] * len(scalars)
        + [pl.BlockSpec(memory_space=pltpu.HBM)] * far
        + [whole] * (len(operands) - far),
        out_specs=whole if single else [whole] * len(outs),
        scratch_shapes=list(scratch),
        compiler_params=pltpu.CompilerParams(vmem_limit_bytes=limit),
        cost_estimate=pl.CostEstimate(flops=cost, bytes_accessed=cost, transcendentals=0),
    )(*scalars, *operands)


def shape(*dims):
    return jax.ShapeDtypeStruct(dims, f32)


def ring(axes, step):
    count = lax.axis_size(axes)
    return [(i, (i + step) % count) for i in range(count)]


def on_device(
    theta, humidity, zonal, meridional, vertical, owner_map, population, squares, numbers, cells
):
    owners = owner_map.reshape(NBD)
    counts = population.reshape(SLOT_ROWS)
    squares = squares.reshape(SLOT_ROWS, DPB)
    numbers = numbers.reshape(SLOT_ROWS, DPB)
    cells = cells.reshape(SLOT_ROWS, DPB)
    tiles = ("grp", "gx")
    tile = shape(CX, CY, LEVELS)
    partial, to_south, to_north, edges = local(
        right_side_kernel,
        [tile, shape(CX + 2, 8, LEVELS), shape(CX + 2, 8, LEVELS), shape(14, CY, LEVELS)],
        [],
        [theta, humidity, zonal, meridional, vertical],
        [pltpu.VMEM((CX, CY, LEVELS), f32)] * 5 + [pltpu.SemaphoreType.DMA((5,))],
        far=5,
        limit=FIRST_LIMIT,
    )
    from_north = lax.ppermute(to_south, "gy", ring("gy", -1))
    from_south = lax.ppermute(to_north, "gy", ring("gy", 1))
    edges, early_squares, early_cells = lax.optimization_barrier((edges, squares, cells))
    drops = local(
        pack_kernel, [shape(SLOT_ROWS * 16, LEVELS)], [], [early_squares, early_cells], cost=COSTP
    )
    edges, drops = lax.optimization_barrier((edges, drops))
    to_west, to_east = local(
        side_kernel,
        [shape(7, EY, LEVELS), shape(7, EY, LEVELS)],
        [],
        [partial, from_north, from_south, edges],
    )
    to_west, to_east, late_numbers = lax.optimization_barrier((to_west, to_east, numbers))
    live = local(pack_live_kernel, [shape(SLOT_ROWS * 8, LEVELS)], [counts], [late_numbers], cost=COSTP)
    from_east = lax.ppermute(to_west, tiles, ring(tiles, -1))
    from_west = lax.ppermute(to_east, tiles, ring(tiles, 1))
    powers, parcels = local(
        power_kernel,
        [shape(ITERS, EX, EY, LEVELS), shape(SLOT_ROWS, PARCEL, LEVELS)],
        [],
        [
            partial,
            from_north,
            from_south,
            meridional,
            to_west,
            to_east,
            from_east,
            from_west,
            drops,
            live,
        ],
    )
    arrived = lax.all_to_all(parcels, "gx", split_axis=0, concat_axis=0, tiled=True)
    shared = jnp.broadcast_to(jnp.sum(arrived[:, 24:], axis=0)[None], (16, 8, LEVELS))
    totals = lax.all_to_all(shared, ("grp", "gy"), split_axis=0, concat_axis=0, tiled=True)
    flat = (CX * CY, LEVELS)
    picked = (NBD * CHUNKS, LEVELS)
    new_theta, new_humidity, new_zonal, new_meridional, new_vertical, returned = local(
        step_kernel,
        [tile] * 5 + [shape(SLOT_ROWS, CHUNKS, LEVELS)],
        [owners],
        [
            totals,
            powers,
            arrived,
            theta,
            humidity,
            zonal,
            meridional,
            vertical,
            from_north,
            from_south,
            from_east,
            from_west,
        ],
        [pltpu.VMEM((CX + 2, EY, LEVELS), f32)]
        + [pltpu.VMEM(flat, f32)] * 2
        + [pltpu.VMEM(picked, f32)]
        + [pltpu.VMEM(flat, f32)] * 2
        + [pltpu.VMEM(picked, f32)] * 2
        + [pltpu.VMEM((12, CX, CY, LEVELS), f32)],
    )
    returned = lax.all_to_all(returned, "gx", split_axis=0, concat_axis=0, tiled=True)
    new_squares = local(
        size_kernel,
        [shape(SLOT_ROWS, DPB)],
        [counts],
        [returned.reshape(SLOT_ROWS * CHUNKS, LEVELS), squares],
    )
    return (
        new_theta,
        new_humidity,
        new_zonal,
        new_meridional,
        new_vertical,
        new_squares[None, None],
    )


def solution(mesh):
    field = P(("grp", "gx"), "gy", None)
    slots = P(("grp", "gx"), "gy", None, None)
    return jax.shard_map(
        on_device,
        mesh=mesh,
        in_specs=(field,) * 7 + (slots,) * 3,
        out_specs=(field,) * 5 + (slots,),
        check_vma=False,
    )
```

```python
import functools

import jax
import jax.numpy as jnp
from jax import lax
from jax.experimental import pallas as pl
from jax.experimental.pallas import tpu as pltpu
from jax.sharding import PartitionSpec as P

TIME_INCREMENT = 0.15
THERMAL_LIFT = 0.5
HUMID_LIFT = 0.3
HELMHOLTZ = 0.001
CLAUSIUS_FACTOR = 0.2
GROWTH = 0.5
GROWTH_SLOPE = 0.1
SUB_STEP = 0.25
CURVATURE = 0.05
FLOOR_SQUARE = 0.04
CONDENSE = 0.2
PHASE_WARMING = 2.5

NSUB = 4
ITERS = 4
NBD = 8
CX = 24
CY = 16
LEVELS = 128
KLO = 48
BAND = 32
EX = 32
EY = 24
SLOT_ROWS = 16
DPB = 1024
CHUNKS = DPB // LEVELS
PARCEL = 32
SCALE = 1.0 / 6.0
VMEM_LIMIT = 24 * 1024 * 1024
COSTP = 1_000_000
FIRST_LIMIT = 54600 * 1024

f32 = jnp.float32
bf16 = jnp.bfloat16


def iota(shape, axis):
    return lax.broadcasted_iota(jnp.int32, shape, axis)


def vertical_profiles():
    level = iota((1, LEVELS), 1)
    height = level.astype(f32)
    centre = jnp.exp(-(height + 0.5) / LEVELS)
    face = jnp.where(level < LEVELS - 1, jnp.exp(-(height + 1.0) / LEVELS), 0.0)
    face_below = jnp.where(level > 0, jnp.exp(-height / LEVELS), 0.0)
    return level, centre, face, face_below


def turn(values, by, axis):
    return pltpu.roll(values, by % values.shape[axis], axis)


def lifted_row(i, theta, humidity, vertical):
    return vertical[i] + TIME_INCREMENT * (THERMAL_LIFT * theta[i] + HUMID_LIFT * humidity[i])


def right_side_kernel(
    theta_far,
    humidity_far,
    zonal_far,
    meridional_far,
    vertical_far,
    partial,
    to_south,
    to_north,
    edges,
    theta,
    humidity,
    zonal,
    meridional,
    vertical,
    arrivals,
):
    copies = [
        pltpu.make_async_copy(far, near, arrivals.at[n])
        for n, (far, near) in enumerate(
            (
                (theta_far, theta),
                (humidity_far, humidity),
                (zonal_far, zonal),
                (meridional_far, meridional),
                (vertical_far, vertical),
            )
        )
    ]
    for copy in copies:
        copy.start()
    for copy in copies:
        copy.wait()
    level, centre, _, _ = vertical_profiles()
    sub = iota((CY, LEVELS), 0)
    sub8 = iota((8, LEVELS), 0)
    for i in range(CX):
        weighted = centre * lifted_row(i, theta, humidity, vertical)
        rise = jnp.where(level < LEVELS - 1, turn(weighted, -1, 1), 0.0) - jnp.where(
            level > 0, turn(weighted, 1, 1), 0.0
        )
        if i == 0:
            across = zonal[1]
        elif i == CX - 1:
            across = -zonal[CX - 2]
        else:
            across = zonal[i + 1] - zonal[i - 1]
        wind = meridional[i]
        along = jnp.where(sub < CY - 1, turn(wind, -1, 0), 0.0) - jnp.where(
            sub > 0, turn(wind, 1, 0), 0.0
        )
        right = (centre * (across * 0.5 + along * 0.5) + 0.5 * rise) * (-1.0 / TIME_INCREMENT)
        partial[i] = right
        warm = theta[i]
        damp = humidity[i]
        to_south[i] = jnp.where(
            sub8 < 4,
            right[0:8],
            jnp.where(sub8 == 4, wind[0:1], jnp.where(sub8 == 5, warm[0:1], damp[0:1])),
        )
        to_north[i] = jnp.where(
            sub8 >= 4,
            right[8:16],
            jnp.where(sub8 == 0, wind[15:16], jnp.where(sub8 == 1, warm[15:16], damp[15:16])),
        )
    for n, i in enumerate((0, CX - 1)):
        to_south[CX + n] = zonal[i, 0:8]
        to_north[CX + n] = zonal[i, 8:16]
        edges[7 * n + 4] = zonal[i]
        edges[7 * n + 5] = theta[i]
        edges[7 * n + 6] = humidity[i]
    for t in range(4):
        edges[t] = meridional[t]
        edges[7 + t] = meridional[CX - 4 + t]


def joined(north, south):
    return jnp.where(iota((8, LEVELS), 0) < 4, north, south)


def completed_row(i, partial, wind, from_north, from_south, third):
    sub8 = iota((8, LEVELS), 0)
    north = from_north[i]
    south = from_south[i]
    low = partial[i, 0:8] + jnp.where(sub8 == 0, third * south[0:1], 0.0)
    high = partial[i, 8:16] - jnp.where(sub8 == 7, third * north[4:5], 0.0)
    halo = (
        joined(north, south)
        + jnp.where(sub8 == 0, third * wind[15:16], 0.0)
        - jnp.where(sub8 == 7, third * wind[0:1], 0.0)
    )
    return low, high, halo


def side_kernel(partial, from_north, from_south, edges, to_west, to_east):
    _, centre, _, _ = vertical_profiles()
    third = centre * (0.5 / TIME_INCREMENT)
    for n, (target, first) in enumerate(((to_west, 0), (to_east, CX - 4))):
        for t in range(4):
            low, high, halo = completed_row(
                first + t, partial, edges[7 * n + t], from_north, from_south, third
            )
            target[t, 0:8] = low
            target[t, 8:16] = high
            target[t, 16:24] = halo
        target[4, 0:16] = edges[7 * n + 4]
        target[4, 16:24] = joined(from_north[CX + n], from_south[CX + n])
        for t in (5, 6):
            target[t, 0:16] = edges[7 * n + t]
            target[t, 16:24] = jnp.zeros((8, LEVELS), f32)


def pack_kernel(squares, cells, packed):
    for s in range(CHUNKS):
        part = slice(LEVELS * s, LEVELS * (s + 1))
        packed[pl.ds(s, SLOT_ROWS, stride=16), :] = squares[:, part]
        packed[pl.ds(8 + s, SLOT_ROWS, stride=16), :] = cells[:, part].astype(f32)


def pack_live_kernel(counts, numbers, packed):
    row = iota((SLOT_ROWS, LEVELS), 0)
    lane = iota((SLOT_ROWS, LEVELS), 1)
    live = jnp.zeros((SLOT_ROWS, LEVELS), jnp.int32)
    for r in range(SLOT_ROWS):
        live = jnp.where(row == r, counts[r], live)
    for s in range(CHUNKS):
        part = slice(LEVELS * s, LEVELS * (s + 1))
        packed[pl.ds(s, SLOT_ROWS, stride=8), :] = jnp.where(
            lane + LEVELS * s < live, numbers[:, part], 0.0
        )


def power_row(inner, outer, j, i):
    return inner[j, i] if j < i < CX - 1 - j else outer[j, i]


def applied(inner, outer, j, i):
    _, centre, face, face_below = vertical_profiles()
    here = ((4.0 + HELMHOLTZ) * centre + face + face_below) * SCALE
    values = power_row(inner, outer, j, i)
    lateral = (
        power_row(inner, outer, j, (i + 1) % EX)
        + power_row(inner, outer, j, (i - 1) % EX)
        + turn(values, -1, 0)
        + turn(values, 1, 0)
    )
    return (
        here * values
        - (centre * SCALE) * lateral
        - (face * SCALE) * turn(values, -1, 1)
        - (face_below * SCALE) * turn(values, 1, 1)
    )


def add_products(sums, inner, outer, rows):
    sums = list(sums)
    for i in rows:
        terms = [power_row(inner, outer, j, i)[0:16] for j in range(ITERS)]
        terms.append(applied(inner, outer, ITERS - 1, i)[0:16])
        for k in range(2 * ITERS):
            product = terms[k // 2] * terms[(k + 1) // 2]
            sums[k] = sums[k] + (product[0:8] + product[8:16])
    return sums


INNER_ROWS = range(ITERS + 1, CX - ITERS - 1)


def inner_kernel(
    partial, from_north, from_south, meridional, to_west, to_east, inner, products
):
    _, centre, _, _ = vertical_profiles()
    third = centre * (0.5 / TIME_INCREMENT)
    for i in range(1, CX - 1):
        if i < 4:
            inner[0, i] = to_west[i]
        elif i >= CX - 4:
            inner[0, i] = to_east[i - (CX - 4)]
        else:
            low, high, halo = completed_row(
                i, partial, meridional[i], from_north, from_south, third
            )
            inner[0, i, 0:8] = low
            inner[0, i, 8:16] = high
            inner[0, i, 16:24] = halo
    for j in range(ITERS - 1):
        for i in range(j + 2, CX - 2 - j):
            inner[j + 1, i] = applied(inner, None, j, i)
    sums = [jnp.zeros((8, LEVELS), f32) for _ in range(2 * ITERS)]
    sums = add_products(sums, inner, None, INNER_ROWS)
    for k in range(2 * ITERS):
        products[k] = sums[k]


def outer_kernel(
    inner,
    products,
    to_west,
    to_east,
    from_east,
    from_west,
    drops,
    live,
    outer,
    parcels,
):
    _, centre, _, _ = vertical_profiles()
    third = centre * (0.5 / TIME_INCREMENT)
    outer[0, 0] = to_west[0] + third * from_west[4]
    outer[0, CX - 1] = to_east[3] - third * from_east[4]
    for t in range(4):
        east = from_east[t]
        west = from_west[t]
        if t == 0:
            east = east + third * to_east[4]
        if t == 3:
            west = west - third * to_west[4]
        outer[0, CX + t] = east
        outer[0, CX + 4 + t] = west
    for j in range(ITERS - 1):
        reach = ITERS - 1 - j
        for i in range(-reach, CX + reach):
            if not j + 1 < i < CX - 2 - j:
                outer[j + 1, i % EX] = applied(inner, outer, j, i % EX)
    sums = [products[k] for k in range(2 * ITERS)]
    sums = add_products(sums, inner, outer, [i for i in range(CX) if i not in INNER_ROWS])
    sub8 = iota((8, LEVELS), 0)
    packed = jnp.zeros((8, LEVELS), f32)
    for k in range(2 * ITERS):
        packed = jnp.where(sub8 == k, jnp.sum(sums[k], axis=0, keepdims=True), packed)
    for r in range(SLOT_ROWS):
        parcels[r, 0:8] = drops[16 * r : 16 * r + 8]
        parcels[r, 8:16] = live[8 * r : 8 * r + 8]
        parcels[r, 16:24] = drops[16 * r + 8 : 16 * r + 16]
        parcels[r, 24:PARCEL] = packed


def two_sum(a, b):
    s = a + b
    t = s - a
    return s, (a - (s - t)) + (b - t)


def quick_sum(a, b):
    s = a + b
    return s, b - (s - a)


def split(a):
    t = a * 4097.0
    high = t - (t - a)
    return high, a - high


def two_product(a, b):
    p = a * b
    ah, al = split(a)
    bh, bl = split(b)
    return p, ((ah * bh - p) + ah * bl + al * bh) + al * bl


def pair_add(a, b):
    s, e = two_sum(a[0], b[0])
    return quick_sum(s, e + (a[1] + b[1]))


def pair_mul(a, b):
    p, e = two_product(a[0], b[0])
    return quick_sum(p, e + (a[0] * b[1] + a[1] * b[0]))


def pair_sub_mul(a, b, c):
    p = pair_mul(b, c)
    return pair_add(a, (-p[0], -p[1]))


def pair_inverse(a):
    guess = 1.0 / a[0]
    p = pair_mul(a, (guess, jnp.zeros_like(guess)))
    rest = (1.0 - p[0]) - p[1]
    return quick_sum(guess, guess * rest)


def coefficients(totals):
    high = totals[0]
    low = jnp.zeros_like(high)
    for t in range(1, totals.shape[0]):
        high, e = two_sum(high, totals[t])
        low = low + e
    bound = 256.0 * jnp.max(jnp.abs(high), axis=1, keepdims=True)
    coarse = (bound + high) - bound
    fine = (high - coarse) + low
    high, low = quick_sum(
        jnp.sum(coarse, axis=1, keepdims=True), jnp.sum(fine, axis=1, keepdims=True)
    )
    moment = []
    for k in range(2 * ITERS):
        moment.append(
            (
                jnp.broadcast_to(high[k : k + 1], (8, LEVELS)),
                jnp.broadcast_to(low[k : k + 1], (8, LEVELS)),
            )
        )
    matrix = [[moment[i + j + 1] for j in range(ITERS)] for i in range(ITERS)]
    side = [moment[i] for i in range(ITERS)]
    inverse = []
    for k in range(ITERS):
        inverse.append(pair_inverse(matrix[k][k]))
        for i in range(k + 1, ITERS):
            factor = pair_mul(matrix[k][i], inverse[k])
            for j in range(i, ITERS):
                matrix[i][j] = pair_sub_mul(matrix[i][j], factor, matrix[k][j])
            side[i] = pair_sub_mul(side[i], factor, side[k])
    result = [None] * ITERS
    for k in reversed(range(ITERS)):
        rest = side[k]
        for j in range(k + 1, ITERS):
            rest = pair_sub_mul(rest, matrix[k][j], result[j])
        result[k] = pair_mul(rest, inverse[k])
    return [(r[0] + r[1])[0:1] * SCALE for r in result]


def halves(values):
    high = values.astype(bf16).astype(f32)
    return high, values - high


HALF = TIME_INCREMENT * 0.5


def new_winds(i, potential, theta, humidity, zonal, meridional, vertical):
    level = iota((1, LEVELS), 1)
    here = potential[i + 1]
    mid = here[0:16]
    east = zonal[i] - HALF * (potential[i + 2, 0:16] - potential[i, 0:16])
    north = meridional[i] - HALF * (turn(here, -1, 0)[0:16] - turn(here, 1, 0)[0:16])
    up = lifted_row(i, theta, humidity, vertical) - HALF * (
        jnp.where(level < LEVELS - 1, turn(mid, -1, 1), 0.0)
        - jnp.where(level > 0, turn(mid, 1, 1), 0.0)
    )
    return east, north, up


def chunk(values, t):
    return jnp.concatenate([values[2 * t : 2 * t + 1], values[2 * t + 1 : 2 * t + 2]], axis=1)


def where_at(arrived, owner):
    cell = arrived[owner, 16:24].astype(jnp.int32)
    column = lax.shift_right_logical(cell, 7)
    return (
        jnp.bitwise_and(cell, LEVELS - 1) - KLO,
        jnp.bitwise_and(column, 1) * CX + lax.shift_right_logical(column, 1),
    )


def step_kernel(
    owners,
    totals,
    inner,
    outer,
    arrived,
    theta,
    humidity,
    zonal,
    meridional,
    vertical,
    from_north,
    from_south,
    from_east,
    from_west,
    far_theta,
    far_humidity,
    far_zonal,
    far_meridional,
    far_vertical,
    returned,
    potential,
    warmth,
    vapour,
    mass,
    excess,
    condensed,
    picked_excess,
    picked_warmth,
    spans,
    new_theta,
    new_humidity,
    new_zonal,
    new_meridional,
    new_vertical,
    departures,
):
    copies = [
        pltpu.make_async_copy(near, far, departures.at[n])
        for n, (near, far) in enumerate(
            (
                (new_theta, far_theta),
                (new_humidity, far_humidity),
                (new_zonal, far_zonal),
                (new_meridional, far_meridional),
                (new_vertical, far_vertical),
            )
        )
    ]
    level, _, _, _ = vertical_profiles()
    sub = iota((CY, LEVELS), 0)
    for i in range(CX):
        for f, (field, side, in_north, in_south) in enumerate(
            ((theta, 5, 5, 1), (humidity, 6, 6, 2))
        ):
            values = field[i]
            f_e = field[i + 1] if i < CX - 1 else from_east[side, 0:16]
            f_w = field[i - 1] if i > 0 else from_west[side, 0:16]
            f_n = jnp.where(
                sub < CY - 1, turn(values, -1, 0), from_north[i, in_north : in_north + 1]
            )
            f_s = jnp.where(sub > 0, turn(values, 1, 0), from_south[i, in_south : in_south + 1])
            f_t = jnp.where(level < LEVELS - 1, turn(values, -1, 1), values)
            f_b = jnp.where(level > 0, turn(values, 1, 1), values)
            for n, span in enumerate(
                (values - f_w, f_e - values, values - f_s, f_n - values, values - f_b, f_t - values)
            ):
                spans[6 * f + n, i] = span
    weights = coefficients(totals)
    for t in range(CX + 2):
        i = (t - 1) % EX
        total = weights[0] * power_row(inner, outer, 0, i)
        for j in range(1, ITERS):
            total = total + weights[j] * power_row(inner, outer, j, i)
        potential[t] = total
    for i in range(CX):
        east, north, up = new_winds(i, potential, theta, humidity, zonal, meridional, vertical)
        new_zonal[i] = east
        new_meridional[i] = north
        new_vertical[i] = up
        moved = []
        for f, field in enumerate((theta, humidity)):
            tendency = (
                east * jnp.where(east > 0.0, spans[6 * f, i], spans[6 * f + 1, i])
                + north * jnp.where(north > 0.0, spans[6 * f + 2, i], spans[6 * f + 3, i])
                + up * jnp.where(up > 0.0, spans[6 * f + 4, i], spans[6 * f + 5, i])
            )
            moved.append(field[i] - TIME_INCREMENT * tendency)
        rows = slice(CY * i, CY * (i + 1))
        warmth[rows] = moved[0]
        vapour[rows] = moved[1]
        excess[rows] = moved[1] * jnp.exp(-CLAUSIUS_FACTOR * moved[0]) - 1.0

    for copy in copies[2:]:
        copy.start()
    lane = iota((2 * CX, LEVELS), 1)
    height = iota((BAND, 2 * LEVELS), 0)
    place = iota((2 * CX, 2 * LEVELS), 0)

    def band(field, b):
        values = jnp.concatenate(
            [
                field[pl.ds(2 * b, CX, stride=CY), :],
                field[pl.ds(2 * b + 1, CX, stride=CY), :],
            ],
            axis=0,
        )
        high, low = halves(values)
        both = jnp.where(lane < BAND, turn(high, -KLO, 1), turn(low, BAND - KLO, 1))
        return both[:, : 2 * BAND].astype(bf16)

    for b in range(NBD):
        table = jnp.concatenate([band(excess, b), band(warmth, b)], axis=0)
        heights, places = where_at(arrived, owners[b])
        for t in range(CHUNKS // 2):
            hot = jnp.where(height == chunk(heights, t), 1.0, 0.0).astype(bf16)
            found = jnp.dot(
                table, jnp.concatenate([hot, hot], axis=0), preferred_element_type=f32
            )
            mine = place == chunk(places, t)
            for target, part in ((picked_excess, found[: 2 * CX]), (picked_warmth, found[2 * CX :])):
                value = jnp.sum(jnp.where(mine, part, 0.0), axis=0, keepdims=True)
                row = CHUNKS * b + 2 * t
                target[row : row + 1] = value[:, :LEVELS]
                target[row + 1 : row + 2] = value[:, LEVELS:]
    returned[...] = jnp.zeros(returned.shape, f32)
    for b in range(NBD):
        rows = slice(CHUNKS * b, CHUNKS * (b + 1))
        owner = owners[b]
        old = arrived[owner, 0:8]
        number = arrived[owner, 8:16]
        oversaturation = picked_excess[rows]
        rate = GROWTH * jnp.exp(GROWTH_SLOPE * picked_warmth[rows])
        now = old
        for substep in range(NSUB):
            now = jnp.maximum(
                now + 2.0 * SUB_STEP * rate * (oversaturation - CURVATURE / jnp.sqrt(now)),
                FLOOR_SQUARE,
            )
        mass[rows] = jnp.where(
            number > 0.0, number * (now * jnp.sqrt(now) - old * jnp.sqrt(old)), 0.0
        )
        returned[owner] = now
    for b in range(NBD):
        heights, places = where_at(arrived, owners[b])
        gained = mass[CHUNKS * b : CHUNKS * (b + 1)]
        total = jnp.zeros((4 * CX, BAND), f32)
        for t in range(CHUNKS // 2):
            hot = jnp.where(height == chunk(heights, t), 1.0, 0.0).astype(bf16)
            mine = place == chunk(places, t)
            high, low = halves(chunk(gained, t))
            spread = jnp.concatenate(
                [
                    jnp.where(mine, high, 0.0).astype(bf16),
                    jnp.where(mine, low, 0.0).astype(bf16),
                ],
                axis=0,
            )
            total = total + lax.dot_general(
                spread, hot, (((1,), (1,)), ((), ())), preferred_element_type=f32
            )
        liquid = CONDENSE * (total[: 2 * CX] + total[2 * CX :])
        liquid = jnp.concatenate([liquid, jnp.zeros((2 * CX, LEVELS - BAND), f32)], axis=1)
        liquid = turn(liquid, KLO, 1)
        condensed[pl.ds(2 * b, CX, stride=CY), :] = liquid[:CX]
        condensed[pl.ds(2 * b + 1, CX, stride=CY), :] = liquid[CX:]
    for i in range(CX):
        rows = slice(CY * i, CY * (i + 1))
        new_theta[i] = warmth[rows] + PHASE_WARMING * condensed[rows]
        new_humidity[i] = vapour[rows] - condensed[rows]
    for copy in copies[:2]:
        copy.start()
    for copy in copies:
        copy.wait()


def size_kernel(counts, returned, squares, new_squares):
    row = iota((SLOT_ROWS, LEVELS), 0)
    lane = iota((SLOT_ROWS, LEVELS), 1)
    live = jnp.zeros((SLOT_ROWS, LEVELS), jnp.int32)
    for r in range(SLOT_ROWS):
        live = jnp.where(row == r, counts[r], live)
    for s in range(CHUNKS):
        part = slice(LEVELS * s, LEVELS * (s + 1))
        new_squares[:, part] = jnp.where(
            lane + LEVELS * s < live,
            returned[pl.ds(s, SLOT_ROWS, stride=CHUNKS), :],
            squares[:, part],
        )


def local(kernel, outs, scalars, operands, scratch=(), far=0, far_outs=0, limit=VMEM_LIMIT, cost=1_000_000):
    whole = pl.BlockSpec(memory_space=pltpu.VMEM)
    single = len(outs) == 1
    return pl.pallas_call(
        kernel,
        out_shape=outs[0] if single else outs,
        in_specs=[pl.BlockSpec(memory_space=pltpu.SMEM)] * len(scalars)
        + [pl.BlockSpec(memory_space=pltpu.HBM)] * far
        + [whole] * (len(operands) - far),
        out_specs=whole
        if single
        else [pl.BlockSpec(memory_space=pltpu.HBM)] * far_outs + [whole] * (len(outs) - far_outs),
        scratch_shapes=list(scratch),
        compiler_params=pltpu.CompilerParams(vmem_limit_bytes=limit),
        cost_estimate=pl.CostEstimate(flops=cost, bytes_accessed=cost, transcendentals=0),
    )(*scalars, *operands)


def shape(*dims):
    return jax.ShapeDtypeStruct(dims, f32)


def ring(axes, step):
    count = lax.axis_size(axes)
    return [(i, (i + step) % count) for i in range(count)]


def on_device(
    theta, humidity, zonal, meridional, vertical, owner_map, population, squares, numbers, cells
):
    owners = owner_map.reshape(NBD)
    counts = population.reshape(SLOT_ROWS)
    squares = squares.reshape(SLOT_ROWS, DPB)
    numbers = numbers.reshape(SLOT_ROWS, DPB)
    cells = cells.reshape(SLOT_ROWS, DPB)
    tiles = ("grp", "gx")
    tile = shape(CX, CY, LEVELS)
    partial, to_south, to_north, edges = local(
        right_side_kernel,
        [tile, shape(CX + 2, 8, LEVELS), shape(CX + 2, 8, LEVELS), shape(14, CY, LEVELS)],
        [],
        [theta, humidity, zonal, meridional, vertical],
        [pltpu.VMEM((CX, CY, LEVELS), f32)] * 5 + [pltpu.SemaphoreType.DMA((5,))],
        far=5,
        limit=FIRST_LIMIT,
    )
    from_north = lax.ppermute(to_south, "gy", ring("gy", -1))
    from_south = lax.ppermute(to_north, "gy", ring("gy", 1))
    edges, early_squares, early_cells = lax.optimization_barrier((edges, squares, cells))
    drops = local(
        pack_kernel, [shape(SLOT_ROWS * 16, LEVELS)], [], [early_squares, early_cells], cost=COSTP
    )
    edges, drops = lax.optimization_barrier((edges, drops))
    to_west, to_east = local(
        side_kernel,
        [shape(7, EY, LEVELS), shape(7, EY, LEVELS)],
        [],
        [partial, from_north, from_south, edges],
    )
    to_west, to_east, late_numbers = lax.optimization_barrier((to_west, to_east, numbers))
    live = local(pack_live_kernel, [shape(SLOT_ROWS * 8, LEVELS)], [counts], [late_numbers], cost=COSTP)
    from_east = lax.ppermute(to_west, tiles, ring(tiles, -1))
    from_west = lax.ppermute(to_east, tiles, ring(tiles, 1))
    inner, products = local(
        inner_kernel,
        [shape(ITERS, CX, EY, LEVELS), shape(2 * ITERS, 8, LEVELS)],
        [],
        [partial, from_north, from_south, meridional, to_west, to_east],
    )
    outer, parcels = local(
        outer_kernel,
        [shape(ITERS, EX, EY, LEVELS), shape(SLOT_ROWS, PARCEL, LEVELS)],
        [],
        [inner, products, to_west, to_east, from_east, from_west, drops, live],
    )
    arrived = lax.all_to_all(parcels, "gx", split_axis=0, concat_axis=0, tiled=True)
    shared = jnp.broadcast_to(jnp.sum(arrived[:, 24:], axis=0)[None], (16, 8, LEVELS))
    totals = lax.all_to_all(shared, ("grp", "gy"), split_axis=0, concat_axis=0, tiled=True)
    flat = (CX * CY, LEVELS)
    picked = (NBD * CHUNKS, LEVELS)
    new_theta, new_humidity, new_zonal, new_meridional, new_vertical, returned = local(
        step_kernel,
        [tile] * 5 + [shape(SLOT_ROWS, CHUNKS, LEVELS)],
        [owners],
        [
            totals,
            inner,
            outer,
            arrived,
            theta,
            humidity,
            zonal,
            meridional,
            vertical,
            from_north,
            from_south,
            from_east,
            from_west,
        ],
        [pltpu.VMEM((CX + 2, EY, LEVELS), f32)]
        + [pltpu.VMEM(flat, f32)] * 2
        + [pltpu.VMEM(picked, f32)]
        + [pltpu.VMEM(flat, f32)] * 2
        + [pltpu.VMEM(picked, f32)] * 2
        + [pltpu.VMEM((12, CX, CY, LEVELS), f32)]
        + [pltpu.VMEM((CX, CY, LEVELS), f32)] * 5
        + [pltpu.SemaphoreType.DMA((5,))],
        far_outs=5,
    )
    returned = lax.all_to_all(returned, "gx", split_axis=0, concat_axis=0, tiled=True)
    new_squares = local(
        size_kernel,
        [shape(SLOT_ROWS, DPB)],
        [counts],
        [returned.reshape(SLOT_ROWS * CHUNKS, LEVELS), squares],
    )
    return (
        new_theta,
        new_humidity,
        new_zonal,
        new_meridional,
        new_vertical,
        new_squares[None, None],
    )


def solution(mesh):
    field = P(("grp", "gx"), "gy", None)
    slots = P(("grp", "gx"), "gy", None, None)
    return jax.shard_map(
        on_device,
        mesh=mesh,
        in_specs=(field,) * 7 + (slots,) * 3,
        out_specs=(field,) * 5 + (slots,),
        check_vma=False,
    )
```

```python
import functools

import jax
import jax.numpy as jnp
from jax import lax
from jax.experimental import pallas as pl
from jax.experimental.pallas import tpu as pltpu
from jax.sharding import PartitionSpec as P

TIME_INCREMENT = 0.15
THERMAL_LIFT = 0.5
HUMID_LIFT = 0.3
HELMHOLTZ = 0.001
CLAUSIUS_FACTOR = 0.2
GROWTH = 0.5
GROWTH_SLOPE = 0.1
SUB_STEP = 0.25
CURVATURE = 0.05
FLOOR_SQUARE = 0.04
CONDENSE = 0.2
PHASE_WARMING = 2.5

NSUB = 4
ITERS = 4
NBD = 8
CX = 24
CY = 16
LEVELS = 128
KLO = 48
BAND = 32
EX = 32
EY = 24
SLOT_ROWS = 16
DPB = 1024
CHUNKS = DPB // LEVELS
PARCEL = 32
SCALE = 1.0 / 6.0
VMEM_LIMIT = 24 * 1024 * 1024
COSTP = 1_000_000
FIRST_LIMIT = 54600 * 1024

f32 = jnp.float32
bf16 = jnp.bfloat16


def iota(shape, axis):
    return lax.broadcasted_iota(jnp.int32, shape, axis)


def vertical_profiles():
    level = iota((1, LEVELS), 1)
    height = level.astype(f32)
    centre = jnp.exp(-(height + 0.5) / LEVELS)
    face = jnp.where(level < LEVELS - 1, jnp.exp(-(height + 1.0) / LEVELS), 0.0)
    face_below = jnp.where(level > 0, jnp.exp(-height / LEVELS), 0.0)
    return level, centre, face, face_below


def turn(values, by, axis):
    return pltpu.roll(values, by % values.shape[axis], axis)


def lifted_row(i, theta, humidity, vertical):
    return vertical[i] + TIME_INCREMENT * (THERMAL_LIFT * theta[i] + HUMID_LIFT * humidity[i])


def right_side_kernel(
    theta_far,
    humidity_far,
    zonal_far,
    meridional_far,
    vertical_far,
    partial,
    to_south,
    to_north,
    edges,
    theta,
    humidity,
    zonal,
    meridional,
    vertical,
    arrivals,
):
    copies = [
        pltpu.make_async_copy(far, near, arrivals.at[n])
        for n, (far, near) in enumerate(
            (
                (theta_far, theta),
                (humidity_far, humidity),
                (zonal_far, zonal),
                (meridional_far, meridional),
                (vertical_far, vertical),
            )
        )
    ]
    for copy in copies:
        copy.start()
    for copy in copies:
        copy.wait()
    level, centre, _, _ = vertical_profiles()
    sub = iota((CY, LEVELS), 0)
    sub8 = iota((8, LEVELS), 0)
    for i in range(CX):
        weighted = centre * lifted_row(i, theta, humidity, vertical)
        rise = jnp.where(level < LEVELS - 1, turn(weighted, -1, 1), 0.0) - jnp.where(
            level > 0, turn(weighted, 1, 1), 0.0
        )
        if i == 0:
            across = zonal[1]
        elif i == CX - 1:
            across = -zonal[CX - 2]
        else:
            across = zonal[i + 1] - zonal[i - 1]
        wind = meridional[i]
        along = jnp.where(sub < CY - 1, turn(wind, -1, 0), 0.0) - jnp.where(
            sub > 0, turn(wind, 1, 0), 0.0
        )
        right = (centre * (across * 0.5 + along * 0.5) + 0.5 * rise) * (-1.0 / TIME_INCREMENT)
        partial[i] = right
        warm = theta[i]
        damp = humidity[i]
        to_south[i] = jnp.where(
            sub8 < 4,
            right[0:8],
            jnp.where(sub8 == 4, wind[0:1], jnp.where(sub8 == 5, warm[0:1], damp[0:1])),
        )
        to_north[i] = jnp.where(
            sub8 >= 4,
            right[8:16],
            jnp.where(sub8 == 0, wind[15:16], jnp.where(sub8 == 1, warm[15:16], damp[15:16])),
        )
    for n, i in enumerate((0, CX - 1)):
        to_south[CX + n] = zonal[i, 0:8]
        to_north[CX + n] = zonal[i, 8:16]
        edges[7 * n + 4] = zonal[i]
        edges[7 * n + 5] = theta[i]
        edges[7 * n + 6] = humidity[i]
    for t in range(4):
        edges[t] = meridional[t]
        edges[7 + t] = meridional[CX - 4 + t]


def joined(north, south):
    return jnp.where(iota((8, LEVELS), 0) < 4, north, south)


def completed_row(i, partial, wind, from_north, from_south, third):
    sub8 = iota((8, LEVELS), 0)
    north = from_north[i]
    south = from_south[i]
    low = partial[i, 0:8] + jnp.where(sub8 == 0, third * south[0:1], 0.0)
    high = partial[i, 8:16] - jnp.where(sub8 == 7, third * north[4:5], 0.0)
    halo = (
        joined(north, south)
        + jnp.where(sub8 == 0, third * wind[15:16], 0.0)
        - jnp.where(sub8 == 7, third * wind[0:1], 0.0)
    )
    return low, high, halo


def side_kernel(partial, from_north, from_south, edges, to_west, to_east):
    _, centre, _, _ = vertical_profiles()
    third = centre * (0.5 / TIME_INCREMENT)
    for n, (target, first) in enumerate(((to_west, 0), (to_east, CX - 4))):
        for t in range(4):
            low, high, halo = completed_row(
                first + t, partial, edges[7 * n + t], from_north, from_south, third
            )
            target[t, 0:8] = low
            target[t, 8:16] = high
            target[t, 16:24] = halo
        target[4, 0:16] = edges[7 * n + 4]
        target[4, 16:24] = joined(from_north[CX + n], from_south[CX + n])
        for t in (5, 6):
            target[t, 0:16] = edges[7 * n + t]
            target[t, 16:24] = jnp.zeros((8, LEVELS), f32)


def pack_kernel(squares, cells, packed):
    for s in range(CHUNKS):
        part = slice(LEVELS * s, LEVELS * (s + 1))
        packed[pl.ds(s, SLOT_ROWS, stride=16), :] = squares[:, part]
        packed[pl.ds(8 + s, SLOT_ROWS, stride=16), :] = cells[:, part].astype(f32)


def pack_live_kernel(counts, numbers, packed):
    row = iota((SLOT_ROWS, LEVELS), 0)
    lane = iota((SLOT_ROWS, LEVELS), 1)
    live = jnp.zeros((SLOT_ROWS, LEVELS), jnp.int32)
    for r in range(SLOT_ROWS):
        live = jnp.where(row == r, counts[r], live)
    for s in range(CHUNKS):
        part = slice(LEVELS * s, LEVELS * (s + 1))
        packed[pl.ds(s, SLOT_ROWS, stride=8), :] = jnp.where(
            lane + LEVELS * s < live, numbers[:, part], 0.0
        )


def power_row(inner, outer, j, i):
    return inner[j, i] if j < i < CX - 1 - j else outer[j, i]


def applied(inner, outer, j, i):
    _, centre, face, face_below = vertical_profiles()
    here = ((4.0 + HELMHOLTZ) * centre + face + face_below) * SCALE
    values = power_row(inner, outer, j, i)
    lateral = (
        power_row(inner, outer, j, (i + 1) % EX)
        + power_row(inner, outer, j, (i - 1) % EX)
        + turn(values, -1, 0)
        + turn(values, 1, 0)
    )
    return (
        here * values
        - (centre * SCALE) * lateral
        - (face * SCALE) * turn(values, -1, 1)
        - (face_below * SCALE) * turn(values, 1, 1)
    )


def add_products(sums, inner, outer, rows):
    sums = list(sums)
    for i in rows:
        terms = [power_row(inner, outer, j, i)[0:16] for j in range(ITERS)]
        terms.append(applied(inner, outer, ITERS - 1, i)[0:16])
        for k in range(2 * ITERS):
            product = terms[k // 2] * terms[(k + 1) // 2]
            sums[k] = sums[k] + (product[0:8] + product[8:16])
    return sums


INNER_ROWS = range(ITERS + 1, CX - ITERS - 1)


def inner_kernel(
    partial, from_north, from_south, meridional, to_west, to_east, inner, products
):
    _, centre, _, _ = vertical_profiles()
    third = centre * (0.5 / TIME_INCREMENT)
    for i in range(1, CX - 1):
        if i < 4:
            inner[0, i] = to_west[i]
        elif i >= CX - 4:
            inner[0, i] = to_east[i - (CX - 4)]
        else:
            low, high, halo = completed_row(
                i, partial, meridional[i], from_north, from_south, third
            )
            inner[0, i, 0:8] = low
            inner[0, i, 8:16] = high
            inner[0, i, 16:24] = halo
    for j in range(ITERS - 1):
        for i in range(j + 2, CX - 2 - j):
            inner[j + 1, i] = applied(inner, None, j, i)
    sums = [jnp.zeros((8, LEVELS), f32) for _ in range(2 * ITERS)]
    sums = add_products(sums, inner, None, INNER_ROWS)
    for k in range(2 * ITERS):
        products[k] = sums[k]


def outer_kernel(
    inner,
    products,
    to_west,
    to_east,
    from_east,
    from_west,
    drops,
    live,
    outer,
    parcels,
):
    _, centre, _, _ = vertical_profiles()
    third = centre * (0.5 / TIME_INCREMENT)
    outer[0, 0] = to_west[0] + third * from_west[4]
    outer[0, CX - 1] = to_east[3] - third * from_east[4]
    for t in range(4):
        east = from_east[t]
        west = from_west[t]
        if t == 0:
            east = east + third * to_east[4]
        if t == 3:
            west = west - third * to_west[4]
        outer[0, CX + t] = east
        outer[0, CX + 4 + t] = west
    for j in range(ITERS - 1):
        reach = ITERS - 1 - j
        for i in range(-reach, CX + reach):
            if not j + 1 < i < CX - 2 - j:
                outer[j + 1, i % EX] = applied(inner, outer, j, i % EX)
    sums = [products[k] for k in range(2 * ITERS)]
    sums = add_products(sums, inner, outer, [i for i in range(CX) if i not in INNER_ROWS])
    sub8 = iota((8, LEVELS), 0)
    packed = jnp.zeros((8, LEVELS), f32)
    for k in range(2 * ITERS):
        packed = jnp.where(sub8 == k, jnp.sum(sums[k], axis=0, keepdims=True), packed)
    for r in range(SLOT_ROWS):
        parcels[r, 0:8] = drops[16 * r : 16 * r + 8]
        parcels[r, 8:16] = live[8 * r : 8 * r + 8]
        parcels[r, 16:24] = drops[16 * r + 8 : 16 * r + 16]
        parcels[r, 24:PARCEL] = packed


def two_sum(a, b):
    s = a + b
    t = s - a
    return s, (a - (s - t)) + (b - t)


def quick_sum(a, b):
    s = a + b
    return s, b - (s - a)


def split(a):
    t = a * 4097.0
    high = t - (t - a)
    return high, a - high


def two_product(a, b):
    p = a * b
    ah, al = split(a)
    bh, bl = split(b)
    return p, ((ah * bh - p) + ah * bl + al * bh) + al * bl


def pair_add(a, b):
    s, e = two_sum(a[0], b[0])
    return quick_sum(s, e + (a[1] + b[1]))


def pair_mul(a, b):
    p, e = two_product(a[0], b[0])
    return quick_sum(p, e + (a[0] * b[1] + a[1] * b[0]))


def pair_sub_mul(a, b, c):
    p = pair_mul(b, c)
    return pair_add(a, (-p[0], -p[1]))


def pair_inverse(a):
    guess = 1.0 / a[0]
    p = pair_mul(a, (guess, jnp.zeros_like(guess)))
    rest = (1.0 - p[0]) - p[1]
    return quick_sum(guess, guess * rest)


def coefficients(totals):
    high = totals[0]
    low = jnp.zeros_like(high)
    for t in range(1, totals.shape[0]):
        high, e = two_sum(high, totals[t])
        low = low + e
    bound = 256.0 * jnp.max(jnp.abs(high), axis=1, keepdims=True)
    coarse = (bound + high) - bound
    fine = (high - coarse) + low
    high, low = quick_sum(
        jnp.sum(coarse, axis=1, keepdims=True), jnp.sum(fine, axis=1, keepdims=True)
    )
    moment = []
    for k in range(2 * ITERS):
        moment.append(
            (
                jnp.broadcast_to(high[k : k + 1], (8, LEVELS)),
                jnp.broadcast_to(low[k : k + 1], (8, LEVELS)),
            )
        )
    matrix = [[moment[i + j + 1] for j in range(ITERS)] for i in range(ITERS)]
    side = [moment[i] for i in range(ITERS)]
    inverse = []
    for k in range(ITERS):
        inverse.append(pair_inverse(matrix[k][k]))
        for i in range(k + 1, ITERS):
            factor = pair_mul(matrix[k][i], inverse[k])
            for j in range(i, ITERS):
                matrix[i][j] = pair_sub_mul(matrix[i][j], factor, matrix[k][j])
            side[i] = pair_sub_mul(side[i], factor, side[k])
    result = [None] * ITERS
    for k in reversed(range(ITERS)):
        rest = side[k]
        for j in range(k + 1, ITERS):
            rest = pair_sub_mul(rest, matrix[k][j], result[j])
        result[k] = pair_mul(rest, inverse[k])
    return [(r[0] + r[1])[0:1] * SCALE for r in result]


def halves(values):
    high = values.astype(bf16).astype(f32)
    return high, values - high


HALF = TIME_INCREMENT * 0.5


def new_winds(i, potential, theta, humidity, zonal, meridional, vertical):
    level = iota((1, LEVELS), 1)
    here = potential[i + 1]
    mid = here[0:16]
    east = zonal[i] - HALF * (potential[i + 2, 0:16] - potential[i, 0:16])
    north = meridional[i] - HALF * (turn(here, -1, 0)[0:16] - turn(here, 1, 0)[0:16])
    up = lifted_row(i, theta, humidity, vertical) - HALF * (
        jnp.where(level < LEVELS - 1, turn(mid, -1, 1), 0.0)
        - jnp.where(level > 0, turn(mid, 1, 1), 0.0)
    )
    return east, north, up


def chunk(values, t):
    return jnp.concatenate([values[2 * t : 2 * t + 1], values[2 * t + 1 : 2 * t + 2]], axis=1)


def where_at(arrived, owner):
    cell = arrived[owner, 16:24].astype(jnp.int32)
    column = lax.shift_right_logical(cell, 7)
    return (
        jnp.bitwise_and(cell, LEVELS - 1) - KLO,
        jnp.bitwise_and(column, 1) * CX + lax.shift_right_logical(column, 1),
    )


def step_kernel(
    owners,
    totals,
    inner,
    outer,
    arrived,
    theta,
    humidity,
    zonal,
    meridional,
    vertical,
    from_north,
    from_south,
    from_east,
    from_west,
    new_theta,
    new_humidity,
    new_zonal,
    new_meridional,
    new_vertical,
    returned,
    potential,
    warmth,
    vapour,
    mass,
    excess,
    condensed,
    picked_excess,
    picked_warmth,
    spans,
):
    level, _, _, _ = vertical_profiles()
    sub = iota((CY, LEVELS), 0)
    for i in range(CX):
        for f, (field, side, in_north, in_south) in enumerate(
            ((theta, 5, 5, 1), (humidity, 6, 6, 2))
        ):
            values = field[i]
            f_e = field[i + 1] if i < CX - 1 else from_east[side, 0:16]
            f_w = field[i - 1] if i > 0 else from_west[side, 0:16]
            f_n = jnp.where(
                sub < CY - 1, turn(values, -1, 0), from_north[i, in_north : in_north + 1]
            )
            f_s = jnp.where(sub > 0, turn(values, 1, 0), from_south[i, in_south : in_south + 1])
            f_t = jnp.where(level < LEVELS - 1, turn(values, -1, 1), values)
            f_b = jnp.where(level > 0, turn(values, 1, 1), values)
            for n, span in enumerate(
                (values - f_w, f_e - values, values - f_s, f_n - values, values - f_b, f_t - values)
            ):
                spans[6 * f + n, i] = span
    weights = coefficients(totals)
    for t in range(CX + 2):
        i = (t - 1) % EX
        total = weights[0] * power_row(inner, outer, 0, i)
        for j in range(1, ITERS):
            total = total + weights[j] * power_row(inner, outer, j, i)
        potential[t] = total
    for i in range(CX):
        east, north, up = new_winds(i, potential, theta, humidity, zonal, meridional, vertical)
        new_zonal[i] = east
        new_meridional[i] = north
        new_vertical[i] = up
        moved = []
        for f, field in enumerate((theta, humidity)):
            tendency = (
                east * jnp.where(east > 0.0, spans[6 * f, i], spans[6 * f + 1, i])
                + north * jnp.where(north > 0.0, spans[6 * f + 2, i], spans[6 * f + 3, i])
                + up * jnp.where(up > 0.0, spans[6 * f + 4, i], spans[6 * f + 5, i])
            )
            moved.append(field[i] - TIME_INCREMENT * tendency)
        rows = slice(CY * i, CY * (i + 1))
        warmth[rows] = moved[0]
        vapour[rows] = moved[1]
        excess[rows] = moved[1] * jnp.exp(-CLAUSIUS_FACTOR * moved[0]) - 1.0

    lane = iota((2 * CX, LEVELS), 1)
    height = iota((BAND, 2 * LEVELS), 0)
    place = iota((2 * CX, 2 * LEVELS), 0)

    def band(field, b):
        values = jnp.concatenate(
            [
                field[pl.ds(2 * b, CX, stride=CY), :],
                field[pl.ds(2 * b + 1, CX, stride=CY), :],
            ],
            axis=0,
        )
        high, low = halves(values)
        both = jnp.where(lane < BAND, turn(high, -KLO, 1), turn(low, BAND - KLO, 1))
        return both[:, : 2 * BAND].astype(bf16)

    for b in range(NBD):
        table = jnp.concatenate([band(excess, b), band(warmth, b)], axis=0)
        heights, places = where_at(arrived, owners[b])
        for t in range(CHUNKS // 2):
            hot = jnp.where(height == chunk(heights, t), 1.0, 0.0).astype(bf16)
            found = jnp.dot(
                table, jnp.concatenate([hot, hot], axis=0), preferred_element_type=f32
            )
            mine = place == chunk(places, t)
            for target, part in ((picked_excess, found[: 2 * CX]), (picked_warmth, found[2 * CX :])):
                value = jnp.sum(jnp.where(mine, part, 0.0), axis=0, keepdims=True)
                row = CHUNKS * b + 2 * t
                target[row : row + 1] = value[:, :LEVELS]
                target[row + 1 : row + 2] = value[:, LEVELS:]
    returned[...] = jnp.zeros(returned.shape, f32)
    for b in range(NBD):
        rows = slice(CHUNKS * b, CHUNKS * (b + 1))
        owner = owners[b]
        old = arrived[owner, 0:8]
        number = arrived[owner, 8:16]
        oversaturation = picked_excess[rows]
        rate = GROWTH * jnp.exp(GROWTH_SLOPE * picked_warmth[rows])
        now = old
        for substep in range(NSUB):
            now = jnp.maximum(
                now + 2.0 * SUB_STEP * rate * (oversaturation - CURVATURE / jnp.sqrt(now)),
                FLOOR_SQUARE,
            )
        mass[rows] = jnp.where(
            number > 0.0, number * (now * jnp.sqrt(now) - old * jnp.sqrt(old)), 0.0
        )
        returned[owner] = now
    for b in range(NBD):
        heights, places = where_at(arrived, owners[b])
        gained = mass[CHUNKS * b : CHUNKS * (b + 1)]
        total = jnp.zeros((4 * CX, BAND), f32)
        for t in range(CHUNKS // 2):
            hot = jnp.where(height == chunk(heights, t), 1.0, 0.0).astype(bf16)
            mine = place == chunk(places, t)
            high, low = halves(chunk(gained, t))
            spread = jnp.concatenate(
                [
                    jnp.where(mine, high, 0.0).astype(bf16),
                    jnp.where(mine, low, 0.0).astype(bf16),
                ],
                axis=0,
            )
            total = total + lax.dot_general(
                spread, hot, (((1,), (1,)), ((), ())), preferred_element_type=f32
            )
        liquid = CONDENSE * (total[: 2 * CX] + total[2 * CX :])
        liquid = jnp.concatenate([liquid, jnp.zeros((2 * CX, LEVELS - BAND), f32)], axis=1)
        liquid = turn(liquid, KLO, 1)
        condensed[pl.ds(2 * b, CX, stride=CY), :] = liquid[:CX]
        condensed[pl.ds(2 * b + 1, CX, stride=CY), :] = liquid[CX:]
    for i in range(CX):
        rows = slice(CY * i, CY * (i + 1))
        new_theta[i] = warmth[rows] + PHASE_WARMING * condensed[rows]
        new_humidity[i] = vapour[rows] - condensed[rows]


def last_kernel(
    counts,
    returned,
    squares,
    theta,
    humidity,
    zonal,
    meridional,
    vertical,
    far_theta,
    far_humidity,
    far_zonal,
    far_meridional,
    far_vertical,
    far_squares,
    new_squares,
    departures,
):
    copies = [
        pltpu.make_async_copy(near, far, departures.at[n])
        for n, (near, far) in enumerate(
            (
                (theta, far_theta),
                (humidity, far_humidity),
                (zonal, far_zonal),
                (meridional, far_meridional),
                (vertical, far_vertical),
                (new_squares, far_squares),
            )
        )
    ]
    for copy in copies[:5]:
        copy.start()
    row = iota((SLOT_ROWS, LEVELS), 0)
    lane = iota((SLOT_ROWS, LEVELS), 1)
    live = jnp.zeros((SLOT_ROWS, LEVELS), jnp.int32)
    for r in range(SLOT_ROWS):
        live = jnp.where(row == r, counts[r], live)
    for s in range(CHUNKS):
        part = slice(LEVELS * s, LEVELS * (s + 1))
        new_squares[:, part] = jnp.where(
            lane + LEVELS * s < live,
            returned[pl.ds(s, SLOT_ROWS, stride=CHUNKS), :],
            squares[:, part],
        )
    copies[5].start()
    for copy in copies:
        copy.wait()


def local(kernel, outs, scalars, operands, scratch=(), far=0, far_outs=0, limit=VMEM_LIMIT, cost=1_000_000):
    whole = pl.BlockSpec(memory_space=pltpu.VMEM)
    single = len(outs) == 1
    return pl.pallas_call(
        kernel,
        out_shape=outs[0] if single else outs,
        in_specs=[pl.BlockSpec(memory_space=pltpu.SMEM)] * len(scalars)
        + [pl.BlockSpec(memory_space=pltpu.HBM)] * far
        + [whole] * (len(operands) - far),
        out_specs=whole
        if single
        else [pl.BlockSpec(memory_space=pltpu.HBM)] * far_outs + [whole] * (len(outs) - far_outs),
        scratch_shapes=list(scratch),
        compiler_params=pltpu.CompilerParams(vmem_limit_bytes=limit),
        cost_estimate=pl.CostEstimate(flops=cost, bytes_accessed=cost, transcendentals=0),
    )(*scalars, *operands)


def shape(*dims):
    return jax.ShapeDtypeStruct(dims, f32)


def ring(axes, step):
    count = lax.axis_size(axes)
    return [(i, (i + step) % count) for i in range(count)]


def on_device(
    theta, humidity, zonal, meridional, vertical, owner_map, population, squares, numbers, cells
):
    owners = owner_map.reshape(NBD)
    counts = population.reshape(SLOT_ROWS)
    squares = squares.reshape(SLOT_ROWS, DPB)
    numbers = numbers.reshape(SLOT_ROWS, DPB)
    cells = cells.reshape(SLOT_ROWS, DPB)
    tiles = ("grp", "gx")
    tile = shape(CX, CY, LEVELS)
    partial, to_south, to_north, edges = local(
        right_side_kernel,
        [tile, shape(CX + 2, 8, LEVELS), shape(CX + 2, 8, LEVELS), shape(14, CY, LEVELS)],
        [],
        [theta, humidity, zonal, meridional, vertical],
        [pltpu.VMEM((CX, CY, LEVELS), f32)] * 5 + [pltpu.SemaphoreType.DMA((5,))],
        far=5,
        limit=FIRST_LIMIT,
    )
    from_north = lax.ppermute(to_south, "gy", ring("gy", -1))
    from_south = lax.ppermute(to_north, "gy", ring("gy", 1))
    edges, early_squares, early_cells = lax.optimization_barrier((edges, squares, cells))
    drops = local(
        pack_kernel, [shape(SLOT_ROWS * 16, LEVELS)], [], [early_squares, early_cells], cost=COSTP
    )
    edges, drops = lax.optimization_barrier((edges, drops))
    to_west, to_east = local(
        side_kernel,
        [shape(7, EY, LEVELS), shape(7, EY, LEVELS)],
        [],
        [partial, from_north, from_south, edges],
    )
    to_west, to_east, late_numbers = lax.optimization_barrier((to_west, to_east, numbers))
    live = local(pack_live_kernel, [shape(SLOT_ROWS * 8, LEVELS)], [counts], [late_numbers], cost=COSTP)
    from_east = lax.ppermute(to_west, tiles, ring(tiles, -1))
    from_west = lax.ppermute(to_east, tiles, ring(tiles, 1))
    inner, products = local(
        inner_kernel,
        [shape(ITERS, CX, EY, LEVELS), shape(2 * ITERS, 8, LEVELS)],
        [],
        [partial, from_north, from_south, meridional, to_west, to_east],
    )
    outer, parcels = local(
        outer_kernel,
        [shape(ITERS, EX, EY, LEVELS), shape(SLOT_ROWS, PARCEL, LEVELS)],
        [],
        [inner, products, to_west, to_east, from_east, from_west, drops, live],
    )
    arrived = lax.all_to_all(parcels, "gx", split_axis=0, concat_axis=0, tiled=True)
    shared = jnp.broadcast_to(jnp.sum(arrived[:, 24:], axis=0)[None], (16, 8, LEVELS))
    totals = lax.all_to_all(shared, ("grp", "gy"), split_axis=0, concat_axis=0, tiled=True)
    flat = (CX * CY, LEVELS)
    picked = (NBD * CHUNKS, LEVELS)
    new_theta, new_humidity, new_zonal, new_meridional, new_vertical, returned = local(
        step_kernel,
        [tile] * 5 + [shape(SLOT_ROWS, CHUNKS, LEVELS)],
        [owners],
        [
            totals,
            inner,
            outer,
            arrived,
            theta,
            humidity,
            zonal,
            meridional,
            vertical,
            from_north,
            from_south,
            from_east,
            from_west,
        ],
        [pltpu.VMEM((CX + 2, EY, LEVELS), f32)]
        + [pltpu.VMEM(flat, f32)] * 2
        + [pltpu.VMEM(picked, f32)]
        + [pltpu.VMEM(flat, f32)] * 2
        + [pltpu.VMEM(picked, f32)] * 2
        + [pltpu.VMEM((12, CX, CY, LEVELS), f32)],
    )
    returned = lax.all_to_all(returned, "gx", split_axis=0, concat_axis=0, tiled=True)
    *outputs, new_squares = local(
        last_kernel,
        [tile] * 5 + [shape(SLOT_ROWS, DPB)],
        [counts],
        [
            returned.reshape(SLOT_ROWS * CHUNKS, LEVELS),
            squares,
            new_theta,
            new_humidity,
            new_zonal,
            new_meridional,
            new_vertical,
        ],
        [pltpu.VMEM((SLOT_ROWS, DPB), f32), pltpu.SemaphoreType.DMA((6,))],
        far_outs=6,
    )
    return (*outputs, new_squares[None, None])


def solution(mesh):
    field = P(("grp", "gx"), "gy", None)
    slots = P(("grp", "gx"), "gy", None, None)
    return jax.shard_map(
        on_device,
        mesh=mesh,
        in_specs=(field,) * 7 + (slots,) * 3,
        out_specs=(field,) * 5 + (slots,),
        check_vma=False,
    )
```

```python
import functools

import jax
import jax.numpy as jnp
from jax import lax
from jax.experimental import pallas as pl
from jax.experimental.pallas import tpu as pltpu
from jax.sharding import PartitionSpec as P

TIME_INCREMENT = 0.15
THERMAL_LIFT = 0.5
HUMID_LIFT = 0.3
HELMHOLTZ = 0.001
CLAUSIUS_FACTOR = 0.2
GROWTH = 0.5
GROWTH_SLOPE = 0.1
SUB_STEP = 0.25
CURVATURE = 0.05
FLOOR_SQUARE = 0.04
CONDENSE = 0.2
PHASE_WARMING = 2.5

NSUB = 4
ITERS = 4
NBD = 8
CX = 24
CY = 16
LEVELS = 128
KLO = 48
BAND = 32
STRIP = 12
EX = 32
EY = 24
SLOT_ROWS = 16
DPB = 1024
CHUNKS = DPB // LEVELS
PARCEL = 32
SCALE = 1.0 / 6.0
VMEM_LIMIT = 24 * 1024 * 1024
COSTP = 1_000_000
FIRST_LIMIT = 54600 * 1024

f32 = jnp.float32
bf16 = jnp.bfloat16


def iota(shape, axis):
    return lax.broadcasted_iota(jnp.int32, shape, axis)


def vertical_profiles():
    level = iota((1, LEVELS), 1)
    height = level.astype(f32)
    centre = jnp.exp(-(height + 0.5) / LEVELS)
    face = jnp.where(level < LEVELS - 1, jnp.exp(-(height + 1.0) / LEVELS), 0.0)
    face_below = jnp.where(level > 0, jnp.exp(-height / LEVELS), 0.0)
    return level, centre, face, face_below


def turn(values, by, axis):
    return pltpu.roll(values, by % values.shape[axis], axis)


def lifted_row(i, theta, humidity, vertical):
    return vertical[i] + TIME_INCREMENT * (THERMAL_LIFT * theta[i] + HUMID_LIFT * humidity[i])


def right_side_kernel(
    theta_far,
    humidity_far,
    zonal_far,
    meridional_far,
    vertical_far,
    partial,
    to_south,
    to_north,
    edges,
    theta,
    humidity,
    zonal,
    meridional,
    vertical,
    arrivals,
):
    fields = (
        (zonal_far, zonal),
        (theta_far, theta),
        (humidity_far, humidity),
        (vertical_far, vertical),
        (meridional_far, meridional),
    )
    copies = [
        [
            pltpu.make_async_copy(
                far.at[first : first + STRIP], near.at[first : first + STRIP], arrivals.at[m, n]
            )
            for n, (far, near) in enumerate(fields)
        ]
        for m, first in enumerate(range(0, CX, STRIP))
    ]
    for strip in copies:
        for copy in strip:
            copy.start()
    copies[0][0].wait()
    level, centre, _, _ = vertical_profiles()
    sub = iota((CY, LEVELS), 0)
    sub8 = iota((8, LEVELS), 0)
    for i in range(CX):
        if i % STRIP == 0:
            for copy in copies[i // STRIP][1:]:
                copy.wait()
            if i + STRIP < CX:
                copies[i // STRIP + 1][0].wait()
        weighted = centre * lifted_row(i, theta, humidity, vertical)
        rise = jnp.where(level < LEVELS - 1, turn(weighted, -1, 1), 0.0) - jnp.where(
            level > 0, turn(weighted, 1, 1), 0.0
        )
        if i == 0:
            across = zonal[1]
        elif i == CX - 1:
            across = -zonal[CX - 2]
        else:
            across = zonal[i + 1] - zonal[i - 1]
        wind = meridional[i]
        along = jnp.where(sub < CY - 1, turn(wind, -1, 0), 0.0) - jnp.where(
            sub > 0, turn(wind, 1, 0), 0.0
        )
        right = (centre * (across * 0.5 + along * 0.5) + 0.5 * rise) * (-1.0 / TIME_INCREMENT)
        partial[i] = right
        warm = theta[i]
        damp = humidity[i]
        to_south[i] = jnp.where(
            sub8 < 4,
            right[0:8],
            jnp.where(sub8 == 4, wind[0:1], jnp.where(sub8 == 5, warm[0:1], damp[0:1])),
        )
        to_north[i] = jnp.where(
            sub8 >= 4,
            right[8:16],
            jnp.where(sub8 == 0, wind[15:16], jnp.where(sub8 == 1, warm[15:16], damp[15:16])),
        )
    for n, i in enumerate((0, CX - 1)):
        to_south[CX + n] = zonal[i, 0:8]
        to_north[CX + n] = zonal[i, 8:16]
        edges[7 * n + 4] = zonal[i]
        edges[7 * n + 5] = theta[i]
        edges[7 * n + 6] = humidity[i]
    for t in range(4):
        edges[t] = meridional[t]
        edges[7 + t] = meridional[CX - 4 + t]


def joined(north, south):
    return jnp.where(iota((8, LEVELS), 0) < 4, north, south)


def completed_row(i, partial, wind, from_north, from_south, third):
    sub8 = iota((8, LEVELS), 0)
    north = from_north[i]
    south = from_south[i]
    low = partial[i, 0:8] + jnp.where(sub8 == 0, third * south[0:1], 0.0)
    high = partial[i, 8:16] - jnp.where(sub8 == 7, third * north[4:5], 0.0)
    halo = (
        joined(north, south)
        + jnp.where(sub8 == 0, third * wind[15:16], 0.0)
        - jnp.where(sub8 == 7, third * wind[0:1], 0.0)
    )
    return low, high, halo


def side_kernel(partial, from_north, from_south, edges, to_west, to_east):
    _, centre, _, _ = vertical_profiles()
    third = centre * (0.5 / TIME_INCREMENT)
    for n, (target, first) in enumerate(((to_west, 0), (to_east, CX - 4))):
        for t in range(4):
            low, high, halo = completed_row(
                first + t, partial, edges[7 * n + t], from_north, from_south, third
            )
            target[t, 0:8] = low
            target[t, 8:16] = high
            target[t, 16:24] = halo
        target[4, 0:16] = edges[7 * n + 4]
        target[4, 16:24] = joined(from_north[CX + n], from_south[CX + n])
        for t in (5, 6):
            target[t, 0:16] = edges[7 * n + t]
            target[t, 16:24] = jnp.zeros((8, LEVELS), f32)


def pack_kernel(squares, cells, packed):
    for s in range(CHUNKS):
        part = slice(LEVELS * s, LEVELS * (s + 1))
        packed[pl.ds(s, SLOT_ROWS, stride=16), :] = squares[:, part]
        packed[pl.ds(8 + s, SLOT_ROWS, stride=16), :] = cells[:, part].astype(f32)


def pack_live_kernel(counts, numbers, packed):
    row = iota((SLOT_ROWS, LEVELS), 0)
    lane = iota((SLOT_ROWS, LEVELS), 1)
    live = jnp.zeros((SLOT_ROWS, LEVELS), jnp.int32)
    for r in range(SLOT_ROWS):
        live = jnp.where(row == r, counts[r], live)
    for s in range(CHUNKS):
        part = slice(LEVELS * s, LEVELS * (s + 1))
        packed[pl.ds(s, SLOT_ROWS, stride=8), :] = jnp.where(
            lane + LEVELS * s < live, numbers[:, part], 0.0
        )


def power_row(inner, outer, j, i):
    return inner[j, i] if j < i < CX - 1 - j else outer[j, i]


def applied(inner, outer, j, i):
    _, centre, face, face_below = vertical_profiles()
    here = ((4.0 + HELMHOLTZ) * centre + face + face_below) * SCALE
    values = power_row(inner, outer, j, i)
    lateral = (
        power_row(inner, outer, j, (i + 1) % EX)
        + power_row(inner, outer, j, (i - 1) % EX)
        + turn(values, -1, 0)
        + turn(values, 1, 0)
    )
    return (
        here * values
        - (centre * SCALE) * lateral
        - (face * SCALE) * turn(values, -1, 1)
        - (face_below * SCALE) * turn(values, 1, 1)
    )


def add_products(sums, inner, outer, rows):
    sums = list(sums)
    for i in rows:
        terms = [power_row(inner, outer, j, i)[0:16] for j in range(ITERS)]
        terms.append(applied(inner, outer, ITERS - 1, i)[0:16])
        for k in range(2 * ITERS):
            product = terms[k // 2] * terms[(k + 1) // 2]
            sums[k] = sums[k] + (product[0:8] + product[8:16])
    return sums


INNER_ROWS = range(ITERS + 1, CX - ITERS - 1)


def inner_kernel(
    partial, from_north, from_south, meridional, to_west, to_east, inner, products
):
    _, centre, _, _ = vertical_profiles()
    third = centre * (0.5 / TIME_INCREMENT)
    for i in range(1, CX - 1):
        if i < 4:
            inner[0, i] = to_west[i]
        elif i >= CX - 4:
            inner[0, i] = to_east[i - (CX - 4)]
        else:
            low, high, halo = completed_row(
                i, partial, meridional[i], from_north, from_south, third
            )
            inner[0, i, 0:8] = low
            inner[0, i, 8:16] = high
            inner[0, i, 16:24] = halo
    for j in range(ITERS - 1):
        for i in range(j + 2, CX - 2 - j):
            inner[j + 1, i] = applied(inner, None, j, i)
    sums = [jnp.zeros((8, LEVELS), f32) for _ in range(2 * ITERS)]
    sums = add_products(sums, inner, None, INNER_ROWS)
    for k in range(2 * ITERS):
        products[k] = sums[k]


def outer_kernel(
    inner,
    products,
    to_west,
    to_east,
    from_east,
    from_west,
    drops,
    live,
    outer,
    parcels,
):
    _, centre, _, _ = vertical_profiles()
    third = centre * (0.5 / TIME_INCREMENT)
    outer[0, 0] = to_west[0] + third * from_west[4]
    outer[0, CX - 1] = to_east[3] - third * from_east[4]
    for t in range(4):
        east = from_east[t]
        west = from_west[t]
        if t == 0:
            east = east + third * to_east[4]
        if t == 3:
            west = west - third * to_west[4]
        outer[0, CX + t] = east
        outer[0, CX + 4 + t] = west
    for j in range(ITERS - 1):
        reach = ITERS - 1 - j
        for i in range(-reach, CX + reach):
            if not j + 1 < i < CX - 2 - j:
                outer[j + 1, i % EX] = applied(inner, outer, j, i % EX)
    sums = [products[k] for k in range(2 * ITERS)]
    sums = add_products(sums, inner, outer, [i for i in range(CX) if i not in INNER_ROWS])
    sub8 = iota((8, LEVELS), 0)
    packed = jnp.zeros((8, LEVELS), f32)
    for k in range(2 * ITERS):
        packed = jnp.where(sub8 == k, jnp.sum(sums[k], axis=0, keepdims=True), packed)
    for r in range(SLOT_ROWS):
        parcels[r, 0:8] = drops[16 * r : 16 * r + 8]
        parcels[r, 8:16] = live[8 * r : 8 * r + 8]
        parcels[r, 16:24] = drops[16 * r + 8 : 16 * r + 16]
        parcels[r, 24:PARCEL] = packed


def two_sum(a, b):
    s = a + b
    t = s - a
    return s, (a - (s - t)) + (b - t)


def quick_sum(a, b):
    s = a + b
    return s, b - (s - a)


def split(a):
    t = a * 4097.0
    high = t - (t - a)
    return high, a - high


def two_product(a, b):
    p = a * b
    ah, al = split(a)
    bh, bl = split(b)
    return p, ((ah * bh - p) + ah * bl + al * bh) + al * bl


def pair_add(a, b):
    s, e = two_sum(a[0], b[0])
    return quick_sum(s, e + (a[1] + b[1]))


def pair_mul(a, b):
    p, e = two_product(a[0], b[0])
    return quick_sum(p, e + (a[0] * b[1] + a[1] * b[0]))


def pair_sub_mul(a, b, c):
    p = pair_mul(b, c)
    return pair_add(a, (-p[0], -p[1]))


def pair_inverse(a):
    guess = 1.0 / a[0]
    p = pair_mul(a, (guess, jnp.zeros_like(guess)))
    rest = (1.0 - p[0]) - p[1]
    return quick_sum(guess, guess * rest)


def coefficients(totals):
    high = totals[0]
    low = jnp.zeros_like(high)
    for t in range(1, totals.shape[0]):
        high, e = two_sum(high, totals[t])
        low = low + e
    bound = 256.0 * jnp.max(jnp.abs(high), axis=1, keepdims=True)
    coarse = (bound + high) - bound
    fine = (high - coarse) + low
    high, low = quick_sum(
        jnp.sum(coarse, axis=1, keepdims=True), jnp.sum(fine, axis=1, keepdims=True)
    )
    moment = []
    for k in range(2 * ITERS):
        moment.append(
            (
                jnp.broadcast_to(high[k : k + 1], (8, LEVELS)),
                jnp.broadcast_to(low[k : k + 1], (8, LEVELS)),
            )
        )
    matrix = [[moment[i + j + 1] for j in range(ITERS)] for i in range(ITERS)]
    side = [moment[i] for i in range(ITERS)]
    inverse = []
    for k in range(ITERS):
        inverse.append(pair_inverse(matrix[k][k]))
        for i in range(k + 1, ITERS):
            factor = pair_mul(matrix[k][i], inverse[k])
            for j in range(i, ITERS):
                matrix[i][j] = pair_sub_mul(matrix[i][j], factor, matrix[k][j])
            side[i] = pair_sub_mul(side[i], factor, side[k])
    result = [None] * ITERS
    for k in reversed(range(ITERS)):
        rest = side[k]
        for j in range(k + 1, ITERS):
            rest = pair_sub_mul(rest, matrix[k][j], result[j])
        result[k] = pair_mul(rest, inverse[k])
    return [(r[0] + r[1])[0:1] * SCALE for r in result]


def halves(values):
    high = values.astype(bf16).astype(f32)
    return high, values - high


HALF = TIME_INCREMENT * 0.5


def new_winds(i, potential, theta, humidity, zonal, meridional, vertical):
    level = iota((1, LEVELS), 1)
    here = potential[i + 1]
    mid = here[0:16]
    east = zonal[i] - HALF * (potential[i + 2, 0:16] - potential[i, 0:16])
    north = meridional[i] - HALF * (turn(here, -1, 0)[0:16] - turn(here, 1, 0)[0:16])
    up = lifted_row(i, theta, humidity, vertical) - HALF * (
        jnp.where(level < LEVELS - 1, turn(mid, -1, 1), 0.0)
        - jnp.where(level > 0, turn(mid, 1, 1), 0.0)
    )
    return east, north, up


def chunk(values, t):
    return jnp.concatenate([values[2 * t : 2 * t + 1], values[2 * t + 1 : 2 * t + 2]], axis=1)


def where_at(arrived, owner):
    cell = arrived[owner, 16:24].astype(jnp.int32)
    column = lax.shift_right_logical(cell, 7)
    return (
        jnp.bitwise_and(cell, LEVELS - 1) - KLO,
        jnp.bitwise_and(column, 1) * CX + lax.shift_right_logical(column, 1),
    )


def step_kernel(
    owners,
    totals,
    inner,
    outer,
    arrived,
    theta,
    humidity,
    zonal,
    meridional,
    vertical,
    from_north,
    from_south,
    from_east,
    from_west,
    new_theta,
    new_humidity,
    new_zonal,
    new_meridional,
    new_vertical,
    returned,
    potential,
    warmth,
    vapour,
    mass,
    excess,
    condensed,
    picked_excess,
    picked_warmth,
    spans,
):
    level, _, _, _ = vertical_profiles()
    sub = iota((CY, LEVELS), 0)
    for i in range(CX):
        for f, (field, side, in_north, in_south) in enumerate(
            ((theta, 5, 5, 1), (humidity, 6, 6, 2))
        ):
            values = field[i]
            f_e = field[i + 1] if i < CX - 1 else from_east[side, 0:16]
            f_w = field[i - 1] if i > 0 else from_west[side, 0:16]
            f_n = jnp.where(
                sub < CY - 1, turn(values, -1, 0), from_north[i, in_north : in_north + 1]
            )
            f_s = jnp.where(sub > 0, turn(values, 1, 0), from_south[i, in_south : in_south + 1])
            f_t = jnp.where(level < LEVELS - 1, turn(values, -1, 1), values)
            f_b = jnp.where(level > 0, turn(values, 1, 1), values)
            for n, span in enumerate(
                (values - f_w, f_e - values, values - f_s, f_n - values, values - f_b, f_t - values)
            ):
                spans[6 * f + n, i] = span
    weights = coefficients(totals)
    for t in range(CX + 2):
        i = (t - 1) % EX
        total = weights[0] * power_row(inner, outer, 0, i)
        for j in range(1, ITERS):
            total = total + weights[j] * power_row(inner, outer, j, i)
        potential[t] = total
    for i in range(CX):
        east, north, up = new_winds(i, potential, theta, humidity, zonal, meridional, vertical)
        new_zonal[i] = east
        new_meridional[i] = north
        new_vertical[i] = up
        moved = []
        for f, field in enumerate((theta, humidity)):
            tendency = (
                east * jnp.where(east > 0.0, spans[6 * f, i], spans[6 * f + 1, i])
                + north * jnp.where(north > 0.0, spans[6 * f + 2, i], spans[6 * f + 3, i])
                + up * jnp.where(up > 0.0, spans[6 * f + 4, i], spans[6 * f + 5, i])
            )
            moved.append(field[i] - TIME_INCREMENT * tendency)
        rows = slice(CY * i, CY * (i + 1))
        warmth[rows] = moved[0]
        vapour[rows] = moved[1]
        excess[rows] = moved[1] * jnp.exp(-CLAUSIUS_FACTOR * moved[0]) - 1.0

    lane = iota((2 * CX, LEVELS), 1)
    height = iota((BAND, 2 * LEVELS), 0)
    place = iota((2 * CX, 2 * LEVELS), 0)

    def band(field, b):
        values = jnp.concatenate(
            [
                field[pl.ds(2 * b, CX, stride=CY), :],
                field[pl.ds(2 * b + 1, CX, stride=CY), :],
            ],
            axis=0,
        )
        high, low = halves(values)
        both = jnp.where(lane < BAND, turn(high, -KLO, 1), turn(low, BAND - KLO, 1))
        return both[:, : 2 * BAND].astype(bf16)

    for b in range(NBD):
        table = jnp.concatenate([band(excess, b), band(warmth, b)], axis=0)
        heights, places = where_at(arrived, owners[b])
        for t in range(CHUNKS // 2):
            hot = jnp.where(height == chunk(heights, t), 1.0, 0.0).astype(bf16)
            found = jnp.dot(
                table, jnp.concatenate([hot, hot], axis=0), preferred_element_type=f32
            )
            mine = place == chunk(places, t)
            for target, part in ((picked_excess, found[: 2 * CX]), (picked_warmth, found[2 * CX :])):
                value = jnp.sum(jnp.where(mine, part, 0.0), axis=0, keepdims=True)
                row = CHUNKS * b + 2 * t
                target[row : row + 1] = value[:, :LEVELS]
                target[row + 1 : row + 2] = value[:, LEVELS:]
    returned[...] = jnp.zeros(returned.shape, f32)
    blocks = range(NBD)
    olds = [arrived[owners[b], 0:8] for b in blocks]
    pulls = [picked_excess[CHUNKS * b : CHUNKS * (b + 1)] for b in blocks]
    rates = [
        (2.0 * SUB_STEP * GROWTH)
        * jnp.exp(GROWTH_SLOPE * picked_warmth[CHUNKS * b : CHUNKS * (b + 1)])
        for b in blocks
    ]
    nows = list(olds)
    for substep in range(NSUB):
        curves = [CURVATURE * lax.rsqrt(now) for now in nows]
        nows = [
            jnp.maximum(now + rate * (pull - curve), FLOOR_SQUARE)
            for now, rate, pull, curve in zip(nows, rates, pulls, curves)
        ]
    for b in blocks:
        old, now = olds[b], nows[b]
        number = arrived[owners[b], 8:16]
        gain = now * (now * lax.rsqrt(now)) - old * (old * lax.rsqrt(old))
        mass[CHUNKS * b : CHUNKS * (b + 1)] = jnp.where(number > 0.0, number * gain, 0.0)
        returned[owners[b]] = now
    for b in range(NBD):
        heights, places = where_at(arrived, owners[b])
        gained = mass[CHUNKS * b : CHUNKS * (b + 1)]
        spreads = []
        hots = []
        for t in range(CHUNKS // 2):
            hots.append(jnp.where(height == chunk(heights, t), 1.0, 0.0).astype(bf16))
            mine = place == chunk(places, t)
            spreads.append(
                jnp.concatenate(
                    [
                        jnp.where(mine, part, 0.0).astype(bf16)
                        for part in halves(chunk(gained, t))
                    ],
                    axis=0,
                )
            )
        total = lax.dot_general(
            jnp.concatenate(spreads, axis=1),
            jnp.concatenate(hots, axis=1),
            (((1,), (1,)), ((), ())),
            preferred_element_type=f32,
        )
        liquid = CONDENSE * (total[: 2 * CX] + total[2 * CX :])
        liquid = jnp.concatenate([liquid, jnp.zeros((2 * CX, LEVELS - BAND), f32)], axis=1)
        liquid = turn(liquid, KLO, 1)
        condensed[pl.ds(2 * b, CX, stride=CY), :] = liquid[:CX]
        condensed[pl.ds(2 * b + 1, CX, stride=CY), :] = liquid[CX:]
    for i in range(CX):
        rows = slice(CY * i, CY * (i + 1))
        new_theta[i] = warmth[rows] + PHASE_WARMING * condensed[rows]
        new_humidity[i] = vapour[rows] - condensed[rows]


def last_kernel(
    counts,
    returned,
    squares,
    theta,
    humidity,
    zonal,
    meridional,
    vertical,
    far_theta,
    far_humidity,
    far_zonal,
    far_meridional,
    far_vertical,
    far_squares,
    new_squares,
    departures,
):
    copies = [
        pltpu.make_async_copy(near, far, departures.at[n])
        for n, (near, far) in enumerate(
            (
                (theta, far_theta),
                (humidity, far_humidity),
                (zonal, far_zonal),
                (meridional, far_meridional),
                (vertical, far_vertical),
                (new_squares, far_squares),
            )
        )
    ]
    for copy in copies[:5]:
        copy.start()
    row = iota((SLOT_ROWS, LEVELS), 0)
    lane = iota((SLOT_ROWS, LEVELS), 1)
    live = jnp.zeros((SLOT_ROWS, LEVELS), jnp.int32)
    for r in range(SLOT_ROWS):
        live = jnp.where(row == r, counts[r], live)
    for s in range(CHUNKS):
        part = slice(LEVELS * s, LEVELS * (s + 1))
        new_squares[:, part] = jnp.where(
            lane + LEVELS * s < live,
            returned[pl.ds(s, SLOT_ROWS, stride=CHUNKS), :],
            squares[:, part],
        )
    copies[5].start()
    for copy in copies:
        copy.wait()


def local(kernel, outs, scalars, operands, scratch=(), far=0, far_outs=0, limit=VMEM_LIMIT, cost=1_000_000):
    whole = pl.BlockSpec(memory_space=pltpu.VMEM)
    single = len(outs) == 1
    return pl.pallas_call(
        kernel,
        out_shape=outs[0] if single else outs,
        in_specs=[pl.BlockSpec(memory_space=pltpu.SMEM)] * len(scalars)
        + [pl.BlockSpec(memory_space=pltpu.HBM)] * far
        + [whole] * (len(operands) - far),
        out_specs=whole
        if single
        else [pl.BlockSpec(memory_space=pltpu.HBM)] * far_outs + [whole] * (len(outs) - far_outs),
        scratch_shapes=list(scratch),
        compiler_params=pltpu.CompilerParams(vmem_limit_bytes=limit),
        cost_estimate=pl.CostEstimate(flops=cost, bytes_accessed=cost, transcendentals=0),
    )(*scalars, *operands)


def shape(*dims):
    return jax.ShapeDtypeStruct(dims, f32)


def ring(axes, step):
    count = lax.axis_size(axes)
    return [(i, (i + step) % count) for i in range(count)]


def on_device(
    theta, humidity, zonal, meridional, vertical, owner_map, population, squares, numbers, cells
):
    owners = owner_map.reshape(NBD)
    counts = population.reshape(SLOT_ROWS)
    squares = squares.reshape(SLOT_ROWS, DPB)
    numbers = numbers.reshape(SLOT_ROWS, DPB)
    cells = cells.reshape(SLOT_ROWS, DPB)
    tiles = ("grp", "gx")
    tile = shape(CX, CY, LEVELS)
    partial, to_south, to_north, edges = local(
        right_side_kernel,
        [tile, shape(CX + 2, 8, LEVELS), shape(CX + 2, 8, LEVELS), shape(14, CY, LEVELS)],
        [],
        [theta, humidity, zonal, meridional, vertical],
        [pltpu.VMEM((CX, CY, LEVELS), f32)] * 5 + [pltpu.SemaphoreType.DMA((CX // STRIP, 5))],
        far=5,
        limit=FIRST_LIMIT,
    )
    from_north = lax.ppermute(to_south, "gy", ring("gy", -1))
    from_south = lax.ppermute(to_north, "gy", ring("gy", 1))
    edges, early_squares, early_cells = lax.optimization_barrier((edges, squares, cells))
    drops = local(
        pack_kernel, [shape(SLOT_ROWS * 16, LEVELS)], [], [early_squares, early_cells], cost=COSTP
    )
    edges, drops = lax.optimization_barrier((edges, drops))
    to_west, to_east = local(
        side_kernel,
        [shape(7, EY, LEVELS), shape(7, EY, LEVELS)],
        [],
        [partial, from_north, from_south, edges],
    )
    to_west, to_east, late_numbers = lax.optimization_barrier((to_west, to_east, numbers))
    live = local(pack_live_kernel, [shape(SLOT_ROWS * 8, LEVELS)], [counts], [late_numbers], cost=COSTP)
    from_east = lax.ppermute(to_west, tiles, ring(tiles, -1))
    from_west = lax.ppermute(to_east, tiles, ring(tiles, 1))
    inner, products = local(
        inner_kernel,
        [shape(ITERS, CX, EY, LEVELS), shape(2 * ITERS, 8, LEVELS)],
        [],
        [partial, from_north, from_south, meridional, to_west, to_east],
    )
    outer, parcels = local(
        outer_kernel,
        [shape(ITERS, EX, EY, LEVELS), shape(SLOT_ROWS, PARCEL, LEVELS)],
        [],
        [inner, products, to_west, to_east, from_east, from_west, drops, live],
    )
    arrived = lax.all_to_all(parcels, "gx", split_axis=0, concat_axis=0, tiled=True)
    shared = jnp.broadcast_to(jnp.sum(arrived[:, 24:], axis=0)[None], (16, 8, LEVELS))
    totals = lax.all_to_all(shared, ("grp", "gy"), split_axis=0, concat_axis=0, tiled=True)
    flat = (CX * CY, LEVELS)
    picked = (NBD * CHUNKS, LEVELS)
    new_theta, new_humidity, new_zonal, new_meridional, new_vertical, returned = local(
        step_kernel,
        [tile] * 5 + [shape(SLOT_ROWS, CHUNKS, LEVELS)],
        [owners],
        [
            totals,
            inner,
            outer,
            arrived,
            theta,
            humidity,
            zonal,
            meridional,
            vertical,
            from_north,
            from_south,
            from_east,
            from_west,
        ],
        [pltpu.VMEM((CX + 2, EY, LEVELS), f32)]
        + [pltpu.VMEM(flat, f32)] * 2
        + [pltpu.VMEM(picked, f32)]
        + [pltpu.VMEM(flat, f32)] * 2
        + [pltpu.VMEM(picked, f32)] * 2
        + [pltpu.VMEM((12, CX, CY, LEVELS), f32)],
    )
    returned = lax.all_to_all(returned, "gx", split_axis=0, concat_axis=0, tiled=True)
    *outputs, new_squares = local(
        last_kernel,
        [tile] * 5 + [shape(SLOT_ROWS, DPB)],
        [counts],
        [
            returned.reshape(SLOT_ROWS * CHUNKS, LEVELS),
            squares,
            new_theta,
            new_humidity,
            new_zonal,
            new_meridional,
            new_vertical,
        ],
        [pltpu.VMEM((SLOT_ROWS, DPB), f32), pltpu.SemaphoreType.DMA((6,))],
        far_outs=6,
    )
    return (*outputs, new_squares[None, None])


def solution(mesh):
    field = P(("grp", "gx"), "gy", None)
    slots = P(("grp", "gx"), "gy", None, None)
    return jax.shard_map(
        on_device,
        mesh=mesh,
        in_specs=(field,) * 7 + (slots,) * 3,
        out_specs=(field,) * 5 + (slots,),
        check_vma=False,
    )
```

```python
import functools

import jax
import jax.numpy as jnp
from jax import lax
from jax.experimental import pallas as pl
from jax.experimental.pallas import tpu as pltpu
from jax.sharding import PartitionSpec as P

TIME_INCREMENT = 0.15
THERMAL_LIFT = 0.5
HUMID_LIFT = 0.3
HELMHOLTZ = 0.001
CLAUSIUS_FACTOR = 0.2
GROWTH = 0.5
GROWTH_SLOPE = 0.1
SUB_STEP = 0.25
CURVATURE = 0.05
FLOOR_SQUARE = 0.04
CONDENSE = 0.2
PHASE_WARMING = 2.5

NSUB = 4
ITERS = 4
NBD = 8
CX = 24
CY = 16
LEVELS = 128
KLO = 48
BAND = 32
EX = 32
EY = 24
SLOT_ROWS = 16
DPB = 1024
CHUNKS = DPB // LEVELS
PARCEL = 32
SCALE = 1.0 / 6.0
VMEM_LIMIT = 24 * 1024 * 1024
COSTP = 1_000_000
FIRST_LIMIT = 54600 * 1024

f32 = jnp.float32
bf16 = jnp.bfloat16


def iota(shape, axis):
    return lax.broadcasted_iota(jnp.int32, shape, axis)


def vertical_profiles():
    level = iota((1, LEVELS), 1)
    height = level.astype(f32)
    centre = jnp.exp(-(height + 0.5) / LEVELS)
    face = jnp.where(level < LEVELS - 1, jnp.exp(-(height + 1.0) / LEVELS), 0.0)
    face_below = jnp.where(level > 0, jnp.exp(-height / LEVELS), 0.0)
    return level, centre, face, face_below


def turn(values, by, axis):
    return pltpu.roll(values, by % values.shape[axis], axis)


def lifted_row(i, theta, humidity, vertical):
    return vertical[i] + TIME_INCREMENT * (THERMAL_LIFT * theta[i] + HUMID_LIFT * humidity[i])


def right_side_kernel(
    theta_far,
    humidity_far,
    zonal_far,
    meridional_far,
    vertical_far,
    partial,
    to_south,
    to_north,
    edges,
    theta,
    humidity,
    zonal,
    meridional,
    vertical,
    arrivals,
):
    copies = [
        pltpu.make_async_copy(far, near, arrivals.at[n])
        for n, (far, near) in enumerate(
            (
                (theta_far, theta),
                (humidity_far, humidity),
                (zonal_far, zonal),
                (meridional_far, meridional),
                (vertical_far, vertical),
            )
        )
    ]
    for copy in copies:
        copy.start()
    for copy in copies:
        copy.wait()
    level, centre, _, _ = vertical_profiles()
    sub = iota((CY, LEVELS), 0)
    sub8 = iota((8, LEVELS), 0)
    for i in range(CX):
        weighted = centre * lifted_row(i, theta, humidity, vertical)
        rise = jnp.where(level < LEVELS - 1, turn(weighted, -1, 1), 0.0) - jnp.where(
            level > 0, turn(weighted, 1, 1), 0.0
        )
        if i == 0:
            across = zonal[1]
        elif i == CX - 1:
            across = -zonal[CX - 2]
        else:
            across = zonal[i + 1] - zonal[i - 1]
        wind = meridional[i]
        along = jnp.where(sub < CY - 1, turn(wind, -1, 0), 0.0) - jnp.where(
            sub > 0, turn(wind, 1, 0), 0.0
        )
        right = (centre * (across * 0.5 + along * 0.5) + 0.5 * rise) * (-1.0 / TIME_INCREMENT)
        partial[i] = right
        warm = theta[i]
        damp = humidity[i]
        to_south[i] = jnp.where(
            sub8 < 4,
            right[0:8],
            jnp.where(sub8 == 4, wind[0:1], jnp.where(sub8 == 5, warm[0:1], damp[0:1])),
        )
        to_north[i] = jnp.where(
            sub8 >= 4,
            right[8:16],
            jnp.where(sub8 == 0, wind[15:16], jnp.where(sub8 == 1, warm[15:16], damp[15:16])),
        )
    for n, i in enumerate((0, CX - 1)):
        to_south[CX + n] = zonal[i, 0:8]
        to_north[CX + n] = zonal[i, 8:16]
        edges[7 * n + 4] = zonal[i]
        edges[7 * n + 5] = theta[i]
        edges[7 * n + 6] = humidity[i]
    for t in range(4):
        edges[t] = meridional[t]
        edges[7 + t] = meridional[CX - 4 + t]


def joined(north, south):
    return jnp.where(iota((8, LEVELS), 0) < 4, north, south)


def completed_row(i, partial, wind, from_north, from_south, third):
    sub8 = iota((8, LEVELS), 0)
    north = from_north[i]
    south = from_south[i]
    low = partial[i, 0:8] + jnp.where(sub8 == 0, third * south[0:1], 0.0)
    high = partial[i, 8:16] - jnp.where(sub8 == 7, third * north[4:5], 0.0)
    halo = (
        joined(north, south)
        + jnp.where(sub8 == 0, third * wind[15:16], 0.0)
        - jnp.where(sub8 == 7, third * wind[0:1], 0.0)
    )
    return low, high, halo


def side_kernel(partial, from_north, from_south, edges, to_west, to_east):
    _, centre, _, _ = vertical_profiles()
    third = centre * (0.5 / TIME_INCREMENT)
    for n, (target, first) in enumerate(((to_west, 0), (to_east, CX - 4))):
        for t in range(4):
            low, high, halo = completed_row(
                first + t, partial, edges[7 * n + t], from_north, from_south, third
            )
            target[t, 0:8] = low
            target[t, 8:16] = high
            target[t, 16:24] = halo
        target[4, 0:16] = edges[7 * n + 4]
        target[4, 16:24] = joined(from_north[CX + n], from_south[CX + n])
        for t in (5, 6):
            target[t, 0:16] = edges[7 * n + t]
            target[t, 16:24] = jnp.zeros((8, LEVELS), f32)


def pack_kernel(squares, cells, packed):
    for s in range(CHUNKS):
        part = slice(LEVELS * s, LEVELS * (s + 1))
        packed[pl.ds(s, SLOT_ROWS, stride=16), :] = squares[:, part]
        packed[pl.ds(8 + s, SLOT_ROWS, stride=16), :] = cells[:, part].astype(f32)


def pack_live_kernel(counts, numbers, packed):
    row = iota((SLOT_ROWS, LEVELS), 0)
    lane = iota((SLOT_ROWS, LEVELS), 1)
    live = jnp.zeros((SLOT_ROWS, LEVELS), jnp.int32)
    for r in range(SLOT_ROWS):
        live = jnp.where(row == r, counts[r], live)
    for s in range(CHUNKS):
        part = slice(LEVELS * s, LEVELS * (s + 1))
        packed[pl.ds(s, SLOT_ROWS, stride=8), :] = jnp.where(
            lane + LEVELS * s < live, numbers[:, part], 0.0
        )


def power_row(inner, outer, j, i):
    return inner[j, i] if j < i < CX - 1 - j else outer[j, i]


def applied(inner, outer, j, i):
    _, centre, face, face_below = vertical_profiles()
    here = ((4.0 + HELMHOLTZ) * centre + face + face_below) * SCALE
    values = power_row(inner, outer, j, i)
    lateral = (
        power_row(inner, outer, j, (i + 1) % EX)
        + power_row(inner, outer, j, (i - 1) % EX)
        + turn(values, -1, 0)
        + turn(values, 1, 0)
    )
    return (
        here * values
        - (centre * SCALE) * lateral
        - (face * SCALE) * turn(values, -1, 1)
        - (face_below * SCALE) * turn(values, 1, 1)
    )


def add_products(sums, inner, outer, rows):
    sums = list(sums)
    for i in rows:
        terms = [power_row(inner, outer, j, i)[0:16] for j in range(ITERS)]
        terms.append(applied(inner, outer, ITERS - 1, i)[0:16])
        for k in range(2 * ITERS):
            product = terms[k // 2] * terms[(k + 1) // 2]
            sums[k] = sums[k] + (product[0:8] + product[8:16])
    return sums


INNER_ROWS = range(ITERS + 1, CX - ITERS - 1)


def inner_kernel(
    partial, from_north, from_south, meridional, to_west, to_east, inner, products
):
    _, centre, _, _ = vertical_profiles()
    third = centre * (0.5 / TIME_INCREMENT)
    for i in range(1, CX - 1):
        if i < 4:
            inner[0, i] = to_west[i]
        elif i >= CX - 4:
            inner[0, i] = to_east[i - (CX - 4)]
        else:
            low, high, halo = completed_row(
                i, partial, meridional[i], from_north, from_south, third
            )
            inner[0, i, 0:8] = low
            inner[0, i, 8:16] = high
            inner[0, i, 16:24] = halo
    for j in range(ITERS - 1):
        for i in range(j + 2, CX - 2 - j):
            inner[j + 1, i] = applied(inner, None, j, i)
    sums = [jnp.zeros((8, LEVELS), f32) for _ in range(2 * ITERS)]
    sums = add_products(sums, inner, None, INNER_ROWS)
    for k in range(2 * ITERS):
        products[k] = sums[k]


def outer_kernel(
    inner,
    products,
    to_west,
    to_east,
    from_east,
    from_west,
    drops,
    live,
    outer,
    parcels,
):
    _, centre, _, _ = vertical_profiles()
    third = centre * (0.5 / TIME_INCREMENT)
    outer[0, 0] = to_west[0] + third * from_west[4]
    outer[0, CX - 1] = to_east[3] - third * from_east[4]
    for t in range(4):
        east = from_east[t]
        west = from_west[t]
        if t == 0:
            east = east + third * to_east[4]
        if t == 3:
            west = west - third * to_west[4]
        outer[0, CX + t] = east
        outer[0, CX + 4 + t] = west
    for j in range(ITERS - 1):
        reach = ITERS - 1 - j
        for i in range(-reach, CX + reach):
            if not j + 1 < i < CX - 2 - j:
                outer[j + 1, i % EX] = applied(inner, outer, j, i % EX)
    sums = [products[k] for k in range(2 * ITERS)]
    sums = add_products(sums, inner, outer, [i for i in range(CX) if i not in INNER_ROWS])
    sub8 = iota((8, LEVELS), 0)
    packed = jnp.zeros((8, LEVELS), f32)
    for k in range(2 * ITERS):
        packed = jnp.where(sub8 == k, jnp.sum(sums[k], axis=0, keepdims=True), packed)
    for r in range(SLOT_ROWS):
        parcels[r, 0:8] = drops[16 * r : 16 * r + 8]
        parcels[r, 8:16] = live[8 * r : 8 * r + 8]
        parcels[r, 16:24] = drops[16 * r + 8 : 16 * r + 16]
        parcels[r, 24:PARCEL] = packed


def two_sum(a, b):
    s = a + b
    t = s - a
    return s, (a - (s - t)) + (b - t)


def quick_sum(a, b):
    s = a + b
    return s, b - (s - a)


def split(a):
    t = a * 4097.0
    high = t - (t - a)
    return high, a - high


def two_product(a, b):
    p = a * b
    ah, al = split(a)
    bh, bl = split(b)
    return p, ((ah * bh - p) + ah * bl + al * bh) + al * bl


def pair_add(a, b):
    s, e = two_sum(a[0], b[0])
    return quick_sum(s, e + (a[1] + b[1]))


def pair_mul(a, b):
    p, e = two_product(a[0], b[0])
    return quick_sum(p, e + (a[0] * b[1] + a[1] * b[0]))


def pair_sub_mul(a, b, c):
    p = pair_mul(b, c)
    return pair_add(a, (-p[0], -p[1]))


def pair_inverse(a):
    guess = 1.0 / a[0]
    p = pair_mul(a, (guess, jnp.zeros_like(guess)))
    rest = (1.0 - p[0]) - p[1]
    return quick_sum(guess, guess * rest)


def coefficients(totals):
    high = totals[0]
    low = jnp.zeros_like(high)
    for t in range(1, totals.shape[0]):
        high, e = two_sum(high, totals[t])
        low = low + e
    bound = 256.0 * jnp.max(jnp.abs(high), axis=1, keepdims=True)
    coarse = (bound + high) - bound
    fine = (high - coarse) + low
    high, low = quick_sum(
        jnp.sum(coarse, axis=1, keepdims=True), jnp.sum(fine, axis=1, keepdims=True)
    )
    moment = []
    for k in range(2 * ITERS):
        moment.append(
            (
                jnp.broadcast_to(high[k : k + 1], (8, LEVELS)),
                jnp.broadcast_to(low[k : k + 1], (8, LEVELS)),
            )
        )
    matrix = [[moment[i + j + 1] for j in range(ITERS)] for i in range(ITERS)]
    side = [moment[i] for i in range(ITERS)]
    inverse = []
    for k in range(ITERS):
        inverse.append(pair_inverse(matrix[k][k]))
        for i in range(k + 1, ITERS):
            factor = pair_mul(matrix[k][i], inverse[k])
            for j in range(i, ITERS):
                matrix[i][j] = pair_sub_mul(matrix[i][j], factor, matrix[k][j])
            side[i] = pair_sub_mul(side[i], factor, side[k])
    result = [None] * ITERS
    for k in reversed(range(ITERS)):
        rest = side[k]
        for j in range(k + 1, ITERS):
            rest = pair_sub_mul(rest, matrix[k][j], result[j])
        result[k] = pair_mul(rest, inverse[k])
    return [(r[0] + r[1])[0:1] * SCALE for r in result]


def halves(values):
    high = values.astype(bf16).astype(f32)
    return high, values - high


HALF = TIME_INCREMENT * 0.5


def new_winds(i, potential, theta, humidity, zonal, meridional, vertical):
    level = iota((1, LEVELS), 1)
    here = potential[i + 1]
    mid = here[0:16]
    east = zonal[i] - HALF * (potential[i + 2, 0:16] - potential[i, 0:16])
    north = meridional[i] - HALF * (turn(here, -1, 0)[0:16] - turn(here, 1, 0)[0:16])
    up = lifted_row(i, theta, humidity, vertical) - HALF * (
        jnp.where(level < LEVELS - 1, turn(mid, -1, 1), 0.0)
        - jnp.where(level > 0, turn(mid, 1, 1), 0.0)
    )
    return east, north, up


def chunk(values, t):
    return jnp.concatenate([values[2 * t : 2 * t + 1], values[2 * t + 1 : 2 * t + 2]], axis=1)


def where_at(arrived, owner):
    cell = arrived[owner, 16:24].astype(jnp.int32)
    column = lax.shift_right_logical(cell, 7)
    return (
        jnp.bitwise_and(cell, LEVELS - 1) - KLO,
        jnp.bitwise_and(column, 1) * CX + lax.shift_right_logical(column, 1),
    )


def step_kernel(
    owners,
    totals,
    inner,
    outer,
    arrived,
    theta,
    humidity,
    zonal,
    meridional,
    vertical,
    from_north,
    from_south,
    from_east,
    from_west,
    new_theta,
    new_humidity,
    new_zonal,
    new_meridional,
    new_vertical,
    returned,
    potential,
    warmth,
    vapour,
    mass,
    excess,
    condensed,
    picked_excess,
    picked_warmth,
    spans,
):
    level, _, _, _ = vertical_profiles()
    sub = iota((CY, LEVELS), 0)
    for i in range(CX):
        for f, (field, side, in_north, in_south) in enumerate(
            ((theta, 5, 5, 1), (humidity, 6, 6, 2))
        ):
            values = field[i]
            f_e = field[i + 1] if i < CX - 1 else from_east[side, 0:16]
            f_w = field[i - 1] if i > 0 else from_west[side, 0:16]
            f_n = jnp.where(
                sub < CY - 1, turn(values, -1, 0), from_north[i, in_north : in_north + 1]
            )
            f_s = jnp.where(sub > 0, turn(values, 1, 0), from_south[i, in_south : in_south + 1])
            f_t = jnp.where(level < LEVELS - 1, turn(values, -1, 1), values)
            f_b = jnp.where(level > 0, turn(values, 1, 1), values)
            for n, span in enumerate(
                (values - f_w, f_e - values, values - f_s, f_n - values, values - f_b, f_t - values)
            ):
                spans[6 * f + n, i] = span
    weights = coefficients(totals)
    for t in range(CX + 2):
        i = (t - 1) % EX
        total = weights[0] * power_row(inner, outer, 0, i)
        for j in range(1, ITERS):
            total = total + weights[j] * power_row(inner, outer, j, i)
        potential[t] = total
    for i in range(CX):
        east, north, up = new_winds(i, potential, theta, humidity, zonal, meridional, vertical)
        new_zonal[i] = east
        new_meridional[i] = north
        new_vertical[i] = up
        moved = []
        for f, field in enumerate((theta, humidity)):
            tendency = (
                east * jnp.where(east > 0.0, spans[6 * f, i], spans[6 * f + 1, i])
                + north * jnp.where(north > 0.0, spans[6 * f + 2, i], spans[6 * f + 3, i])
                + up * jnp.where(up > 0.0, spans[6 * f + 4, i], spans[6 * f + 5, i])
            )
            moved.append(field[i] - TIME_INCREMENT * tendency)
        rows = slice(CY * i, CY * (i + 1))
        warmth[rows] = moved[0]
        vapour[rows] = moved[1]
        excess[rows] = moved[1] * jnp.exp(-CLAUSIUS_FACTOR * moved[0]) - 1.0

    lane = iota((2 * CX, LEVELS), 1)
    height = iota((BAND, 2 * LEVELS), 0)
    place = iota((2 * CX, 2 * LEVELS), 0)

    def band(field, b):
        values = jnp.concatenate(
            [
                field[pl.ds(2 * b, CX, stride=CY), :],
                field[pl.ds(2 * b + 1, CX, stride=CY), :],
            ],
            axis=0,
        )
        high, low = halves(values)
        both = jnp.where(lane < BAND, turn(high, -KLO, 1), turn(low, BAND - KLO, 1))
        return both[:, : 2 * BAND].astype(bf16)

    for b in range(NBD):
        table = jnp.concatenate([band(excess, b), band(warmth, b)], axis=0)
        heights, places = where_at(arrived, owners[b])
        for t in range(CHUNKS // 2):
            hot = jnp.where(height == chunk(heights, t), 1.0, 0.0).astype(bf16)
            found = jnp.dot(
                table, jnp.concatenate([hot, hot], axis=0), preferred_element_type=f32
            )
            mine = place == chunk(places, t)
            for target, part in ((picked_excess, found[: 2 * CX]), (picked_warmth, found[2 * CX :])):
                value = jnp.sum(jnp.where(mine, part, 0.0), axis=0, keepdims=True)
                row = CHUNKS * b + 2 * t
                target[row : row + 1] = value[:, :LEVELS]
                target[row + 1 : row + 2] = value[:, LEVELS:]
    returned[...] = jnp.zeros(returned.shape, f32)
    blocks = range(NBD)
    olds = [arrived[owners[b], 0:8] for b in blocks]
    pulls = [picked_excess[CHUNKS * b : CHUNKS * (b + 1)] for b in blocks]
    rates = [
        (2.0 * SUB_STEP * GROWTH)
        * jnp.exp(GROWTH_SLOPE * picked_warmth[CHUNKS * b : CHUNKS * (b + 1)])
        for b in blocks
    ]
    nows = list(olds)
    for substep in range(NSUB):
        curves = [CURVATURE * lax.rsqrt(now) for now in nows]
        nows = [
            jnp.maximum(now + rate * (pull - curve), FLOOR_SQUARE)
            for now, rate, pull, curve in zip(nows, rates, pulls, curves)
        ]
    for b in blocks:
        old, now = olds[b], nows[b]
        number = arrived[owners[b], 8:16]
        gain = now * (now * lax.rsqrt(now)) - old * (old * lax.rsqrt(old))
        mass[CHUNKS * b : CHUNKS * (b + 1)] = jnp.where(number > 0.0, number * gain, 0.0)
        returned[owners[b]] = now
    for b in range(NBD):
        heights, places = where_at(arrived, owners[b])
        gained = mass[CHUNKS * b : CHUNKS * (b + 1)]
        spreads = []
        hots = []
        for t in range(CHUNKS // 2):
            hots.append(jnp.where(height == chunk(heights, t), 1.0, 0.0).astype(bf16))
            mine = place == chunk(places, t)
            spreads.append(
                jnp.concatenate(
                    [
                        jnp.where(mine, part, 0.0).astype(bf16)
                        for part in halves(chunk(gained, t))
                    ],
                    axis=0,
                )
            )
        total = lax.dot_general(
            jnp.concatenate(spreads, axis=1),
            jnp.concatenate(hots, axis=1),
            (((1,), (1,)), ((), ())),
            preferred_element_type=f32,
        )
        liquid = CONDENSE * (total[: 2 * CX] + total[2 * CX :])
        liquid = jnp.concatenate([liquid, jnp.zeros((2 * CX, LEVELS - BAND), f32)], axis=1)
        liquid = turn(liquid, KLO, 1)
        condensed[pl.ds(2 * b, CX, stride=CY), :] = liquid[:CX]
        condensed[pl.ds(2 * b + 1, CX, stride=CY), :] = liquid[CX:]
    for i in range(CX):
        rows = slice(CY * i, CY * (i + 1))
        new_theta[i] = warmth[rows] + PHASE_WARMING * condensed[rows]
        new_humidity[i] = vapour[rows] - condensed[rows]


def last_kernel(
    counts,
    returned,
    squares,
    theta,
    humidity,
    zonal,
    meridional,
    vertical,
    far_theta,
    far_humidity,
    far_zonal,
    far_meridional,
    far_vertical,
    far_squares,
    new_squares,
    departures,
):
    copies = [
        pltpu.make_async_copy(near, far, departures.at[n])
        for n, (near, far) in enumerate(
            (
                (theta, far_theta),
                (humidity, far_humidity),
                (zonal, far_zonal),
                (meridional, far_meridional),
                (vertical, far_vertical),
                (new_squares, far_squares),
            )
        )
    ]
    for copy in copies[:5]:
        copy.start()
    row = iota((SLOT_ROWS, LEVELS), 0)
    lane = iota((SLOT_ROWS, LEVELS), 1)
    live = jnp.zeros((SLOT_ROWS, LEVELS), jnp.int32)
    for r in range(SLOT_ROWS):
        live = jnp.where(row == r, counts[r], live)
    for s in range(CHUNKS):
        part = slice(LEVELS * s, LEVELS * (s + 1))
        new_squares[:, part] = jnp.where(
            lane + LEVELS * s < live,
            returned[pl.ds(s, SLOT_ROWS, stride=CHUNKS), :],
            squares[:, part],
        )
    copies[5].start()
    for copy in copies:
        copy.wait()


def local(kernel, outs, scalars, operands, scratch=(), far=0, far_outs=0, limit=VMEM_LIMIT, cost=1_000_000):
    whole = pl.BlockSpec(memory_space=pltpu.VMEM)
    single = len(outs) == 1
    return pl.pallas_call(
        kernel,
        out_shape=outs[0] if single else outs,
        in_specs=[pl.BlockSpec(memory_space=pltpu.SMEM)] * len(scalars)
        + [pl.BlockSpec(memory_space=pltpu.HBM)] * far
        + [whole] * (len(operands) - far),
        out_specs=whole
        if single
        else [pl.BlockSpec(memory_space=pltpu.HBM)] * far_outs + [whole] * (len(outs) - far_outs),
        scratch_shapes=list(scratch),
        compiler_params=pltpu.CompilerParams(vmem_limit_bytes=limit),
        cost_estimate=pl.CostEstimate(flops=cost, bytes_accessed=cost, transcendentals=0),
    )(*scalars, *operands)


def shape(*dims):
    return jax.ShapeDtypeStruct(dims, f32)


def ring(axes, step):
    count = lax.axis_size(axes)
    return [(i, (i + step) % count) for i in range(count)]


def on_device(
    theta, humidity, zonal, meridional, vertical, owner_map, population, squares, numbers, cells
):
    owners = owner_map.reshape(NBD)
    counts = population.reshape(SLOT_ROWS)
    squares = squares.reshape(SLOT_ROWS, DPB)
    numbers = numbers.reshape(SLOT_ROWS, DPB)
    cells = cells.reshape(SLOT_ROWS, DPB)
    tiles = ("grp", "gx")
    tile = shape(CX, CY, LEVELS)
    partial, to_south, to_north, edges = local(
        right_side_kernel,
        [tile, shape(CX + 2, 8, LEVELS), shape(CX + 2, 8, LEVELS), shape(14, CY, LEVELS)],
        [],
        [theta, humidity, zonal, meridional, vertical],
        [pltpu.VMEM((CX, CY, LEVELS), f32)] * 5 + [pltpu.SemaphoreType.DMA((5,))],
        far=5,
        limit=FIRST_LIMIT,
    )
    from_north = lax.ppermute(to_south, "gy", ring("gy", -1))
    from_south = lax.ppermute(to_north, "gy", ring("gy", 1))
    edges, early_squares, early_cells = lax.optimization_barrier((edges, squares, cells))
    drops = local(
        pack_kernel, [shape(SLOT_ROWS * 16, LEVELS)], [], [early_squares, early_cells], cost=COSTP
    )
    edges, drops = lax.optimization_barrier((edges, drops))
    to_west, to_east = local(
        side_kernel,
        [shape(7, EY, LEVELS), shape(7, EY, LEVELS)],
        [],
        [partial, from_north, from_south, edges],
    )
    to_west, to_east, late_numbers = lax.optimization_barrier((to_west, to_east, numbers))
    live = local(pack_live_kernel, [shape(SLOT_ROWS * 8, LEVELS)], [counts], [late_numbers], cost=COSTP)
    from_east = lax.ppermute(to_west, tiles, ring(tiles, -1))
    from_west = lax.ppermute(to_east, tiles, ring(tiles, 1))
    inner, products = local(
        inner_kernel,
        [shape(ITERS, CX, EY, LEVELS), shape(2 * ITERS, 8, LEVELS)],
        [],
        [partial, from_north, from_south, meridional, to_west, to_east],
    )
    outer, parcels = local(
        outer_kernel,
        [shape(ITERS, EX, EY, LEVELS), shape(SLOT_ROWS, PARCEL, LEVELS)],
        [],
        [inner, products, to_west, to_east, from_east, from_west, drops, live],
    )
    arrived = lax.all_to_all(parcels, "gx", split_axis=0, concat_axis=0, tiled=True)
    shared = jnp.broadcast_to(jnp.sum(arrived[:, 24:], axis=0)[None], (16, 8, LEVELS))
    totals = lax.all_to_all(shared, ("grp", "gy"), split_axis=0, concat_axis=0, tiled=True)
    flat = (CX * CY, LEVELS)
    picked = (NBD * CHUNKS, LEVELS)
    new_theta, new_humidity, new_zonal, new_meridional, new_vertical, returned = local(
        step_kernel,
        [tile] * 5 + [shape(SLOT_ROWS, CHUNKS, LEVELS)],
        [owners],
        [
            totals,
            inner,
            outer,
            arrived,
            theta,
            humidity,
            zonal,
            meridional,
            vertical,
            from_north,
            from_south,
            from_east,
            from_west,
        ],
        [pltpu.VMEM((CX + 2, EY, LEVELS), f32)]
        + [pltpu.VMEM(flat, f32)] * 2
        + [pltpu.VMEM(picked, f32)]
        + [pltpu.VMEM(flat, f32)] * 2
        + [pltpu.VMEM(picked, f32)] * 2
        + [pltpu.VMEM((12, CX, CY, LEVELS), f32)],
    )
    returned = lax.all_to_all(returned, "gx", split_axis=0, concat_axis=0, tiled=True)
    *outputs, new_squares = local(
        last_kernel,
        [tile] * 5 + [shape(SLOT_ROWS, DPB)],
        [counts],
        [
            returned.reshape(SLOT_ROWS * CHUNKS, LEVELS),
            squares,
            new_theta,
            new_humidity,
            new_zonal,
            new_meridional,
            new_vertical,
        ],
        [pltpu.VMEM((SLOT_ROWS, DPB), f32), pltpu.SemaphoreType.DMA((6,))],
        far_outs=6,
    )
    return (*outputs, new_squares[None, None])


def solution(mesh):
    field = P(("grp", "gx"), "gy", None)
    slots = P(("grp", "gx"), "gy", None, None)
    return jax.shard_map(
        on_device,
        mesh=mesh,
        in_specs=(field,) * 7 + (slots,) * 3,
        out_specs=(field,) * 5 + (slots,),
        check_vma=False,
    )
```
